512 devices in a mesh: ang: 8 (over x, z_hi), slab: 64 (over y, z_lo, core).
Axes of the slice: x: 4, y: 4, z: 16 (z_hi: 2, z_lo: 8; z = z_hi * 8 + z_lo), core: 2. Of those that a mesh axis runs over, the one named last changes fastest.
Arguments:
- weights: float32 [16, 4, 256], P('ang', None, 'slab'), may hold values from 0.05 to 1
- shifts: int32 [8, 64], P('ang', 'slab'), may hold values from 0 to 1, as said below
- bands: int32 [8, 64], P('ang', 'slab'), may hold values from 1 to 4, as said below
- volume: float32 [256, 64, 1024], P('slab'), may hold values from -6 to 6
- measured: bfloat16 [16, 128, 64, 1024], P('ang', 'slab'), may hold values from -12 to 12
Outputs:
- updated: float32 [256, 64, 1024], P('slab')
- residual: float32 [16, 128, 64, 1024], P('ang', 'slab')
The draws below stay inside these ranges and needn't reach their ends.
Inputs may be any that keep to these rules, and one draw needn't show every extreme that they name: `shifts`: each band starts within the first 2 rows counted from its slab's first row. shifts plus bands never exceeds 2 * 2, so each band lies in the detector rows of its slab and of the next slab.
All inputs are finite; a program needn't handle non-finite values.
Results may differ from the reference program's by a relative error of at most 0.0003.
Values sent between devices are 32-bit elements; how exact they have to be, the bound alone decides.
No kernel may reach another device: no remote copies, remote signals or barrier semaphores. Data moves between devices by JAX's collectives and lax.ppermute only.
A program may use at most 64 MiB of HBM per device.

```python
import math
import jax
import jax.numpy as jnp
from jax import lax

DETECTOR_COLUMNS = 1024
VOLUME_ROWS = 64
SLAB_LAYERS = 4
RS = 2
AD = 2
BAND = 4
GROUPS = 8
SLAB_TOTAL = 64
ANGLES = 16
NZ = 256
R = 128


def band_layout(key):
    first, second = jax.random.split(key)
    shift = jax.random.randint(first, (GROUPS, SLAB_TOTAL), 0, RS, dtype=jnp.int32)
    width = jax.random.randint(second, (GROUPS, SLAB_TOTAL), 1, 2 * RS - shift + 1, dtype=jnp.int32)
    shift = shift.at[0, 0].set(0).at[GROUPS - 1, 1].set(RS - 1)
    width = width.at[0, 0].set(2 * RS).at[GROUPS - 1, 1].set(1)
    return (shift, width)


def draw_shifts(key, part):
    layout = band_layout(key)
    return layout[0]


def draw_bands(key, part):
    layout = band_layout(key)
    return layout[1]


def block_levels(own_key, extent, cuts, least, largest):
    loudness = 1.0
    for dim, blocks in cuts:
        draws = jax.random.uniform(jax.random.fold_in(jax.random.fold_in(own_key, 6), dim), (blocks,), jnp.float32, least / len(cuts), largest / len(cuts))
        loudness = loudness * jnp.repeat(jnp.exp(draws), extent[dim] // blocks).reshape((-1,) + (1,) * (len(extent) - 1 - dim))
    return loudness


def gaussian(key, shape, scale, most, shards=(), held_as=jnp.bfloat16):
    factor_of = block_levels(key, shape, shards, -0.22, 0.18) if shards else 1.0
    entries = jax.random.normal(key, shape, jnp.float32) * scale * factor_of
    return jnp.minimum(jnp.maximum(entries, -most), most).astype(held_as)


def setup_inputs(seed: int = 0) -> dict:
    key_list = jax.random.split(jax.random.key(seed), 6)
    return {
        "weights": jnp.clip(jnp.exp(math.log(1.0) - 2.9957323 * jax.random.uniform(key_list[0], (ANGLES, BAND, NZ), jnp.float32) ** block_levels(key_list[0], (ANGLES, BAND, NZ), ((0, 8), (2, 64)), -0.2, 0.2)), 0.05, 1.0),
        "shifts": draw_shifts(jax.random.fold_in(key_list[5], 71), 0),
        "bands": draw_bands(jax.random.fold_in(key_list[5], 71), 0),
        "volume": gaussian(key_list[3], (NZ, VOLUME_ROWS, DETECTOR_COLUMNS), 1.0, 6.0, ((0, 64),), jnp.float32),
        "measured": gaussian(key_list[4], (ANGLES, R, VOLUME_ROWS, DETECTOR_COLUMNS), 2.0, 12.0, ((0, 8), (1, 64))),
    }


PRECISION_HIGH = lax.Precision.HIGHEST

def band_windows(weights, shifts, bands):
    four = weights.reshape(ANGLES, BAND, SLAB_TOTAL, SLAB_LAYERS).transpose(0, 2, 1, 3)
    shift_rep = jnp.repeat(shifts, AD, axis=0)
    band_rep = jnp.repeat(bands, AD, axis=0)
    rows_i = jnp.arange(BAND, dtype=jnp.int32)[:, None]
    rows_j = jnp.arange(BAND, dtype=jnp.int32)[None, :]
    placer = ((rows_i[None, None] == rows_j[None, None] + shift_rep[:, :, None, None]) & (rows_j[None, None] < band_rep[:, :, None, None])).astype(jnp.float32)
    return jnp.einsum('asij,asjz->asiz', placer, four, precision=PRECISION_HIGH)

def smooth(field):
    padded = jnp.pad(field, ((1, 1), (0, 0), (0, 0)))
    base = padded[:-1]
    grad_z = padded[1:] - base
    grad_y = jnp.concatenate([base[:, 1:] - base[:, :-1], jnp.zeros_like(base[:, :1])], axis=1)
    grad_x = jnp.concatenate([base[:, :, 1:] - base[:, :, :-1], jnp.zeros_like(base[:, :, :1])], axis=2)
    size = jnp.sqrt(grad_z * grad_z + grad_y * grad_y + grad_x * grad_x + 0.01)
    flow_z = grad_z / size
    flow_y = (grad_y / size)[1:]
    flow_x = (grad_x / size)[1:]
    div = flow_z[1:] - flow_z[:-1]
    div = div + flow_y - jnp.concatenate([jnp.zeros_like(flow_y[:, :1]), flow_y[:, :-1]], axis=1)
    div = div + flow_x - jnp.concatenate([jnp.zeros_like(flow_x[:, :, :1]), flow_x[:, :, :-1]], axis=2)
    return field + 0.05 * div

def reference(weights, shifts, bands, volume, measured):
    window = band_windows(weights, shifts, bands)
    slab_split_volume = volume.reshape(SLAB_TOTAL, SLAB_LAYERS, VOLUME_ROWS, DETECTOR_COLUMNS)
    got_all = measured.astype(jnp.float32).reshape(ANGLES, SLAB_TOTAL, RS, VOLUME_ROWS, DETECTOR_COLUMNS)

    def one_angle(carry, item):
        row_window, got = item
        part = jnp.einsum('uej,ujql->ueql', row_window, slab_split_volume, precision=PRECISION_HIGH)
        rows = lax.optimization_barrier(jnp.sum(row_window, axis=2))
        spill = jnp.concatenate([jnp.zeros_like(part[:1, RS:]), part[:-1, RS:]], axis=0)
        projected = part[:, :RS] + spill
        row_spill = jnp.concatenate([jnp.zeros_like(rows[:1, RS:]), rows[:-1, RS:]], axis=0)
        row_total = rows[:, :RS] + row_spill
        resid = got - projected
        scaled = resid / jnp.maximum(row_total, 1.0)[:, :, None, None]
        following = jnp.concatenate([scaled[1:], jnp.zeros_like(scaled[:1])], axis=0)
        reach = jnp.concatenate([scaled, following], axis=1)
        carry = carry + jnp.einsum('siz,siyx->szyx', row_window, reach, precision=PRECISION_HIGH)
        return (carry, resid)
    start = jnp.zeros((SLAB_TOTAL, SLAB_LAYERS, VOLUME_ROWS, DETECTOR_COLUMNS), jnp.float32)
    back, resid = lax.scan(one_angle, start, (window, got_all))
    residual = resid.reshape(ANGLES, R, VOLUME_ROWS, DETECTOR_COLUMNS)
    column_total = lax.optimization_barrier(jnp.sum(window, axis=(0, 2))).reshape(NZ)
    field = volume + back.reshape(NZ, VOLUME_ROWS, DETECTOR_COLUMNS) / column_total[:, None, None]
    field = smooth(field)
    field = smooth(field)
    return (field, residual)
```

```python
import jax
import jax.numpy as jnp
from jax import lax
from jax.sharding import PartitionSpec as P

PRECISION_HIGH = lax.Precision.HIGHEST


def from_behind(block, axis, distance):
    devices = range(lax.axis_size(axis))
    route = [(i - distance, i) for i in devices if i - distance in devices]
    return lax.ppermute(block, axis, route)


def extended(cells, sides, width):
    for axis, dim in sides:
        count = lax.axis_size(axis)
        ends = count - 1
        head = lax.slice_in_dim(cells, 0, width, axis=dim)
        tail = lax.slice_in_dim(cells, cells.shape[dim] - width, cells.shape[dim], axis=dim)
        cells = jnp.concatenate(
            [
                lax.ppermute(tail, axis, [(i, (i + 1) % count) for i in range(ends)]),
                cells,
                lax.ppermute(head, axis, [((i + 1) % count, i) for i in range(ends)]),
            ],
            axis=dim,
        )
    return cells


def sweep(padded):
    base = padded[:-1]
    grad_z = padded[1:] - base
    grad_y = jnp.concatenate([base[:, 1:] - base[:, :-1], jnp.zeros_like(base[:, :1])], axis=1)
    grad_x = jnp.concatenate(
        [base[:, :, 1:] - base[:, :, :-1], jnp.zeros_like(base[:, :, :1])], axis=2
    )
    size = jnp.sqrt(grad_z * grad_z + grad_y * grad_y + grad_x * grad_x + 0.01)
    flow_z = grad_z / size
    flow_y = (grad_y / size)[1:]
    flow_x = (grad_x / size)[1:]
    div = flow_z[1:] - flow_z[:-1]
    div = div + flow_y - jnp.concatenate([jnp.zeros_like(flow_y[:, :1]), flow_y[:, :-1]], axis=1)
    div = (
        div
        + flow_x
        - jnp.concatenate([jnp.zeros_like(flow_x[:, :, :1]), flow_x[:, :, :-1]], axis=2)
    )
    return padded[1:-1] + 0.05 * div


RING = 4


def from_ring(block, distance):
    return lax.ppermute(block, "ang", [(a, (a + 2 * distance) % 8) for a in range(8)])


def from_far(block):
    return lax.ppermute(block, "ang", [(a, a ^ 1) for a in range(8)])


def summed_over_angles(planes, totals):
    rows = planes.shape[1] // RING
    place = lax.axis_index("ang") // 2
    packed = jnp.concatenate(
        [
            planes.reshape(4, RING, rows, 1024).transpose(1, 0, 2, 3).reshape(RING, 4 * rows, 1024),
            jnp.broadcast_to(jnp.pad(totals, (0, 4))[None, :, None], (RING, 8, 1024)),
        ],
        axis=1,
    )

    def piece(distance):
        return lax.dynamic_index_in_dim(packed, (place + distance) % RING, 0, keepdims=False)

    mine = piece(0) + from_ring(piece(1), 1) + from_ring(piece(3), 3) + from_ring(piece(2), 2)
    mine = mine + from_far(mine)
    whole = jnp.zeros((4, RING, rows, 1024), jnp.float32)
    block = mine[: 4 * rows].reshape(4, 1, rows, 1024)
    for distance in range(RING):
        got = block if distance == 0 else from_ring(block, distance)
        whole = lax.dynamic_update_slice_in_dim(whole, got, (place - distance) % RING, 1)
    return whole.reshape(planes.shape), mine[4 * rows : 4 * rows + 4, 0]


def per_device(weights, shifts, bands, volume, measured):
    angles_dev, band_rows, layers = weights.shape
    own_rows = measured.shape[1]
    rows_i = jnp.arange(band_rows, dtype=jnp.int32)[:, None]
    rows_j = jnp.arange(band_rows, dtype=jnp.int32)[None, :]
    placer = ((rows_i == rows_j + shifts[0, 0]) & (rows_j < bands[0, 0])).astype(jnp.float32)
    window = jnp.einsum("ij,ajz->aiz", placer, weights, precision=PRECISION_HIGH)
    partial_value = jnp.einsum("aiz,zyx->aiyx", window, volume, precision=PRECISION_HIGH)
    row_part = jnp.sum(window, axis=2)
    arrived = from_behind((partial_value[:, own_rows:], row_part[:, own_rows:]), "slab", 1)
    projected = partial_value[:, :own_rows] + arrived[0]
    row_total = row_part[:, :own_rows] + arrived[1]
    residual = measured.astype(jnp.float32) - projected
    scaled = residual / jnp.maximum(row_total, 1.0)[:, :, None, None]
    following = from_behind(scaled, "slab", -1)
    reach = jnp.concatenate([scaled, following], axis=1)
    back_part = jnp.einsum("aiz,aiyx->zyx", window, reach, precision=PRECISION_HIGH)
    column_part = jnp.sum(window, axis=(0, 1))
    back, column_total = summed_over_angles(back_part, column_part)
    field = volume + back / column_total[:, None, None]
    for sweep_turn in range(2):
        padded = extended(field, (("slab", 0),), 1)
        field = sweep(padded)
    return (field, residual)


def solution(mesh):
    return jax.shard_map(
        per_device,
        mesh=mesh,
        in_specs=(
            P("ang", None, "slab"),
            P("ang", "slab"),
            P("ang", "slab"),
            P("slab", None, None),
            P("ang", "slab", None, None),
        ),
        out_specs=(P("slab", None, None), P("ang", "slab", None, None)),
        check_vma=False,
    )
```

```python
import functools

import jax
import jax.numpy as jnp
from jax import lax
from jax.experimental import pallas as pl
from jax.experimental.pallas import tpu as pltpu
from jax.sharding import PartitionSpec as P

TILE = 8
LANES = 128
HALO = 2


def from_behind(block, axis, distance):
    devices = range(lax.axis_size(axis))
    route = [(i - distance, i) for i in devices if i - distance in devices]
    return lax.ppermute(block, axis, route)


def ring_groups():
    count = lax.axis_size("ang")
    return [list(range(0, count, 2)), list(range(1, count, 2))]


def from_far(block):
    return lax.ppermute(block, "ang", [(a, a ^ 1) for a in range(lax.axis_size("ang"))])


def over_ring(pieces):
    return lax.all_to_all(
        pieces, "ang", split_axis=0, concat_axis=0, axis_index_groups=ring_groups()
    )


def tile_rows(z, j, t, ytiles, xtiles):
    return pl.ds(((z * ytiles + j) * xtiles + t) * TILE, TILE)


def spread_kernel(coef_ref, sums_ref, own_ref, next_ref, out_ref):
    angles, rows, depth, columns = own_ref.shape
    layers = coef_ref.shape[1]
    ytiles, xtiles = depth // TILE, columns // LANES
    coefs = [[coef_ref[k, z] for z in range(layers)] for k in range(coef_ref.shape[0])]
    for t in range(xtiles):
        lanes = pl.ds(t * LANES, LANES)
        planes = []
        for ref in (own_ref, next_ref):
            for a in range(angles):
                for r in range(rows):
                    planes.append(ref[a, r, :, lanes].astype(jnp.float32))
        for z in range(layers):
            total = planes[0] * coefs[0][z]
            for k in range(1, len(planes)):
                total = total + planes[k] * coefs[k][z]
            for j in range(ytiles):
                out_ref[0, tile_rows(z, j, t, ytiles, xtiles), :] = total[
                    j * TILE : (j + 1) * TILE
                ]
    body = layers * ytiles * xtiles * TILE
    out_ref[0, body : body + TILE, :] = sums_ref[...]


def spread(coefs, sums, measured, following, ring):
    angles, rows, height, columns = measured.shape
    layers = coefs.shape[1]
    depth = height // ring
    length = layers * depth * columns // LANES + TILE
    block = pl.BlockSpec((angles, rows, depth, columns), lambda i: (0, 0, i, 0))
    return pl.pallas_call(
        spread_kernel,
        grid=(ring,),
        in_specs=[
            pl.BlockSpec(memory_space=pltpu.SMEM),
            pl.BlockSpec((TILE, LANES), lambda i: (0, 0)),
            block,
            block,
        ],
        out_specs=pl.BlockSpec((1, length, LANES), lambda i: (i, 0, 0)),
        out_shape=jax.ShapeDtypeStruct((ring, length, LANES), jnp.float32),
        compiler_params=pltpu.CompilerParams(vmem_limit_bytes=8 * 2**20),
        name="spread",
    )(coefs, sums, measured, following)


def residual_kernel(coef_ref, before_ref, volume_ref, measured_ref, out_ref):
    angles, rows, depth, columns = measured_ref.shape
    layers = volume_ref.shape[0]
    for t in range(columns // LANES):
        lanes = pl.ds(t * LANES, LANES)
        planes = [ref[z, :, lanes] for ref in (before_ref, volume_ref) for z in range(layers)]
        for a in range(angles):
            for r in range(rows):
                total = planes[0] * coef_ref[a * rows + r, 0]
                for k in range(1, len(planes)):
                    total = total + planes[k] * coef_ref[a * rows + r, k]
                out_ref[a, r, :, lanes] = (
                    measured_ref[a, r, :, lanes].astype(jnp.float32) - total
                )


def residual_of(coefs, before, volume, measured):
    angles, rows, height, columns = measured.shape
    layers = volume.shape[0]
    depth = 16
    slab = pl.BlockSpec((layers, depth, columns), lambda i: (0, i, 0))
    block = pl.BlockSpec((angles, rows, depth, columns), lambda i: (0, 0, i, 0))
    return pl.pallas_call(
        residual_kernel,
        grid=(height // depth,),
        in_specs=[pl.BlockSpec(memory_space=pltpu.SMEM), slab, slab, block],
        out_specs=block,
        out_shape=jax.ShapeDtypeStruct(measured.shape, jnp.float32),
        compiler_params=pltpu.CompilerParams(vmem_limit_bytes=8 * 2**20),
        name="residual",
    )(coefs, before, volume, measured)


def update_kernel(place_ref, mine_ref, far_ref, before_ref, volume_ref, after_ref, out_ref, low_ref, high_ref):
    layers, depth, columns = volume_ref.shape
    ytiles, xtiles = depth // TILE, columns // LANES
    body = layers * ytiles * xtiles * TILE
    sums = mine_ref[body : body + TILE, :] + far_ref[body : body + TILE, :]
    share = 1.0 / sums[:, 3 * layers : 3 * layers + 1]
    sums = sums * share

    def splat(value):
        return jnp.broadcast_to(value, (TILE, LANES))

    shares = [splat(share[z : z + 1, :]) for z in range(layers)]
    coefs = [
        [splat(sums[z : z + 1, k : k + 1]) for k in range(3 * layers)] for z in range(layers)
    ]
    for t in range(xtiles):
        lanes = pl.ds(t * LANES, LANES)
        for j in range(ytiles):
            rows = pl.ds(j * TILE, TILE)
            planes = [
                ref[z, rows, lanes]
                for ref in (before_ref, volume_ref, after_ref)
                for z in range(layers)
            ]
            for z in range(layers):
                place = tile_rows(z, j, t, ytiles, xtiles)
                total = (mine_ref[place, :] + far_ref[place, :]) * shares[z]
                for k in range(3 * layers):
                    total = total - planes[k] * coefs[z][k]
                value = planes[layers + z] + total
                out_ref[z, rows, lanes] = value
                if z < HALO:
                    low_ref[z, rows, lanes] = value
                if z >= layers - HALO:
                    high_ref[z - (layers - HALO), rows, lanes] = value


def update(place, mine, far, before, volume, after):
    layers, depth, columns = after.shape
    whole = lambda i, p: (0, 0)
    piece = pl.BlockSpec((layers, depth, columns), lambda i, p: (0, p[0], 0))
    edge = jax.ShapeDtypeStruct((HALO, depth, columns), jnp.float32)
    edge_spec = pl.BlockSpec((HALO, depth, columns), lambda i, p: (0, 0, 0))
    return pl.pallas_call(
        update_kernel,
        grid_spec=pltpu.PrefetchScalarGridSpec(
            num_scalar_prefetch=1,
            grid=(1,),
            in_specs=[
                pl.BlockSpec(mine.shape, whole),
                pl.BlockSpec(far.shape, whole),
                piece,
                piece,
                pl.BlockSpec((layers, depth, columns), lambda i, p: (0, 0, 0)),
            ],
            out_specs=[
                pl.BlockSpec((layers, depth, columns), lambda i, p: (0, 0, 0)),
                edge_spec,
                edge_spec,
            ],
        ),
        out_shape=[jax.ShapeDtypeStruct(after.shape, jnp.float32), edge, edge],
        compiler_params=pltpu.CompilerParams(vmem_limit_bytes=8 * 2**20),
        name="update",
    )(place, mine, far, before, volume, after)


def smooth_kernel(
    place_ref, own_ref, low_ref, high_ref, left_ref, right_ref, out_ref, field, flow_z, flow_y, flow_x
):
    layers, depth, columns = own_ref.shape
    deep = layers + 2 * HALO
    tall = field.shape[1]
    first = place_ref[0] * depth - HALO
    last = place_ref[1] - 1
    keep_low = place_ref[2].astype(jnp.float32)
    keep_high = place_ref[3].astype(jnp.float32)
    field[...] = jnp.zeros(field.shape, jnp.float32)
    field[0:HALO, HALO : HALO + depth, :] = low_ref[...]
    field[HALO : HALO + layers, HALO : HALO + depth, :] = own_ref[...]
    field[HALO + layers :, HALO : HALO + depth, :] = high_ref[...]
    field[:, 0:HALO, :] = left_ref[...]
    field[:, HALO + depth : 2 * HALO + depth, :] = right_ref[...]
    flow_y[:, 0:TILE, :] = jnp.zeros((flow_y.shape[0], TILE, columns), jnp.float32)
    inner_x = lax.broadcasted_iota(jnp.int32, (TILE, columns), 1) < columns - 1
    first_x = lax.broadcasted_iota(jnp.int32, (TILE, columns), 1) == 0
    tiles = (depth + 2 * HALO + TILE - 1) // TILE
    inner_y = []
    for i in range(tiles):
        rows = lax.broadcasted_iota(jnp.int32, (TILE, columns), 0) + (i * TILE + first)
        inner_y.append((rows >= 0) & (rows < last))

    for turn in range(2):
        for z in range(turn, deep - 1 - turn):
            for i in range(tiles):
                rows = pl.ds(i * TILE, TILE)
                base = field[z, rows, :]
                grad_z = field[z + 1, rows, :] - base
                grad_y = jnp.where(inner_y[i], field[z, pl.ds(i * TILE + 1, TILE), :] - base, 0.0)
                grad_x = jnp.where(inner_x, pltpu.roll(base, columns - 1, 1) - base, 0.0)
                scale = lax.rsqrt(grad_z * grad_z + grad_y * grad_y + grad_x * grad_x + 0.01)
                flow_z[z, rows, :] = grad_z * scale
                if z > turn:
                    flow_y[z, pl.ds((i + 1) * TILE, TILE), :] = grad_y * scale
                    across = grad_x * scale
                    flow_x[z, rows, :] = across - jnp.where(
                        first_x, 0.0, pltpu.roll(across, 1, 1)
                    )
        for z in range(turn + 1, deep - 1 - turn):
            for i in range(tiles):
                rows = pl.ds(i * TILE, TILE)
                div = flow_z[z, rows, :] - flow_z[z - 1, rows, :] + flow_x[z, rows, :]
                div = div + (
                    flow_y[z, pl.ds((i + 1) * TILE, TILE), :]
                    - flow_y[z, pl.ds((i + 1) * TILE - 1, TILE), :]
                )
                value = field[z, rows, :] + 0.05 * div
                if turn == 0 and z == HALO - 1:
                    value = value * keep_low
                if turn == 0 and z == HALO + layers:
                    value = value * keep_high
                field[z, rows, :] = value
    for copy in range(out_ref.shape[0]):
        for z in range(layers):
            out_ref[copy, z, :, :] = field[HALO + z, HALO : HALO + depth, :]


def smooth(place, own, low, high, left, right, copies):
    layers, depth, columns = own.shape
    deep, tall = layers + 2 * HALO, depth + 2 * TILE
    return pl.pallas_call(
        smooth_kernel,
        in_specs=[pl.BlockSpec(memory_space=pltpu.SMEM)]
        + [pl.BlockSpec(memory_space=pltpu.VMEM)] * 5,
        out_specs=pl.BlockSpec(memory_space=pltpu.VMEM),
        out_shape=jax.ShapeDtypeStruct((copies,) + own.shape, jnp.float32),
        scratch_shapes=[pltpu.VMEM((deep, tall, columns), jnp.float32)]
        + [pltpu.VMEM((deep, tall, columns), jnp.float32)] * 3,
        compiler_params=pltpu.CompilerParams(vmem_limit_bytes=16 * 2**20),
        name="smooth",
    )(place, own, low, high, left, right)


def windows(weights, shifts, bands):
    band_rows = weights.shape[1]
    rows_i = jnp.arange(band_rows, dtype=jnp.int32)[:, None]
    rows_j = jnp.arange(band_rows, dtype=jnp.int32)[None, :]
    placer = ((rows_i == rows_j + shifts[0, 0]) & (rows_j < bands[0, 0])).astype(jnp.float32)
    return jnp.sum(placer[None, :, :, None] * weights[:, None, :, :], axis=2)


def per_device(weights, shifts, bands, volume, measured):
    layers, height, columns = volume.shape
    own_rows = measured.shape[1]
    ring = lax.axis_size("ang") // 2
    depth = height // ring
    x = lax.axis_index("ang") // 2
    slab = lax.axis_index("slab")
    last_slab = lax.axis_size("slab") - 1

    before = from_behind(volume, "slab", 1)
    following = from_behind(measured.astype(jnp.float32), "slab", -1)
    piece = lax.dynamic_slice_in_dim(volume, x * depth, depth, 1)
    after = from_behind(piece, "slab", -1)

    window = windows(weights, shifts, bands)
    window_before = from_behind(window, "slab", 1)
    window_after = from_behind(window, "slab", -1)
    low, high = window[:, :own_rows], window[:, own_rows:]
    low_after, high_before = window_after[:, :own_rows], window_before[:, own_rows:]
    total_own = jnp.sum(low, axis=2) + jnp.sum(high_before, axis=2)
    total_next = jnp.sum(low_after, axis=2) + jnp.sum(high, axis=2)
    share_own = 1.0 / jnp.maximum(total_own, 1.0)
    share_next = jnp.where(slab < last_slab, 1.0 / jnp.maximum(total_next, 1.0), 0.0)
    count = low.shape[0] * own_rows
    back_coefs = jnp.concatenate(
        [
            (low * share_own[:, :, None]).reshape(count, layers),
            (high * share_next[:, :, None]).reshape(count, layers),
        ]
    )
    nothing = jnp.zeros((count, layers), jnp.float32)
    flat = lambda block: block.reshape(count, layers)
    own_coefs = jnp.concatenate([flat(high_before), flat(low)], axis=1)
    forward_coefs = jnp.concatenate(
        [
            jnp.concatenate([own_coefs, nothing], axis=1),
            jnp.concatenate([nothing, flat(high), flat(low_after)], axis=1),
        ]
    )
    normal = jnp.sum(back_coefs[:, :, None] * forward_coefs[:, None, :], axis=0)
    column_part = jnp.sum(window, axis=(0, 1))
    sums = jnp.concatenate([normal, column_part[:, None]], axis=1)
    sums = jnp.pad(sums, ((0, TILE - layers), (0, LANES - 3 * layers - 1)))

    sent = spread(back_coefs, sums, measured, following, ring)
    mine = jnp.sum(over_ring(sent), axis=0)
    far = from_far(mine)
    residual = residual_of(own_coefs, before, volume, measured)
    place = jnp.stack([x]).astype(jnp.int32)
    field, edge_low, edge_high = update(place, mine, far, before, volume, after)

    halo_low = from_behind(edge_high, "slab", 1)
    halo_high = from_behind(edge_low, "slab", -1)
    deep = jnp.concatenate([halo_low, field, halo_high], axis=0)
    neighbours = [(a, a + 2) for a in range(2 * ring - 2)]
    halo_left = lax.ppermute(deep[:, depth - HALO :], "ang", neighbours)
    halo_right = lax.ppermute(deep[:, :HALO], "ang", [(b, a) for a, b in neighbours])
    place = jnp.stack(
        [x, jnp.int32(height), (slab > 0).astype(jnp.int32), (slab < last_slab).astype(jnp.int32)]
    ).astype(jnp.int32)
    pieces = smooth(place, field, halo_low, halo_high, halo_left, halo_right, ring)
    whole = over_ring(pieces)
    updated = whole.transpose(1, 0, 2, 3).reshape(volume.shape)
    return (updated, residual)


def solution(mesh):
    return jax.shard_map(
        per_device,
        mesh=mesh,
        in_specs=(
            P("ang", None, "slab"),
            P("ang", "slab"),
            P("ang", "slab"),
            P("slab", None, None),
            P("ang", "slab", None, None),
        ),
        out_specs=(P("slab", None, None), P("ang", "slab", None, None)),
        check_vma=False,
    )
```

```python
import jax
import jax.numpy as jnp
from jax import lax
from jax.experimental import pallas as pl
from jax.experimental.pallas import tpu as pltpu
from jax.sharding import PartitionSpec as P

TILE = 8
LANES = 128
HALO = 2


def from_behind(block, axis, distance):
    devices = range(lax.axis_size(axis))
    route = [(i - distance, i) for i in devices if i - distance in devices]
    return lax.ppermute(block, axis, route)


def ring_groups():
    count = lax.axis_size("ang")
    return [list(range(0, count, 2)), list(range(1, count, 2))]


def from_far(block):
    return lax.ppermute(block, "ang", [(a, a ^ 1) for a in range(lax.axis_size("ang"))])


def over_ring(pieces):
    return lax.all_to_all(
        pieces, "ang", split_axis=0, concat_axis=0, axis_index_groups=ring_groups()
    )


VMEM = pl.BlockSpec(memory_space=pltpu.VMEM)
SMEM = pl.BlockSpec(memory_space=pltpu.SMEM)
ANY = pl.BlockSpec(memory_space=pl.ANY)


def pack_kernel(place_ref, window_ref, volume_ref, measured_ref, back_ref, ahead_ref):
    angles, rows, height, columns = measured_ref.shape
    layers, depth = volume_ref.shape[:2]
    for a in range(angles):
        for r in range(rows):
            back_ref[pl.ds((a * rows + r) * height, height), :] = measured_ref[a, r].astype(
                jnp.float32
            )
    base = angles * rows * height
    for z in range(layers):
        piece = volume_ref[z]
        back_ref[pl.ds(base + z * depth, depth), :] = piece
        ahead_ref[pl.ds(z * depth, depth), :] = piece
    back_ref[pl.ds(base + layers * depth, TILE), :] = window_ref[...]
    ahead_ref[pl.ds(layers * depth, TILE), :] = window_ref[...]


def pack(place, window, volume, measured, depth):
    angles, rows, height, columns = measured.shape
    layers = volume.shape[0]
    small = layers * depth + TILE
    shape = lambda n: jax.ShapeDtypeStruct((n, columns), jnp.float32)
    large = angles * rows * height + small
    return pl.pallas_call(
        pack_kernel,
        grid_spec=pltpu.PrefetchScalarGridSpec(
            num_scalar_prefetch=1,
            grid=(1,),
            in_specs=[
                pl.BlockSpec((TILE, columns), lambda i, p: (0, 0)),
                pl.BlockSpec((layers, depth, columns), lambda i, p: (0, p[0], 0)),
                pl.BlockSpec(measured.shape, lambda i, p: (0, 0, 0, 0)),
            ],
            out_specs=[
                pl.BlockSpec((large, columns), lambda i, p: (0, 0)),
                pl.BlockSpec((small, columns), lambda i, p: (0, 0)),
            ],
        ),
        out_shape=[shape(large), shape(small)],
        compiler_params=pltpu.CompilerParams(vmem_limit_bytes=12 * 2**20),
        name="pack",
    )(place, window, volume, measured)


def spread_kernel(coef_ref, sums_ref, own_ref, next_ref, out_ref):
    angles, rows, height, columns = own_ref.shape
    count, layers = coef_ref.shape
    ring = out_ref.shape[0]
    depth = height // ring
    ytiles, xtiles = depth // TILE, columns // LANES
    coefs = [[coef_ref[k, z] for z in range(layers)] for k in range(count)]
    body = layers * ytiles * xtiles * TILE

    def chunk(i, carry):
        top = pl.multiple_of(i * depth, depth)
        for t in range(xtiles):
            lanes = pl.ds(t * LANES, LANES)
            planes = []
            for a in range(angles):
                for r in range(rows):
                    planes.append(own_ref[a, r, pl.ds(top, depth), lanes].astype(jnp.float32))
            for k in range(angles * rows):
                planes.append(next_ref[pl.ds(k * height + top, depth), lanes])
            for z in range(layers):
                total = planes[0] * coefs[0][z]
                for k in range(1, count):
                    total = total + planes[k] * coefs[k][z]
                for j in range(ytiles):
                    row = ((z * ytiles + j) * xtiles + t) * TILE
                    out_ref[i, row : row + TILE, :] = total[j * TILE : (j + 1) * TILE]
        out_ref[i, body : body + TILE, :] = sums_ref[...]
        return carry

    lax.fori_loop(0, ring, chunk, 0)


def spread(coefs, sums, measured, following, ring):
    height, columns = measured.shape[2:]
    length = coefs.shape[1] * (height // ring) * columns // LANES + TILE
    return pl.pallas_call(
        spread_kernel,
        in_specs=[SMEM, VMEM, VMEM, VMEM],
        out_specs=VMEM,
        out_shape=jax.ShapeDtypeStruct((ring, length, LANES), jnp.float32),
        compiler_params=pltpu.CompilerParams(vmem_limit_bytes=8 * 2**20),
        name="spread",
    )(coefs, sums, measured, following)


def gather_kernel(parts_ref, before_ref, mine_ref, copies_ref):
    ring, length, _ = parts_ref.shape
    step = 40

    def add(i, carry):
        rows = pl.ds(pl.multiple_of(i * step, TILE), step)
        total = parts_ref[0, rows, :]
        for part in range(1, ring):
            total = total + parts_ref[part, rows, :]
        mine_ref[rows, :] = total
        return carry

    lax.fori_loop(0, length // step, add, 0)
    for done in range(length // step * step, length, TILE):
        total = parts_ref[0, done : done + TILE, :]
        for part in range(1, ring):
            total = total + parts_ref[part, done : done + TILE, :]
        mine_ref[done : done + TILE, :] = total

    def copy(i, carry):
        rows = pl.ds(pl.multiple_of(i * TILE, TILE), TILE)
        piece = before_ref[rows, :]
        for part in range(ring):
            copies_ref[part, rows, :] = piece
        return carry

    lax.fori_loop(0, copies_ref.shape[1] // TILE, copy, 0)


def gather(parts, before, height):
    ring, length, _ = parts.shape
    return pl.pallas_call(
        gather_kernel,
        in_specs=[VMEM, VMEM],
        out_specs=[VMEM, VMEM],
        out_shape=[
            jax.ShapeDtypeStruct((length, LANES), jnp.float32),
            jax.ShapeDtypeStruct((ring, height, before.shape[1]), jnp.float32),
        ],
        compiler_params=pltpu.CompilerParams(vmem_limit_bytes=8 * 2**20),
        name="gather",
    )(parts, before)


def residual_kernel(coef_ref, before_ref, volume_ref, measured_ref, out_ref, done_ref):
    done_ref[...] = jnp.zeros_like(done_ref)
    angles, rows, depth, columns = measured_ref.shape
    layers = volume_ref.shape[0]
    coefs = [[coef_ref[k, z] for z in range(2 * layers)] for k in range(angles * rows)]
    for t in range(columns // LANES):
        lanes = pl.ds(t * LANES, LANES)
        planes = [before_ref[0, pl.ds(z * depth, depth), lanes] for z in range(layers)]
        planes += [volume_ref[z, :, lanes] for z in range(layers)]
        for a in range(angles):
            for r in range(rows):
                total = planes[0] * coefs[a * rows + r][0]
                for k in range(1, len(planes)):
                    total = total + planes[k] * coefs[a * rows + r][k]
                out_ref[a, r, :, lanes] = (
                    measured_ref[a, r, :, lanes].astype(jnp.float32) - total
                )


def residual_of(coefs, before, volume, measured):
    angles, rows, height, columns = measured.shape
    layers = volume.shape[0]
    ring = before.shape[0]
    depth = height // ring
    slab = pl.BlockSpec((layers, depth, columns), lambda i: (0, i, 0))
    block = pl.BlockSpec((angles, rows, depth, columns), lambda i: (0, 0, i, 0))
    return pl.pallas_call(
        residual_kernel,
        grid=(ring,),
        in_specs=[
            SMEM,
            pl.BlockSpec((1, layers * depth, columns), lambda i: (i, 0, 0)),
            slab,
            block,
        ],
        out_specs=[block, pl.BlockSpec((TILE, LANES), lambda i: (0, 0))],
        out_shape=[
            jax.ShapeDtypeStruct(measured.shape, jnp.float32),
            jax.ShapeDtypeStruct((TILE, LANES), jnp.float32),
        ],
        compiler_params=pltpu.CompilerParams(vmem_limit_bytes=8 * 2**20),
        name="residual",
    )(coefs, before, volume, measured)


def update_kernel(place_ref, mine_ref, far_ref, before_ref, volume_ref, back_ref, done_ref, out_ref):
    layers, depth, columns = volume_ref.shape
    ytiles, xtiles = depth // TILE, columns // LANES
    body = layers * ytiles * xtiles * TILE
    first = back_ref.shape[0] - TILE - layers * depth
    sums = mine_ref[body : body + TILE, :] + far_ref[body : body + TILE, :]
    share = 1.0 / sums[:, 3 * layers : 3 * layers + 1]
    sums = sums * share

    def splat(value):
        return jnp.broadcast_to(value, (TILE, LANES))

    shares = [splat(share[z : z + 1, :]) for z in range(layers)]
    coefs = [
        [splat(sums[z : z + 1, k : k + 1]) for k in range(3 * layers)] for z in range(layers)
    ]
    for t in range(xtiles):
        lanes = pl.ds(t * LANES, LANES)
        for j in range(ytiles):
            planes = [
                before_ref[pl.ds(z * depth + j * TILE, TILE), lanes] for z in range(layers)
            ]
            planes += [volume_ref[z, pl.ds(j * TILE, TILE), lanes] for z in range(layers)]
            planes += [
                back_ref[pl.ds(first + z * depth + j * TILE, TILE), lanes]
                for z in range(layers)
            ]
            for z in range(layers):
                row = ((z * ytiles + j) * xtiles + t) * TILE
                total = (mine_ref[row : row + TILE, :] + far_ref[row : row + TILE, :]) * shares[z]
                for k in range(3 * layers):
                    total = total - planes[k] * coefs[z][k]
                value = planes[layers + z] + total
                for copy in range(out_ref.shape[0]):
                    out_ref[copy, z, pl.ds(j * TILE, TILE), lanes] = value


def update(place, mine, far, before, volume, back, done, ring):
    layers, height, columns = volume.shape
    depth = height // ring
    whole = lambda i, p: (0, 0)
    return pl.pallas_call(
        update_kernel,
        grid_spec=pltpu.PrefetchScalarGridSpec(
            num_scalar_prefetch=1,
            grid=(1,),
            in_specs=[
                pl.BlockSpec(mine.shape, whole),
                pl.BlockSpec(far.shape, whole),
                pl.BlockSpec(before.shape, whole),
                pl.BlockSpec((layers, depth, columns), lambda i, p: (0, p[0], 0)),
                pl.BlockSpec(back.shape, whole),
                ANY,
            ],
            out_specs=pl.BlockSpec((ring, layers, depth, columns), lambda i, p: (0, 0, 0, 0)),
        ),
        out_shape=jax.ShapeDtypeStruct((ring, layers, depth, columns), jnp.float32),
        compiler_params=pltpu.CompilerParams(vmem_limit_bytes=12 * 2**20),
        name="update",
    )(place, mine, far, before, volume, back, done)


def sweep(source, target, edge, lowest, highest):
    tall, columns = source.shape[1:]
    height = tall - TILE
    xtiles = columns // LANES
    lane = lax.broadcasted_iota(jnp.int32, (TILE, LANES), 1)
    level = lax.broadcasted_iota(jnp.int32, (TILE, LANES), 0)
    last_lane, first_lane = lane == LANES - 1, lane == 0
    last_row, first_row = level == TILE - 1, level == 0
    spans = [pl.ds(t * LANES, LANES) for t in range(xtiles)]
    for z in range(lowest, highest + 1):
        edge[z, :, :] = jnp.zeros((TILE, columns), jnp.float32)

    def band(i, carry):
        top = pl.multiple_of(i * TILE, TILE)
        rows = pl.ds(top, TILE)
        below = pl.ds(top + TILE, 1)
        upper = [source[lowest - 1, rows, span] for span in spans]
        flow_z = None
        for z in range(lowest - 1, highest + 1):
            base, upper = upper, [source[z + 1, rows, span] for span in spans]
            turned = [pltpu.roll(b, LANES - 1, 1) for b in base]
            grad_z, along, scaled = [], [], []
            for t in range(xtiles):
                rise = upper[t] - base[t]
                nearby = jnp.where(
                    last_row,
                    jnp.broadcast_to(source[z, below, spans[t]], (TILE, LANES)),
                    pltpu.roll(base[t], TILE - 1, 0),
                )
                down = nearby - base[t]
                right = jnp.where(
                    last_lane, turned[t + 1] if t + 1 < xtiles else base[t], turned[t]
                )
                across = right - base[t]
                scale = lax.rsqrt(rise * rise + down * down + across * across + 0.01)
                grad_z.append(rise * scale)
                along.append(down * scale)
                scaled.append(across * scale)
            if z >= lowest:
                moved = [pltpu.roll(p, 1, 1) for p in scaled]
                for t in range(xtiles):
                    left = jnp.where(first_lane, moved[t - 1] if t else 0.0, moved[t])
                    above = jnp.where(
                        first_row,
                        jnp.broadcast_to(edge[z, TILE - 1 : TILE, spans[t]], (TILE, LANES)),
                        pltpu.roll(along[t], 1, 0),
                    )
                    edge[z, :, spans[t]] = along[t]
                    div = (grad_z[t] - flow_z[t]) + (along[t] - above) + (scaled[t] - left)
                    target(z, rows, spans[t], base[t] + 0.05 * div)
            flow_z = grad_z
        return carry

    lax.fori_loop(0, height // TILE, band, 0)


def smooth_kernel(place_ref, own_ref, low_ref, high_ref, out_ref, field, middle, edge):
    ring, layers, depth, columns = own_ref.shape
    height = ring * depth
    keep_low = place_ref[0].astype(jnp.float32)
    keep_high = place_ref[1].astype(jnp.float32)

    def fill(i, carry):
        top = pl.multiple_of(i * depth, depth)
        for z in range(HALO):
            field[z, pl.ds(top, depth), :] = low_ref[i, z]
            field[HALO + layers + z, pl.ds(top, depth), :] = high_ref[i, z]
        for z in range(layers):
            field[HALO + z, pl.ds(top, depth), :] = own_ref[i, z]
        return carry

    lax.fori_loop(0, ring, fill, 0)
    for z in range(layers + 2 * HALO):
        field[z, height : height + 1, :] = field[z, height - 1 : height, :]

    def keep(z, rows, span, value):
        if z == HALO - 1:
            value = value * keep_low
        if z == HALO + layers:
            value = value * keep_high
        middle[z, rows, span] = value

    def finish(z, rows, span, value):
        out_ref[z - HALO, rows, span] = value

    sweep(field, keep, edge, HALO - 1, HALO + layers)
    for z in range(HALO - 1, HALO + layers + 1):
        middle[z, height : height + 1, :] = middle[z, height - 1 : height, :]
    sweep(middle, finish, edge, HALO, HALO + layers - 1)


def smooth(place, own, low, high):
    ring, layers, depth, columns = own.shape
    deep, height = layers + 2 * HALO, ring * depth
    return pl.pallas_call(
        smooth_kernel,
        in_specs=[SMEM, VMEM, VMEM, VMEM],
        out_specs=VMEM,
        out_shape=jax.ShapeDtypeStruct((layers, height, columns), jnp.float32),
        scratch_shapes=[
            pltpu.VMEM((deep, height + TILE, columns), jnp.float32),
            pltpu.VMEM((deep, height + TILE, columns), jnp.float32),
            pltpu.VMEM((deep, TILE, columns), jnp.float32),
        ],
        compiler_params=pltpu.CompilerParams(vmem_limit_bytes=16 * 2**20),
        name="smooth",
    )(place, own, low, high)


def windows(weights, shifts, bands):
    band_rows = weights.shape[1]
    rows_i = jnp.arange(band_rows, dtype=jnp.int32)[:, None]
    rows_j = jnp.arange(band_rows, dtype=jnp.int32)[None, :]
    placer = ((rows_i == rows_j + shifts[0, 0]) & (rows_j < bands[0, 0])).astype(jnp.float32)
    return jnp.sum(placer[None, :, :, None] * weights[:, None, :, :], axis=2)


def per_device(weights, shifts, bands, volume, measured):
    layers, height, columns = volume.shape
    own_rows = measured.shape[1]
    ring = lax.axis_size("ang") // 2
    depth = height // ring
    place = (lax.axis_index("ang") // 2).astype(jnp.int32).reshape(1)
    slab = lax.axis_index("slab")
    last_slab = lax.axis_size("slab") - 1

    window = windows(weights, shifts, bands)
    line = jnp.pad(window.reshape(1, -1), ((0, TILE - 1), (0, columns - window.size)))
    back, ahead = pack(place, line, volume, measured, depth)
    following = from_behind(back, "slab", -1)
    before = from_behind(ahead, "slab", 1)
    unpacked = lambda block: block[-TILE, : window.size].reshape(window.shape)
    window_after, window_before = unpacked(following), unpacked(before)

    low, high = window[:, :own_rows], window[:, own_rows:]
    low_after, high_before = window_after[:, :own_rows], window_before[:, own_rows:]
    total_own = jnp.sum(low, axis=2) + jnp.sum(high_before, axis=2)
    total_next = jnp.sum(low_after, axis=2) + jnp.sum(high, axis=2)
    share_own = 1.0 / jnp.maximum(total_own, 1.0)
    share_next = jnp.where(slab < last_slab, 1.0 / jnp.maximum(total_next, 1.0), 0.0)
    count = low.shape[0] * own_rows
    back_coefs = jnp.concatenate(
        [
            (low * share_own[:, :, None]).reshape(count, layers),
            (high * share_next[:, :, None]).reshape(count, layers),
        ]
    )
    nothing = jnp.zeros((count, layers), jnp.float32)
    flat = lambda block: block.reshape(count, layers)
    own_coefs = jnp.concatenate([flat(high_before), flat(low)], axis=1)
    forward_coefs = jnp.concatenate(
        [
            jnp.concatenate([own_coefs, nothing], axis=1),
            jnp.concatenate([nothing, flat(high), flat(low_after)], axis=1),
        ]
    )
    normal = jnp.sum(back_coefs[:, :, None] * forward_coefs[:, None, :], axis=0)
    column_part = jnp.sum(window, axis=(0, 1))
    sums = jnp.concatenate([normal, column_part[:, None]], axis=1)
    sums = jnp.pad(sums, ((0, TILE - layers), (0, LANES - 3 * layers - 1)))

    sent = spread(back_coefs, sums, measured, following, ring)
    mine, copies = gather(over_ring(sent), before, layers * depth)
    far = from_far(mine)
    residual, done = residual_of(own_coefs, over_ring(copies), volume, measured)
    pieces = update(place, mine, far, before, volume, following, done, ring)
    field = over_ring(pieces)
    halo_low = from_behind(field[:, layers - HALO :], "slab", 1)
    halo_high = from_behind(field[:, :HALO], "slab", -1)
    keep = jnp.stack([slab > 0, slab < last_slab]).astype(jnp.int32)
    updated = smooth(keep, field, halo_low, halo_high)
    return (updated, residual)


def solution(mesh):
    return jax.shard_map(
        per_device,
        mesh=mesh,
        in_specs=(
            P("ang", None, "slab"),
            P("ang", "slab"),
            P("ang", "slab"),
            P("slab", None, None),
            P("ang", "slab", None, None),
        ),
        out_specs=(P("slab", None, None), P("ang", "slab", None, None)),
        check_vma=False,
    )
```

```python
import jax
import jax.numpy as jnp
from jax import lax
from jax.experimental import pallas as pl
from jax.experimental.pallas import tpu as pltpu
from jax.sharding import PartitionSpec as P

TILE = 8
LANES = 128
HALO = 2


def from_behind(block, axis, distance):
    devices = range(lax.axis_size(axis))
    route = [(i - distance, i) for i in devices if i - distance in devices]
    return lax.ppermute(block, axis, route)


def ring_groups():
    count = lax.axis_size("ang")
    return [list(range(0, count, 2)), list(range(1, count, 2))]


def from_far(block):
    return lax.ppermute(block, "ang", [(a, a ^ 1) for a in range(lax.axis_size("ang"))])


def over_ring(pieces):
    return lax.all_to_all(
        pieces, "ang", split_axis=0, concat_axis=0, axis_index_groups=ring_groups()
    )


VMEM = pl.BlockSpec(memory_space=pltpu.VMEM)
SMEM = pl.BlockSpec(memory_space=pltpu.SMEM)
ANY = pl.BlockSpec(memory_space=pl.ANY)


def pack_kernel(window_ref, measured_ref, *back_refs):
    angles, rows, height, columns = measured_ref.shape
    parts = len(back_refs)
    depth = parts * TILE
    for a in range(angles):
        for r in range(rows):
            for i in range(height // depth):
                block = measured_ref[a, r, i * depth : (i + 1) * depth, :].astype(jnp.float32)
                row = ((a * rows + r) * (height // depth) + i) * TILE
                for part in range(parts):
                    back_refs[part][row : row + TILE, :] = block[
                        part * TILE : (part + 1) * TILE
                    ]
    back_refs[0][angles * rows * height // parts :, :] = window_ref[...]


def pack(window, measured, parts):
    angles, rows, height, columns = measured.shape
    length = angles * rows * height // parts
    return pl.pallas_call(
        pack_kernel,
        in_specs=[VMEM, VMEM],
        out_specs=[VMEM] * parts,
        out_shape=[
            jax.ShapeDtypeStruct((length + (0 if part else TILE), columns), jnp.float32)
            for part in range(parts)
        ],
        compiler_params=pltpu.CompilerParams(vmem_limit_bytes=8 * 2**20),
        name="pack",
    )(window, measured)


def spread_kernel(coef_ref, sums_ref, own_ref, next_ref, earlier_ref, out_ref):
    count, layers = coef_ref.shape
    ring = out_ref.shape[0]
    columns = own_ref.shape[1]
    xtiles = columns // LANES
    coefs = [[coef_ref[k, z] for z in range(layers)] for k in range(count)]
    body = layers * xtiles * TILE

    def chunk(i, carry):
        for t in range(xtiles):
            lanes = pl.ds(t * LANES, LANES)
            planes = [
                ref[pl.ds(pl.multiple_of((k * ring + i) * TILE, TILE), TILE), lanes]
                for ref in (own_ref, next_ref)
                for k in range(count // 2)
            ]
            for z in range(layers):
                total = planes[0] * coefs[0][z]
                for k in range(1, count):
                    total = total + planes[k] * coefs[k][z]
                row = (z * xtiles + t) * TILE
                out_ref[i, row : row + TILE, :] = total
        out_ref[i, body : body + TILE, :] = sums_ref[...]
        return carry

    lax.fori_loop(0, ring, chunk, 0)


def spread(coefs, sums, own, following, earlier, ring):
    layers, columns = coefs.shape[1], own.shape[1]
    length = layers * TILE * columns // LANES + TILE
    return pl.pallas_call(
        spread_kernel,
        in_specs=[SMEM, VMEM, VMEM, VMEM, ANY],
        out_specs=VMEM,
        out_shape=jax.ShapeDtypeStruct((ring, length, LANES), jnp.float32),
        compiler_params=pltpu.CompilerParams(vmem_limit_bytes=8 * 2**20),
        name="spread",
    )(coefs, sums, own, following, earlier)


def add_parts(parts_ref, mine_ref):
    ring, length, _ = parts_ref.shape
    step = 24 if length % 24 == 0 else TILE

    def add(i, carry):
        rows = pl.ds(pl.multiple_of(i * step, TILE), step)
        total = parts_ref[0, rows, :]
        for part in range(1, ring):
            total = total + parts_ref[part, rows, :]
        mine_ref[rows, :] = total
        return carry

    lax.fori_loop(0, length // step, add, 0)


def gather_kernel(parts_ref, mine_ref):
    add_parts(parts_ref, mine_ref)


def gather(parts):
    return pl.pallas_call(
        gather_kernel,
        in_specs=[VMEM],
        out_specs=VMEM,
        out_shape=jax.ShapeDtypeStruct(parts.shape[1:], jnp.float32),
        compiler_params=pltpu.CompilerParams(vmem_limit_bytes=8 * 2**20),
        name="gather",
    )(parts)


def gather_copy_kernel(parts_ref, before_ref, mine_ref, copies_ref):
    add_parts(parts_ref, mine_ref)
    layers, depth, _ = before_ref.shape

    def copy(i, carry):
        for z in range(layers):
            rows = pl.ds(pl.multiple_of(i * TILE, TILE), TILE)
            piece = before_ref[z, rows, :]
            for part in range(copies_ref.shape[0]):
                copies_ref[part, z, rows, :] = piece
        return carry

    lax.fori_loop(0, depth // TILE, copy, 0)


def gather_copy(parts, before):
    ring = parts.shape[0]
    return pl.pallas_call(
        gather_copy_kernel,
        in_specs=[VMEM, VMEM],
        out_specs=[VMEM, VMEM],
        out_shape=[
            jax.ShapeDtypeStruct(parts.shape[1:], jnp.float32),
            jax.ShapeDtypeStruct((ring,) + before.shape, jnp.float32),
        ],
        compiler_params=pltpu.CompilerParams(vmem_limit_bytes=8 * 2**20),
        name="gather_copy",
    )(parts, before)


def piece_kernel(place_ref, volume_ref, after_spread_ref, out_ref):
    out_ref[...] = volume_ref[...]


def piece_of(place, volume, after_spread, depth):
    layers, _, columns = volume.shape
    return pl.pallas_call(
        piece_kernel,
        grid_spec=pltpu.PrefetchScalarGridSpec(
            num_scalar_prefetch=1,
            grid=(1,),
            in_specs=[pl.BlockSpec((layers, depth, columns), lambda i, p: (0, p[0], 0)), ANY],
            out_specs=pl.BlockSpec((layers, depth, columns), lambda i, p: (0, 0, 0)),
        ),
        out_shape=jax.ShapeDtypeStruct((layers, depth, columns), jnp.float32),
        compiler_params=pltpu.CompilerParams(vmem_limit_bytes=8 * 2**20),
        name="piece",
    )(place, volume, after_spread)


def residual_kernel(coef_ref, before_ref, volume_ref, measured_ref, out_ref, done_ref):
    done_ref[...] = jnp.zeros_like(done_ref)
    angles, rows, depth, columns = measured_ref.shape
    layers = volume_ref.shape[0]
    coefs = [[coef_ref[k, z] for z in range(2 * layers)] for k in range(angles * rows)]
    for t in range(columns // LANES):
        lanes = pl.ds(t * LANES, LANES)
        planes = [before_ref[0, z, :, lanes] for z in range(layers)]
        planes += [volume_ref[z, :, lanes] for z in range(layers)]
        for a in range(angles):
            for r in range(rows):
                total = planes[0] * coefs[a * rows + r][0]
                for k in range(1, len(planes)):
                    total = total + planes[k] * coefs[a * rows + r][k]
                out_ref[a, r, :, lanes] = (
                    measured_ref[a, r, :, lanes].astype(jnp.float32) - total
                )


def residual_of(coefs, before, volume, measured):
    angles, rows, height, columns = measured.shape
    layers = volume.shape[0]
    ring = before.shape[0]
    depth = height // ring
    slab = pl.BlockSpec((layers, depth, columns), lambda i: (0, i, 0))
    block = pl.BlockSpec((angles, rows, depth, columns), lambda i: (0, 0, i, 0))
    return pl.pallas_call(
        residual_kernel,
        grid=(ring,),
        in_specs=[
            SMEM,
            pl.BlockSpec((1, layers, depth, columns), lambda i: (i, 0, 0, 0)),
            slab,
            block,
        ],
        out_specs=[block, pl.BlockSpec((TILE, LANES), lambda i: (0, 0))],
        out_shape=[
            jax.ShapeDtypeStruct(measured.shape, jnp.float32),
            jax.ShapeDtypeStruct((TILE, LANES), jnp.float32),
        ],
        compiler_params=pltpu.CompilerParams(vmem_limit_bytes=8 * 2**20),
        name="residual",
    )(coefs, before, volume, measured)


def update_kernel(mine_ref, far_ref, before_ref, piece_ref, after_ref, earlier_ref, out_ref):
    layers, _, columns = piece_ref.shape
    xtiles = columns // LANES
    body = layers * xtiles * TILE
    sums = mine_ref[body : body + TILE, :] + far_ref[body : body + TILE, :]
    share = 1.0 / sums[:, 3 * layers : 3 * layers + 1]
    sums = sums * share

    def splat(value):
        return jnp.broadcast_to(value, (TILE, LANES))

    shares = [splat(share[z : z + 1, :]) for z in range(layers)]
    coefs = [
        [splat(sums[z : z + 1, k : k + 1]) for k in range(3 * layers)] for z in range(layers)
    ]
    for t in range(xtiles):
        lanes = pl.ds(t * LANES, LANES)
        planes = [
            ref[z, :, lanes] for ref in (before_ref, piece_ref, after_ref) for z in range(layers)
        ]
        for z in range(layers):
            row = (z * xtiles + t) * TILE
            total = (mine_ref[row : row + TILE, :] + far_ref[row : row + TILE, :]) * shares[z]
            for k in range(3 * layers):
                total = total - planes[k] * coefs[z][k]
            value = planes[layers + z] + total
            for copy in range(out_ref.shape[0]):
                out_ref[copy, z, :, lanes] = value


def update(part, mine, far, before, piece, after, earlier, ring):
    layers, _, columns = piece.shape
    whole = lambda i: (0, 0)
    block = pl.BlockSpec((layers, TILE, columns), lambda i: (0, part, 0))
    return pl.pallas_call(
        update_kernel,
        grid=(1,),
        in_specs=[
            pl.BlockSpec(mine.shape, whole),
            pl.BlockSpec(far.shape, whole),
            block,
            block,
            block,
            ANY,
        ],
        out_specs=pl.BlockSpec((ring, layers, TILE, columns), lambda i: (0, 0, 0, 0)),
        out_shape=jax.ShapeDtypeStruct((ring, layers, TILE, columns), jnp.float32),
        compiler_params=pltpu.CompilerParams(vmem_limit_bytes=8 * 2**20),
        name="update",
    )(mine, far, before, piece, after, earlier)


def sweep(source, target, edge, lowest, highest):
    tall, columns = source.shape[1:]
    height = tall - TILE
    xtiles = columns // LANES
    lane = lax.broadcasted_iota(jnp.int32, (TILE, LANES), 1)
    level = lax.broadcasted_iota(jnp.int32, (TILE, LANES), 0)
    last_lane, first_lane = lane == LANES - 1, lane == 0
    last_row, first_row = level == TILE - 1, level == 0
    spans = [pl.ds(t * LANES, LANES) for t in range(xtiles)]
    for z in range(lowest, highest + 1):
        edge[z, :, :] = jnp.zeros((TILE, columns), jnp.float32)

    def band(i, carry):
        top = pl.multiple_of(i * TILE, TILE)
        rows = pl.ds(top, TILE)
        below = pl.ds(top + TILE, 1)
        upper = [source[lowest - 1, rows, span] for span in spans]
        flow_z = None
        for z in range(lowest - 1, highest + 1):
            base, upper = upper, [source[z + 1, rows, span] for span in spans]
            turned = [pltpu.roll(b, LANES - 1, 1) for b in base]
            grad_z, along, scaled = [], [], []
            for t in range(xtiles):
                rise = upper[t] - base[t]
                nearby = jnp.where(
                    last_row,
                    jnp.broadcast_to(source[z, below, spans[t]], (TILE, LANES)),
                    pltpu.roll(base[t], TILE - 1, 0),
                )
                down = nearby - base[t]
                right = jnp.where(
                    last_lane, turned[t + 1] if t + 1 < xtiles else base[t], turned[t]
                )
                across = right - base[t]
                scale = lax.rsqrt(rise * rise + down * down + across * across + 0.01)
                grad_z.append(rise * scale)
                along.append(down * scale)
                scaled.append(across * scale)
            if z >= lowest:
                moved = [pltpu.roll(p, 1, 1) for p in scaled]
                for t in range(xtiles):
                    left = jnp.where(first_lane, moved[t - 1] if t else 0.0, moved[t])
                    above = jnp.where(
                        first_row,
                        jnp.broadcast_to(edge[z, TILE - 1 : TILE, spans[t]], (TILE, LANES)),
                        pltpu.roll(along[t], 1, 0),
                    )
                    edge[z, :, spans[t]] = along[t]
                    div = (grad_z[t] - flow_z[t]) + (along[t] - above) + (scaled[t] - left)
                    target(z, rows, spans[t], base[t] + 0.05 * div)
            flow_z = grad_z
        return carry

    lax.fori_loop(0, height // TILE, band, 0)


def smooth_kernel(place_ref, *refs):
    out_ref, field, middle, edge = refs[-4:]
    parts = len(refs[:-4]) // 3
    own_refs, low_refs, high_refs = (refs[k * parts : (k + 1) * parts] for k in range(3))
    ring, layers = own_refs[0].shape[:2]
    height = out_ref.shape[1]
    keep_low = place_ref[0].astype(jnp.float32)
    keep_high = place_ref[1].astype(jnp.float32)

    def fill(i, carry):
        for part in range(parts):
            rows = pl.ds(pl.multiple_of((i * parts + part) * TILE, TILE), TILE)
            for z in range(HALO):
                field[z, rows, :] = low_refs[part][i, z]
                field[HALO + layers + z, rows, :] = high_refs[part][i, z]
            for z in range(layers):
                field[HALO + z, rows, :] = own_refs[part][i, z]
        return carry

    lax.fori_loop(0, ring, fill, 0)
    for z in range(layers + 2 * HALO):
        field[z, height : height + 1, :] = field[z, height - 1 : height, :]

    def keep(z, rows, span, value):
        if z == HALO - 1:
            value = value * keep_low
        if z == HALO + layers:
            value = value * keep_high
        middle[z, rows, span] = value

    def finish(z, rows, span, value):
        out_ref[z - HALO, rows, span] = value

    sweep(field, keep, edge, HALO - 1, HALO + layers)
    for z in range(HALO - 1, HALO + layers + 1):
        middle[z, height : height + 1, :] = middle[z, height - 1 : height, :]
    sweep(middle, finish, edge, HALO, HALO + layers - 1)


def smooth(place, own, low, high):
    ring, layers, _, columns = own[0].shape
    deep, height = layers + 2 * HALO, ring * len(own) * TILE
    return pl.pallas_call(
        smooth_kernel,
        in_specs=[SMEM] + [VMEM] * (3 * len(own)),
        out_specs=VMEM,
        out_shape=jax.ShapeDtypeStruct((layers, height, columns), jnp.float32),
        scratch_shapes=[
            pltpu.VMEM((deep, height + TILE, columns), jnp.float32),
            pltpu.VMEM((deep, height + TILE, columns), jnp.float32),
            pltpu.VMEM((deep, TILE, columns), jnp.float32),
        ],
        compiler_params=pltpu.CompilerParams(vmem_limit_bytes=16 * 2**20),
        name="smooth",
    )(place, *own, *low, *high)


def windows(weights, shifts, bands):
    band_rows = weights.shape[1]
    rows_i = jnp.arange(band_rows, dtype=jnp.int32)[:, None]
    rows_j = jnp.arange(band_rows, dtype=jnp.int32)[None, :]
    placer = ((rows_i == rows_j + shifts[0, 0]) & (rows_j < bands[0, 0])).astype(jnp.float32)
    return jnp.sum(placer[None, :, :, None] * weights[:, None, :, :], axis=2)


def per_device(weights, shifts, bands, volume, measured):
    layers, height, columns = volume.shape
    own_rows = measured.shape[1]
    ring = lax.axis_size("ang") // 2
    depth = height // ring
    parts = depth // TILE
    place = (lax.axis_index("ang") // 2).astype(jnp.int32).reshape(1)
    slab = lax.axis_index("slab")
    last_slab = lax.axis_size("slab") - 1

    window = windows(weights, shifts, bands)
    line = jnp.pad(window.reshape(1, -1), ((0, TILE - 1), (0, columns - window.size)))
    backs = pack(line, measured, parts)
    following = [from_behind(back, "slab", -1) for back in backs]
    window_before = from_behind(window, "slab", 1)
    window_after = following[0][-TILE, : window.size].reshape(window.shape)

    low, high = window[:, :own_rows], window[:, own_rows:]
    low_after, high_before = window_after[:, :own_rows], window_before[:, own_rows:]
    total_own = jnp.sum(low, axis=2) + jnp.sum(high_before, axis=2)
    total_next = jnp.sum(low_after, axis=2) + jnp.sum(high, axis=2)
    share_own = 1.0 / jnp.maximum(total_own, 1.0)
    share_next = jnp.where(slab < last_slab, 1.0 / jnp.maximum(total_next, 1.0), 0.0)
    count = low.shape[0] * own_rows
    back_coefs = jnp.concatenate(
        [
            (low * share_own[:, :, None]).reshape(count, layers),
            (high * share_next[:, :, None]).reshape(count, layers),
        ]
    )
    nothing = jnp.zeros((count, layers), jnp.float32)
    flat = lambda block: block.reshape(count, layers)
    own_coefs = jnp.concatenate([flat(high_before), flat(low)], axis=1)
    forward_coefs = jnp.concatenate(
        [
            jnp.concatenate([own_coefs, nothing], axis=1),
            jnp.concatenate([nothing, flat(high), flat(low_after)], axis=1),
        ]
    )
    normal = jnp.sum(back_coefs[:, :, None] * forward_coefs[:, None, :], axis=0)
    column_part = jnp.sum(window, axis=(0, 1))
    sums = jnp.concatenate([normal, column_part[:, None]], axis=1)
    sums = jnp.pad(sums, ((0, TILE - layers), (0, LANES - 3 * layers - 1)))

    sent = []
    for back, arrived in zip(backs, following):
        sent.append(spread(back_coefs, sums, back, arrived, sent[-1] if sent else sums, ring))
    piece = piece_of(place, volume, sent[-1], depth)
    before = from_behind(piece, "slab", 1)
    after = from_behind(piece, "slab", -1)
    scattered = [over_ring(block) for block in sent]
    first, copies = gather_copy(scattered[0], before)
    mine = [first] + [gather(block) for block in scattered[1:]]
    far = [from_far(block) for block in mine]
    residual, done = residual_of(own_coefs, over_ring(copies), volume, measured)
    field, halo_low, halo_high = [], [], []
    for part in range(parts):
        earlier = done if part == parts - 1 else sums
        pieces = update(part, mine[part], far[part], before, piece, after, earlier, ring)
        field.append(over_ring(pieces))
        halo_low.append(from_behind(field[part][:, layers - HALO :], "slab", 1))
        halo_high.append(from_behind(field[part][:, :HALO], "slab", -1))
    keep = jnp.stack([slab > 0, slab < last_slab]).astype(jnp.int32)
    updated = smooth(keep, field, halo_low, halo_high)
    return (updated, residual)


def solution(mesh):
    return jax.shard_map(
        per_device,
        mesh=mesh,
        in_specs=(
            P("ang", None, "slab"),
            P("ang", "slab"),
            P("ang", "slab"),
            P("slab", None, None),
            P("ang", "slab", None, None),
        ),
        out_specs=(P("slab", None, None), P("ang", "slab", None, None)),
        check_vma=False,
    )
```

```python
import jax
import jax.numpy as jnp
from jax import lax
from jax.experimental import pallas as pl
from jax.experimental.pallas import tpu as pltpu
from jax.sharding import PartitionSpec as P

TILE = 8
LANES = 128
HALO = 2


def from_behind(block, axis, distance):
    devices = range(lax.axis_size(axis))
    route = [(i - distance, i) for i in devices if i - distance in devices]
    return lax.ppermute(block, axis, route)


def ring_groups():
    count = lax.axis_size("ang")
    return [list(range(0, count, 2)), list(range(1, count, 2))]


def from_far(block):
    return lax.ppermute(block, "ang", [(a, a ^ 1) for a in range(lax.axis_size("ang"))])


def within_chip(block):
    return lax.ppermute(block, "slab", [(s, s ^ 1) for s in range(lax.axis_size("slab"))])


def across_chips(block):
    last = lax.axis_size("slab") - 1
    ahead = [(s, s + 1) for s in range(1, last, 2)]
    return lax.ppermute(block, "slab", ahead + [(b, a) for a, b in ahead])


def over_ring(pieces):
    return lax.all_to_all(
        pieces, "ang", split_axis=0, concat_axis=0, axis_index_groups=ring_groups()
    )


VMEM = pl.BlockSpec(memory_space=pltpu.VMEM)
SMEM = pl.BlockSpec(memory_space=pltpu.SMEM)
ANY = pl.BlockSpec(memory_space=pl.ANY)


def pack_kernel(window_ref, measured_ref, out_ref):
    angles, rows, height, columns = measured_ref.shape
    for a in range(angles):
        for r in range(rows):
            row = (a * rows + r) * height
            out_ref[row : row + height, :] = measured_ref[a, r].astype(jnp.float32)
    out_ref[angles * rows * height :, :] = window_ref[...]


def pack(window, measured):
    angles, rows, height, columns = measured.shape
    return pl.pallas_call(
        pack_kernel,
        in_specs=[VMEM, VMEM],
        out_specs=VMEM,
        out_shape=jax.ShapeDtypeStruct((angles * rows * height + TILE, columns), jnp.float32),
        compiler_params=pltpu.CompilerParams(vmem_limit_bytes=8 * 2**20),
        name="pack",
    )(window, measured)


def spread_kernel(coef_ref, sums_ref, own_ref, next_ref, out_ref):
    count, layers = coef_ref.shape
    ring = out_ref.shape[0]
    columns = own_ref.shape[1]
    height = (own_ref.shape[0] - TILE) // (count // 2)
    depth = height // ring
    ytiles, xtiles = depth // TILE, columns // LANES
    coefs = [[coef_ref[k, z] for z in range(layers)] for k in range(count)]
    body = layers * ytiles * xtiles * TILE

    def chunk(i, carry):
        top = pl.multiple_of(i * depth, depth)
        for t in range(xtiles):
            lanes = pl.ds(t * LANES, LANES)
            planes = [
                ref[pl.ds(k * height + top, depth), lanes]
                for ref in (own_ref, next_ref)
                for k in range(count // 2)
            ]
            for z in range(layers):
                total = planes[0] * coefs[0][z]
                for k in range(1, count):
                    total = total + planes[k] * coefs[k][z]
                for j in range(ytiles):
                    row = ((z * ytiles + j) * xtiles + t) * TILE
                    out_ref[i, row : row + TILE, :] = total[j * TILE : (j + 1) * TILE]
        out_ref[i, body : body + TILE, :] = sums_ref[...]
        return carry

    lax.fori_loop(0, ring, chunk, 0)


def spread(coefs, sums, own, following, height, ring):
    layers, columns = coefs.shape[1], own.shape[1]
    length = layers * (height // ring) * columns // LANES + TILE
    return pl.pallas_call(
        spread_kernel,
        in_specs=[SMEM, VMEM, VMEM, VMEM],
        out_specs=VMEM,
        out_shape=jax.ShapeDtypeStruct((ring, length, LANES), jnp.float32),
        compiler_params=pltpu.CompilerParams(vmem_limit_bytes=8 * 2**20),
        name="spread",
    )(coefs, sums, own, following)


def gather_kernel(parts_ref, before_ref, after_ref, mine_ref):
    ring, length, _ = parts_ref.shape
    step = next(n for n in (5 * TILE, 3 * TILE, TILE) if length % n == 0)

    def add(i, carry):
        rows = pl.ds(pl.multiple_of(i * step, TILE), step)
        total = parts_ref[0, rows, :]
        for part in range(1, ring):
            total = total + parts_ref[part, rows, :]
        mine_ref[rows, :] = total
        return carry

    lax.fori_loop(0, length // step, add, 0)


def gather(parts, before, after):
    return pl.pallas_call(
        gather_kernel,
        in_specs=[VMEM, ANY, ANY],
        out_specs=VMEM,
        out_shape=jax.ShapeDtypeStruct(parts.shape[1:], jnp.float32),
        compiler_params=pltpu.CompilerParams(vmem_limit_bytes=8 * 2**20),
        name="gather",
    )(parts, before, after)


def copies_kernel(block_ref, earlier_ref, out_ref):
    for z in range(block_ref.shape[0]):
        block = block_ref[z]
        for copy in range(out_ref.shape[0]):
            out_ref[copy, z] = block


def copies_of(block, earlier, count):
    shape = (count,) + block.shape
    return pl.pallas_call(
        copies_kernel,
        in_specs=[VMEM, ANY],
        out_specs=VMEM,
        out_shape=jax.ShapeDtypeStruct(shape, jnp.float32),
        compiler_params=pltpu.CompilerParams(vmem_limit_bytes=8 * 2**20),
        cost_estimate=pl.CostEstimate(
            flops=0, bytes_accessed=32 * 2**20, transcendentals=0
        ),
        name="copies",
    )(block, earlier)


def piece_kernel(place_ref, volume_ref, earlier_ref, out_ref):
    out_ref[...] = volume_ref[...]


def piece_of(place, volume, earlier, depth):
    layers, _, columns = volume.shape
    return pl.pallas_call(
        piece_kernel,
        grid_spec=pltpu.PrefetchScalarGridSpec(
            num_scalar_prefetch=1,
            grid=(1,),
            in_specs=[pl.BlockSpec((layers, depth, columns), lambda i, p: (0, p[0], 0)), ANY],
            out_specs=pl.BlockSpec((layers, depth, columns), lambda i, p: (0, 0, 0)),
        ),
        out_shape=jax.ShapeDtypeStruct((layers, depth, columns), jnp.float32),
        compiler_params=pltpu.CompilerParams(vmem_limit_bytes=8 * 2**20),
        cost_estimate=pl.CostEstimate(
            flops=0, bytes_accessed=32 * 2**20, transcendentals=0
        ),
        name="piece",
    )(place, volume, earlier)


def residual_kernel(coef_ref, before_ref, volume_ref, measured_ref, out_ref, done_ref):
    done_ref[...] = jnp.zeros_like(done_ref)
    angles, rows, depth, columns = measured_ref.shape
    layers = volume_ref.shape[0]
    coefs = [[coef_ref[k, z] for z in range(2 * layers)] for k in range(angles * rows)]
    for t in range(columns // LANES):
        lanes = pl.ds(t * LANES, LANES)
        planes = [before_ref[0, z, :, lanes] for z in range(layers)]
        planes += [volume_ref[z, :, lanes] for z in range(layers)]
        for a in range(angles):
            for r in range(rows):
                total = planes[0] * coefs[a * rows + r][0]
                for k in range(1, len(planes)):
                    total = total + planes[k] * coefs[a * rows + r][k]
                out_ref[a, r, :, lanes] = (
                    measured_ref[a, r, :, lanes].astype(jnp.float32) - total
                )


def residual_of(coefs, before, volume, measured):
    angles, rows, height, columns = measured.shape
    ring, layers, depth, _ = before.shape
    block = pl.BlockSpec((angles, rows, depth, columns), lambda i: (0, 0, i, 0))
    return pl.pallas_call(
        residual_kernel,
        grid=(ring,),
        in_specs=[
            SMEM,
            pl.BlockSpec((1, layers, depth, columns), lambda i: (i, 0, 0, 0)),
            pl.BlockSpec((layers, depth, columns), lambda i: (0, i, 0)),
            block,
        ],
        out_specs=[block, pl.BlockSpec((TILE, LANES), lambda i: (0, 0))],
        out_shape=[
            jax.ShapeDtypeStruct(measured.shape, jnp.float32),
            jax.ShapeDtypeStruct((TILE, LANES), jnp.float32),
        ],
        compiler_params=pltpu.CompilerParams(vmem_limit_bytes=8 * 2**20),
        name="residual",
    )(coefs, before, volume, measured)


def update_kernel(
    place_ref, mine_ref, far_ref, before_ref, piece_ref, after_ref, earlier_ref, out_ref, cross_ref
):
    layers, depth, columns = piece_ref.shape
    ytiles, xtiles = depth // TILE, columns // LANES
    body = layers * ytiles * xtiles * TILE
    sums = mine_ref[body : body + TILE, :] + far_ref[body : body + TILE, :]
    share = 1.0 / sums[:, 3 * layers : 3 * layers + 1]
    sums = sums * share
    odd = place_ref[1] == 1

    def splat(value):
        return jnp.broadcast_to(value, (TILE, LANES))

    shares = [splat(share[z : z + 1, :]) for z in range(layers)]
    coefs = [
        [splat(sums[z : z + 1, k : k + 1]) for k in range(3 * layers)] for z in range(layers)
    ]
    for t in range(xtiles):
        lanes = pl.ds(t * LANES, LANES)
        for j in range(ytiles):
            rows = pl.ds(j * TILE, TILE)
            planes = [
                ref[z, rows, lanes]
                for ref in (before_ref, piece_ref, after_ref)
                for z in range(layers)
            ]
            values = []
            for z in range(layers):
                row = ((z * ytiles + j) * xtiles + t) * TILE
                total = (mine_ref[row : row + TILE, :] + far_ref[row : row + TILE, :]) * shares[z]
                for k in range(3 * layers):
                    total = total - planes[k] * coefs[z][k]
                values.append(planes[layers + z] + total)
                for copy in range(out_ref.shape[0]):
                    out_ref[copy, z, rows, lanes] = values[z]
            for z in range(HALO):
                cross_ref[z, rows, lanes] = jnp.where(odd, values[layers - HALO + z], values[z])


def update(place, mine, far, before, piece, after, earlier, ring):
    layers, depth, columns = piece.shape
    shape = lambda *sizes: jax.ShapeDtypeStruct(sizes + (depth, columns), jnp.float32)
    return pl.pallas_call(
        update_kernel,
        in_specs=[SMEM] + [VMEM] * 5 + [ANY],
        out_specs=[VMEM, VMEM],
        out_shape=[shape(ring, layers), shape(HALO)],
        compiler_params=pltpu.CompilerParams(vmem_limit_bytes=8 * 2**20),
        name="update",
    )(place, mine, far, before, piece, after, earlier)


def sweep(source, target, edge, lowest, highest):
    tall, columns = source.shape[1:]
    height = tall - TILE
    xtiles = columns // LANES
    lane = lax.broadcasted_iota(jnp.int32, (TILE, LANES), 1)
    level = lax.broadcasted_iota(jnp.int32, (TILE, LANES), 0)
    last_lane, first_lane = lane == LANES - 1, lane == 0
    last_row, first_row = level == TILE - 1, level == 0
    spans = [pl.ds(t * LANES, LANES) for t in range(xtiles)]
    for z in range(lowest, highest + 1):
        edge[z, :, :] = jnp.zeros((TILE, columns), jnp.float32)

    def band(i, carry):
        top = pl.multiple_of(i * TILE, TILE)
        rows = pl.ds(top, TILE)
        below = pl.ds(top + TILE, 1)
        upper = [source[lowest - 1, rows, span] for span in spans]
        flow_z = None
        for z in range(lowest - 1, highest + 1):
            base, upper = upper, [source[z + 1, rows, span] for span in spans]
            turned = [pltpu.roll(b, LANES - 1, 1) for b in base]
            grad_z, along, scaled = [], [], []
            for t in range(xtiles):
                rise = upper[t] - base[t]
                nearby = jnp.where(
                    last_row,
                    jnp.broadcast_to(source[z, below, spans[t]], (TILE, LANES)),
                    pltpu.roll(base[t], TILE - 1, 0),
                )
                down = nearby - base[t]
                right = jnp.where(
                    last_lane, turned[t + 1] if t + 1 < xtiles else base[t], turned[t]
                )
                across = right - base[t]
                scale = lax.rsqrt(rise * rise + down * down + across * across + 0.01)
                grad_z.append(rise * scale)
                along.append(down * scale)
                scaled.append(across * scale)
            if z >= lowest:
                moved = [pltpu.roll(p, 1, 1) for p in scaled]
                for t in range(xtiles):
                    left = jnp.where(first_lane, moved[t - 1] if t else 0.0, moved[t])
                    above = jnp.where(
                        first_row,
                        jnp.broadcast_to(edge[z, TILE - 1 : TILE, spans[t]], (TILE, LANES)),
                        pltpu.roll(along[t], 1, 0),
                    )
                    edge[z, :, spans[t]] = along[t]
                    div = (grad_z[t] - flow_z[t]) + (along[t] - above) + (scaled[t] - left)
                    target(z, rows, spans[t], base[t] + 0.05 * div)
            flow_z = grad_z
        return carry

    lax.fori_loop(0, height // TILE, band, 0)


def smooth_kernel(place_ref, own_ref, cross_ref, inner_ref, out_ref, field, middle, edge):
    ring, layers, depth, columns = own_ref.shape
    height = ring * depth
    odd = place_ref[1] == 1
    keep_low = place_ref[2].astype(jnp.float32)
    keep_high = place_ref[3].astype(jnp.float32)

    def fill(i, carry):
        rows = pl.ds(pl.multiple_of(i * depth, depth), depth)
        for z in range(HALO):
            cross, inner = cross_ref[i, z], inner_ref[i, z]
            field[z, rows, :] = jnp.where(odd, inner, cross)
            field[HALO + layers + z, rows, :] = jnp.where(odd, cross, inner)
        for z in range(layers):
            field[HALO + z, rows, :] = own_ref[i, z]
        return carry

    lax.fori_loop(0, ring, fill, 0)
    for z in range(layers + 2 * HALO):
        field[z, height : height + 1, :] = field[z, height - 1 : height, :]

    def keep(z, rows, span, value):
        if z == HALO - 1:
            value = value * keep_low
        if z == HALO + layers:
            value = value * keep_high
        middle[z, rows, span] = value

    def finish(z, rows, span, value):
        out_ref[z - HALO, rows, span] = value

    sweep(field, keep, edge, HALO - 1, HALO + layers)
    for z in range(HALO - 1, HALO + layers + 1):
        middle[z, height : height + 1, :] = middle[z, height - 1 : height, :]
    sweep(middle, finish, edge, HALO, HALO + layers - 1)


def smooth(place, own, cross, inner):
    ring, layers, depth, columns = own.shape
    deep, height = layers + 2 * HALO, ring * depth
    return pl.pallas_call(
        smooth_kernel,
        in_specs=[SMEM, VMEM, VMEM, VMEM],
        out_specs=VMEM,
        out_shape=jax.ShapeDtypeStruct((layers, height, columns), jnp.float32),
        scratch_shapes=[
            pltpu.VMEM((deep, height + TILE, columns), jnp.float32),
            pltpu.VMEM((deep, height + TILE, columns), jnp.float32),
            pltpu.VMEM((deep, TILE, columns), jnp.float32),
        ],
        compiler_params=pltpu.CompilerParams(vmem_limit_bytes=16 * 2**20),
        name="smooth",
    )(place, own, cross, inner)


def windows(weights, shifts, bands):
    band_rows = weights.shape[1]
    rows_i = jnp.arange(band_rows, dtype=jnp.int32)[:, None]
    rows_j = jnp.arange(band_rows, dtype=jnp.int32)[None, :]
    placer = ((rows_i == rows_j + shifts[0, 0]) & (rows_j < bands[0, 0])).astype(jnp.float32)
    return jnp.sum(placer[None, :, :, None] * weights[:, None, :, :], axis=2)


def per_device(weights, shifts, bands, volume, measured):
    layers, height, columns = volume.shape
    own_rows = measured.shape[1]
    ring = lax.axis_size("ang") // 2
    depth = height // ring
    slab = lax.axis_index("slab")
    last_slab = lax.axis_size("slab") - 1
    place = jnp.stack(
        [lax.axis_index("ang") // 2, slab % 2, slab > 0, slab < last_slab]
    ).astype(jnp.int32)

    window = windows(weights, shifts, bands)
    line = jnp.pad(window.reshape(1, -1), ((0, TILE - 1), (0, columns - window.size)))
    back = pack(line, measured)
    following = from_behind(back, "slab", -1)
    window_before = from_behind(window, "slab", 1)
    window_after = following[-TILE, : window.size].reshape(window.shape)

    low, high = window[:, :own_rows], window[:, own_rows:]
    low_after, high_before = window_after[:, :own_rows], window_before[:, own_rows:]
    total_own = jnp.sum(low, axis=2) + jnp.sum(high_before, axis=2)
    total_next = jnp.sum(low_after, axis=2) + jnp.sum(high, axis=2)
    share_own = 1.0 / jnp.maximum(total_own, 1.0)
    share_next = jnp.where(slab < last_slab, 1.0 / jnp.maximum(total_next, 1.0), 0.0)
    count = low.shape[0] * own_rows
    back_coefs = jnp.concatenate(
        [
            (low * share_own[:, :, None]).reshape(count, layers),
            (high * share_next[:, :, None]).reshape(count, layers),
        ]
    )
    nothing = jnp.zeros((count, layers), jnp.float32)
    flat = lambda block: block.reshape(count, layers)
    own_coefs = jnp.concatenate([flat(high_before), flat(low)], axis=1)
    forward_coefs = jnp.concatenate(
        [
            jnp.concatenate([own_coefs, nothing], axis=1),
            jnp.concatenate([nothing, flat(high), flat(low_after)], axis=1),
        ]
    )
    normal = jnp.sum(back_coefs[:, :, None] * forward_coefs[:, None, :], axis=0)
    column_part = jnp.sum(window, axis=(0, 1))
    sums = jnp.concatenate([normal, column_part[:, None]], axis=1)
    sums = jnp.pad(sums, ((0, TILE - layers), (0, LANES - 3 * layers - 1)))

    sent = spread(back_coefs, sums, back, following, height, ring)
    piece = piece_of(place, volume, sent, depth)
    before = from_behind(piece, "slab", 1)
    after = from_behind(piece, "slab", -1)
    mine = gather(over_ring(sent), before, after)
    far = from_far(mine)
    volume_before = over_ring(copies_of(before, mine, ring))
    residual, done = residual_of(own_coefs, volume_before, volume, measured)
    pieces, cross = update(place, mine, far, before, piece, after, done, ring)
    field = over_ring(pieces)
    cross = across_chips(cross)
    cross = over_ring(jnp.broadcast_to(cross[None], (ring,) + cross.shape))
    facing = lax.dynamic_slice_in_dim(field, (1 - slab % 2) * (layers - HALO), HALO, 1)
    updated = smooth(place, field, cross, within_chip(facing))
    return (updated, residual)


def solution(mesh):
    return jax.shard_map(
        per_device,
        mesh=mesh,
        in_specs=(
            P("ang", None, "slab"),
            P("ang", "slab"),
            P("ang", "slab"),
            P("slab", None, None),
            P("ang", "slab", None, None),
        ),
        out_specs=(P("slab", None, None), P("ang", "slab", None, None)),
        check_vma=False,
    )
```

```python
import functools

import jax
import jax.numpy as jnp
from jax import lax
from jax.experimental import pallas as pl
from jax.experimental.pallas import tpu as pltpu
from jax.sharding import PartitionSpec as P

TILE = 8
LANES = 128
HALO = 2


def from_behind(block, axis, distance):
    devices = range(lax.axis_size(axis))
    route = [(i - distance, i) for i in devices if i - distance in devices]
    return lax.ppermute(block, axis, route)


def ring_groups():
    count = lax.axis_size("ang")
    return [list(range(0, count, 2)), list(range(1, count, 2))]


def from_far(block):
    return lax.ppermute(block, "ang", [(a, a ^ 1) for a in range(lax.axis_size("ang"))])


def along_ring(block, distance):
    count = lax.axis_size("ang")
    return lax.ppermute(block, "ang", [(a, (a + 2 * distance) % count) for a in range(count)])


def over_ring(pieces):
    return lax.all_to_all(
        pieces, "ang", split_axis=0, concat_axis=0, axis_index_groups=ring_groups()
    )


ROW = 16


def route(pairs):
    count, slabs = lax.axis_size("ang"), lax.axis_size("slab")
    return [
        (a * slabs + s, (a if s // ROW == t // ROW else a ^ 1) * slabs + t)
        for a in range(count)
        for s, t in pairs
        if 0 <= t < slabs
    ]


def within_chip(block):
    return lax.ppermute(block, "slab", [(s, s ^ 1) for s in range(lax.axis_size("slab"))])


def across_chips(block):
    pairs = [(s, s + 1 if s % 2 else s - 1) for s in range(lax.axis_size("slab"))]
    return lax.ppermute(block, ("ang", "slab"), route(pairs))


def to_previous(block):
    pairs = [(s, s - 1) for s in range(lax.axis_size("slab"))]
    return lax.ppermute(block, ("ang", "slab"), route(pairs))


VMEM = pl.BlockSpec(memory_space=pltpu.VMEM)
SMEM = pl.BlockSpec(memory_space=pltpu.SMEM)
ANY = pl.BlockSpec(memory_space=pl.ANY)


def wide_kernel(measured_ref, out_ref):
    angles, rows, height, columns = measured_ref.shape
    for a in range(angles):
        for r in range(rows):
            row = (a * rows + r) * height
            out_ref[row : row + height, :] = measured_ref[a, r].astype(jnp.float32)


def wide(measured):
    angles, rows, height, columns = measured.shape
    return pl.pallas_call(
        wide_kernel,
        in_specs=[VMEM],
        out_specs=VMEM,
        out_shape=jax.ShapeDtypeStruct((angles * rows * height, columns), jnp.float32),
        compiler_params=pltpu.CompilerParams(vmem_limit_bytes=8 * 2**20),
        name="wide",
    )(measured)


def spread_piece(place_ref, coef_ref, own_ref, next_ref, distance, ring, store):
    count, layers = coef_ref.shape
    columns = own_ref.shape[1]
    height = own_ref.shape[0] // (count // 2)
    depth = height // ring
    top = pl.multiple_of(lax.rem(place_ref[0] + distance, ring) * depth, depth)
    coefs = [[coef_ref[k, z] for z in range(layers)] for k in range(count)]

    def column(t, carry):
        lanes = pl.ds(pl.multiple_of(t * LANES, LANES), LANES)
        planes = [
            ref[pl.ds(k * height + top, depth), lanes]
            for ref in (own_ref, next_ref)
            for k in range(count // 2)
        ]
        for z in range(layers):
            total = planes[0] * coefs[0][z]
            for k in range(1, count):
                total = total + planes[k] * coefs[k][z]
            for j in range(depth // TILE):
                store(z, j, t, total[j * TILE : (j + 1) * TILE])
        return carry

    lax.fori_loop(0, columns // LANES, column, 0)


def spread_far_kernel(ring, place_ref, coef_ref, sums_ref, own_ref, next_ref, low_ref, high_ref):
    layers = coef_ref.shape[1]
    xtiles = own_ref.shape[1] // LANES
    tiles = high_ref.shape[0] // TILE // xtiles // (layers // 2)

    def store(z, j, t, value):
        ref = low_ref if z < layers // 2 else high_ref
        row = ((z % (layers // 2) * tiles + j) * xtiles + t) * TILE
        ref[pl.ds(pl.multiple_of(row, TILE), TILE), :] = value

    spread_piece(place_ref, coef_ref, own_ref, next_ref, 2, ring, store)
    low_ref[high_ref.shape[0] :, :] = sums_ref[...]


def spread_near_kernel(
    ring, place_ref, coef_ref, sums_ref, own_ref, next_ref, earlier_ref, mine_ref, plus_ref, minus_ref
):
    layers = coef_ref.shape[1]
    xtiles = own_ref.shape[1] // LANES
    body = mine_ref.shape[0] - TILE
    tiles = body // TILE // xtiles // layers
    for distance, ref in ((1, plus_ref), (3, minus_ref), (0, mine_ref)):

        def store(z, j, t, value, ref=ref):
            row = ((z * tiles + j) * xtiles + t) * TILE
            ref[pl.ds(pl.multiple_of(row, TILE), TILE), :] = value

        spread_piece(place_ref, coef_ref, own_ref, next_ref, distance, ring, store)
        ref[body:, :] = sums_ref[...]


def spread(place, coefs, sums, own, following, ring):
    layers = coefs.shape[1]
    body = layers * own.size // (coefs.shape[0] // 2) // ring // LANES
    shape = lambda rows: jax.ShapeDtypeStruct((rows, LANES), jnp.float32)
    params = pltpu.CompilerParams(vmem_limit_bytes=8 * 2**20)
    low, high = pl.pallas_call(
        functools.partial(spread_far_kernel, ring),
        in_specs=[SMEM, SMEM, VMEM, VMEM, VMEM],
        out_specs=[VMEM, VMEM],
        out_shape=[shape(body // 2 + TILE), shape(body // 2)],
        compiler_params=params,
        name="spread_far",
    )(place, coefs, sums, own, following)
    near = pl.pallas_call(
        functools.partial(spread_near_kernel, ring),
        in_specs=[SMEM, SMEM, VMEM, VMEM, VMEM, ANY],
        out_specs=[VMEM] * 3,
        out_shape=[shape(body + TILE)] * 3,
        compiler_params=params,
        cost_estimate=pl.CostEstimate(flops=0, bytes_accessed=16 * 2**20, transcendentals=0),
        name="spread_near",
    )(place, coefs, sums, own, following, low)
    return low, high, *near


def join_kernel(at, whole_ref, part_ref, out_ref):
    out_ref[...] = whole_ref[...]
    rows = part_ref.shape[0] if at else part_ref.shape[0] - TILE
    out_ref[at : at + rows, :] = whole_ref[at : at + rows, :] + part_ref[:rows, :]
    if not at:
        end = whole_ref.shape[0] - TILE
        out_ref[end:, :] = whole_ref[end:, :] + part_ref[rows:, :]


def join(whole, part, at):
    return pl.pallas_call(
        functools.partial(join_kernel, at),
        in_specs=[VMEM, VMEM],
        out_specs=VMEM,
        out_shape=jax.ShapeDtypeStruct(whole.shape, jnp.float32),
        compiler_params=pltpu.CompilerParams(vmem_limit_bytes=8 * 2**20),
        name="join",
    )(whole, part)


def gather_kernel(mine_ref, left_ref, right_ref, cross_ref, inner_ref, out_ref):
    out_ref[...] = mine_ref[...] + left_ref[...] + right_ref[...]


def gather(mine, left, right, cross, inner):
    return pl.pallas_call(
        gather_kernel,
        in_specs=[VMEM, VMEM, VMEM, ANY, ANY],
        out_specs=VMEM,
        out_shape=jax.ShapeDtypeStruct(mine.shape, jnp.float32),
        compiler_params=pltpu.CompilerParams(vmem_limit_bytes=8 * 2**20),
        name="gather",
    )(mine, left, right, cross, inner)


def copies_kernel(place_ref, cross_ref, inner_ref, earlier_ref, out_ref):
    odd = place_ref[1] == 1
    for z in range(cross_ref.shape[0]):
        block = jnp.where(odd, inner_ref[z], cross_ref[z])
        for copy in range(out_ref.shape[0]):
            out_ref[copy, z] = block


def copies_of(place, cross, inner, earlier, count):
    shape = (count,) + cross.shape
    return pl.pallas_call(
        copies_kernel,
        in_specs=[SMEM, VMEM, VMEM, ANY],
        out_specs=VMEM,
        out_shape=jax.ShapeDtypeStruct(shape, jnp.float32),
        compiler_params=pltpu.CompilerParams(vmem_limit_bytes=8 * 2**20),
        cost_estimate=pl.CostEstimate(flops=0, bytes_accessed=32 * 2**20, transcendentals=0),
        name="copies",
    )(place, cross, inner, earlier)


def piece_kernel(place_ref, volume_ref, earlier_ref, out_ref):
    out_ref[...] = volume_ref[...]


def piece_of(place, volume, earlier, depth):
    layers, _, columns = volume.shape
    return pl.pallas_call(
        piece_kernel,
        grid_spec=pltpu.PrefetchScalarGridSpec(
            num_scalar_prefetch=1,
            grid=(1,),
            in_specs=[pl.BlockSpec((layers, depth, columns), lambda i, p: (0, p[0], 0)), ANY],
            out_specs=pl.BlockSpec((layers, depth, columns), lambda i, p: (0, 0, 0)),
        ),
        out_shape=jax.ShapeDtypeStruct((layers, depth, columns), jnp.float32),
        compiler_params=pltpu.CompilerParams(vmem_limit_bytes=8 * 2**20),
        cost_estimate=pl.CostEstimate(
            flops=0, bytes_accessed=32 * 2**20, transcendentals=0
        ),
        name="piece",
    )(place, volume, earlier)


def residual_kernel(coef_ref, before_ref, volume_ref, measured_ref, out_ref, done_ref):
    done_ref[...] = jnp.zeros_like(done_ref)
    angles, rows, depth, columns = measured_ref.shape
    layers = volume_ref.shape[0]
    coefs = [[coef_ref[k, z] for z in range(2 * layers)] for k in range(angles * rows)]
    for t in range(columns // LANES):
        lanes = pl.ds(t * LANES, LANES)
        planes = [before_ref[0, z, :, lanes] for z in range(layers)]
        planes += [volume_ref[z, :, lanes] for z in range(layers)]
        for a in range(angles):
            for r in range(rows):
                total = planes[0] * coefs[a * rows + r][0]
                for k in range(1, len(planes)):
                    total = total + planes[k] * coefs[a * rows + r][k]
                out_ref[a, r, :, lanes] = (
                    measured_ref[a, r, :, lanes].astype(jnp.float32) - total
                )


def residual_of(coefs, before, volume, measured):
    angles, rows, height, columns = measured.shape
    ring, layers, depth, _ = before.shape
    block = pl.BlockSpec((angles, rows, depth, columns), lambda i: (0, 0, i, 0))
    return pl.pallas_call(
        residual_kernel,
        grid=(ring,),
        in_specs=[
            SMEM,
            pl.BlockSpec((1, layers, depth, columns), lambda i: (i, 0, 0, 0)),
            pl.BlockSpec((layers, depth, columns), lambda i: (0, i, 0)),
            block,
        ],
        out_specs=[block, pl.BlockSpec((TILE, LANES), lambda i: (0, 0))],
        out_shape=[
            jax.ShapeDtypeStruct(measured.shape, jnp.float32),
            jax.ShapeDtypeStruct((TILE, LANES), jnp.float32),
        ],
        compiler_params=pltpu.CompilerParams(vmem_limit_bytes=8 * 2**20),
        name="residual",
    )(coefs, before, volume, measured)


def update_kernel(
    place_ref, mine_ref, far_ref, cross_ref, piece_ref, inner_ref, earlier_ref,
    out_ref, to_cross_ref, to_inner_ref,
):
    layers, depth, columns = piece_ref.shape
    ytiles, xtiles = depth // TILE, columns // LANES
    body = layers * ytiles * xtiles * TILE
    sums = mine_ref[body : body + TILE, :] + far_ref[body : body + TILE, :]
    share = 1.0 / sums[:, 3 * layers : 3 * layers + 1]
    sums = sums * share
    odd = place_ref[1] == 1

    def splat(value):
        return jnp.broadcast_to(value, (TILE, LANES))

    shares = [splat(share[z : z + 1, :]) for z in range(layers)]
    before, here, after = (
        [
            [splat(sums[z : z + 1, k : k + 1]) for k in range(side * layers, (side + 1) * layers)]
            for z in range(layers)
        ]
        for side in range(3)
    )
    coefs = [
        [jnp.where(odd, a, b) for a, b in zip(after[z], before[z])]
        + here[z]
        + [jnp.where(odd, b, a) for a, b in zip(after[z], before[z])]
        for z in range(layers)
    ]
    for t in range(xtiles):
        lanes = pl.ds(t * LANES, LANES)
        for j in range(ytiles):
            rows = pl.ds(j * TILE, TILE)
            planes = [
                ref[z, rows, lanes]
                for ref in (cross_ref, piece_ref, inner_ref)
                for z in range(layers)
            ]
            values = []
            for z in range(layers):
                row = ((z * ytiles + j) * xtiles + t) * TILE
                total = (mine_ref[row : row + TILE, :] + far_ref[row : row + TILE, :]) * shares[z]
                for k in range(3 * layers):
                    total = total - planes[k] * coefs[z][k]
                values.append(planes[layers + z] + total)
                out_ref[z, rows, lanes] = values[z]
            for z in range(HALO):
                top, bottom = values[layers - HALO + z], values[z]
                to_cross_ref[z, rows, lanes] = jnp.where(odd, top, bottom)
                to_inner_ref[z, rows, lanes] = jnp.where(odd, bottom, top)


def update(place, mine, far, cross, piece, inner, earlier):
    layers, depth, columns = piece.shape
    shape = lambda *sizes: jax.ShapeDtypeStruct(sizes + (depth, columns), jnp.float32)
    return pl.pallas_call(
        update_kernel,
        in_specs=[SMEM] + [VMEM] * 5 + [ANY],
        out_specs=[VMEM] * 3,
        out_shape=[shape(layers), shape(HALO), shape(HALO)],
        compiler_params=pltpu.CompilerParams(vmem_limit_bytes=8 * 2**20),
        name="update",
    )(place, mine, far, cross, piece, inner, earlier)


def stack_kernel(place_ref, own_ref, cross_ref, inner_ref, out_ref):
    odd = place_ref[1] == 1
    layers = own_ref.shape[0]
    for z in range(HALO):
        cross, inner = cross_ref[z], inner_ref[z]
        out_ref[z] = jnp.where(odd, inner, cross)
        out_ref[HALO + layers + z] = jnp.where(odd, cross, inner)
    for z in range(layers):
        out_ref[HALO + z] = own_ref[z]


def stack(place, own, cross, inner):
    layers, depth, columns = own.shape
    return pl.pallas_call(
        stack_kernel,
        in_specs=[SMEM, VMEM, VMEM, VMEM],
        out_specs=VMEM,
        out_shape=jax.ShapeDtypeStruct((layers + 2 * HALO, depth, columns), jnp.float32),
        compiler_params=pltpu.CompilerParams(vmem_limit_bytes=8 * 2**20),
        name="stack",
    )(place, own, cross, inner)


def sweep(source, target, edge, lowest, highest):
    tall, columns = source.shape[1:]
    height = tall - TILE
    xtiles = columns // LANES
    lane = lax.broadcasted_iota(jnp.int32, (TILE, LANES), 1)
    level = lax.broadcasted_iota(jnp.int32, (TILE, LANES), 0)
    last_lane, first_lane = lane == LANES - 1, lane == 0
    last_row, first_row = level == TILE - 1, level == 0
    spans = [pl.ds(t * LANES, LANES) for t in range(xtiles)]
    for z in range(lowest, highest + 1):
        edge[z, :, :] = jnp.zeros((TILE, columns), jnp.float32)

    def band(i, carry):
        top = pl.multiple_of(i * TILE, TILE)
        rows = pl.ds(top, TILE)
        below = pl.ds(top + TILE, 1)
        upper = [source[lowest - 1, rows, span] for span in spans]
        flow_z = None
        for z in range(lowest - 1, highest + 1):
            base, upper = upper, [source[z + 1, rows, span] for span in spans]
            turned = [pltpu.roll(b, LANES - 1, 1) for b in base]
            grad_z, along, scaled = [], [], []
            for t in range(xtiles):
                rise = upper[t] - base[t]
                nearby = jnp.where(
                    last_row,
                    jnp.broadcast_to(source[z, below, spans[t]], (TILE, LANES)),
                    pltpu.roll(base[t], TILE - 1, 0),
                )
                down = nearby - base[t]
                right = jnp.where(
                    last_lane, turned[t + 1] if t + 1 < xtiles else base[t], turned[t]
                )
                across = right - base[t]
                scale = lax.rsqrt(rise * rise + down * down + across * across + 0.01)
                grad_z.append(rise * scale)
                along.append(down * scale)
                scaled.append(across * scale)
            if z >= lowest:
                moved = [pltpu.roll(p, 1, 1) for p in scaled]
                for t in range(xtiles):
                    left = jnp.where(first_lane, moved[t - 1] if t else 0.0, moved[t])
                    above = jnp.where(
                        first_row,
                        jnp.broadcast_to(edge[z, TILE - 1 : TILE, spans[t]], (TILE, LANES)),
                        pltpu.roll(along[t], 1, 0),
                    )
                    edge[z, :, spans[t]] = along[t]
                    div = (grad_z[t] - flow_z[t]) + (along[t] - above) + (scaled[t] - left)
                    target(z, rows, spans[t], base[t] + 0.05 * div)
            flow_z = grad_z
        return carry

    lax.fori_loop(0, height // TILE, band, 0)


def smooth_kernel(
    place_ref, mine_ref, left_ref, right_ref, far_low_ref, far_high_ref, out_ref, field, middle, edge
):
    deep, depth, columns = mine_ref.shape
    layers, height = out_ref.shape[:2]
    ring = height // depth
    keep_low = place_ref[2].astype(jnp.float32)
    keep_high = place_ref[3].astype(jnp.float32)
    rows = [
        pl.ds(pl.multiple_of(lax.rem(place_ref[0] + k, ring) * depth, depth), depth)
        for k in range(ring)
    ]
    for z in range(deep):
        far_ref = far_low_ref if z < deep // 2 else far_high_ref
        field[z, rows[0], :] = mine_ref[z]
        field[z, rows[1], :] = right_ref[z]
        field[z, rows[2], :] = far_ref[z % (deep // 2)]
        field[z, rows[3], :] = left_ref[z]
    for z in range(deep):
        field[z, height : height + 1, :] = field[z, height - 1 : height, :]

    def keep(z, rows, span, value):
        if z == HALO - 1:
            value = value * keep_low
        if z == HALO + layers:
            value = value * keep_high
        middle[z, rows, span] = value

    def finish(z, rows, span, value):
        out_ref[z - HALO, rows, span] = value

    sweep(field, keep, edge, HALO - 1, HALO + layers)
    for z in range(HALO - 1, HALO + layers + 1):
        middle[z, height : height + 1, :] = middle[z, height - 1 : height, :]
    sweep(middle, finish, edge, HALO, HALO + layers - 1)


def smooth(place, mine, left, right, far_low, far_high, ring):
    deep, depth, columns = mine.shape
    layers, height = deep - 2 * HALO, ring * depth
    return pl.pallas_call(
        smooth_kernel,
        in_specs=[SMEM] + [VMEM] * 5,
        out_specs=VMEM,
        out_shape=jax.ShapeDtypeStruct((layers, height, columns), jnp.float32),
        scratch_shapes=[
            pltpu.VMEM((deep, height + TILE, columns), jnp.float32),
            pltpu.VMEM((deep, height + TILE, columns), jnp.float32),
            pltpu.VMEM((deep, TILE, columns), jnp.float32),
        ],
        compiler_params=pltpu.CompilerParams(vmem_limit_bytes=16 * 2**20),
        name="smooth",
    )(place, mine, left, right, far_low, far_high)


def windows(weights, shifts, bands):
    band_rows = weights.shape[1]
    rows_i = jnp.arange(band_rows, dtype=jnp.int32)[:, None]
    rows_j = jnp.arange(band_rows, dtype=jnp.int32)[None, :]
    placer = ((rows_i == rows_j + shifts[0, 0]) & (rows_j < bands[0, 0])).astype(jnp.float32)
    return jnp.sum(placer[None, :, :, None] * weights[:, None, :, :], axis=2)


def per_device(weights, shifts, bands, volume, measured):
    layers, height, columns = volume.shape
    own_rows = measured.shape[1]
    ring = lax.axis_size("ang") // 2
    depth = height // ring
    slab = lax.axis_index("slab")
    last_slab = lax.axis_size("slab") - 1
    place = jnp.stack(
        [lax.axis_index("ang") // 2, slab % 2, slab > 0, slab < last_slab]
    ).astype(jnp.int32)

    window = windows(weights, shifts, bands)
    window_before = from_behind(window, "slab", 1)
    own = wide(measured)
    following = to_previous(own)

    count = window.shape[0] * own_rows
    flat = lambda block: block.reshape(count, layers)
    low, high_before = window[:, :own_rows], window_before[:, own_rows:]
    share = 1.0 / jnp.maximum(jnp.sum(low, axis=2) + jnp.sum(high_before, axis=2), 1.0)
    forward = jnp.concatenate([flat(high_before), flat(low)], axis=1)
    back_coefs = forward * share.reshape(count, 1)
    arrived = to_previous(jnp.concatenate([back_coefs[:, :layers], forward], axis=1))
    back_coefs = jnp.concatenate([back_coefs[:, layers:], arrived[:, :layers]])
    nothing = jnp.zeros((count, layers), jnp.float32)
    forward_coefs = jnp.concatenate(
        [
            jnp.concatenate([forward, nothing], axis=1),
            jnp.concatenate([nothing, arrived[:, layers:]], axis=1),
        ]
    )
    normal = jnp.sum(back_coefs[:, :, None] * forward_coefs[:, None, :], axis=0)
    column_part = jnp.sum(window, axis=(0, 1))
    sums = jnp.concatenate([normal, column_part[:, None]], axis=1)
    sums = jnp.pad(sums, ((0, TILE - layers), (0, LANES - 3 * layers - 1)))

    far_low, far_high, mine, plus, minus = spread(place, back_coefs, sums, own, following, ring)
    piece = piece_of(place, volume, plus, depth)
    plus = along_ring(join(plus, along_ring(far_low, 1), 0), 1)
    minus = along_ring(join(minus, along_ring(far_high, -1), far_high.shape[0]), -1)
    cross, inner = across_chips(piece), within_chip(piece)
    mine = gather(mine, plus, minus, cross, inner)
    far = from_far(mine)
    volume_before = over_ring(copies_of(place, cross, inner, mine, ring))
    residual, done = residual_of(forward, volume_before, volume, measured)
    field, cross, inner = update(place, mine, far, cross, piece, inner, done)
    field = stack(place, field, across_chips(cross), within_chip(inner))
    left, right = along_ring(field, 1), along_ring(field, -1)
    half = field.shape[0] // 2
    far_low, far_high = along_ring(left[:half], 1), along_ring(right[half:], -1)
    updated = smooth(place, field, left, right, far_low, far_high, ring)
    return (updated, residual)


def solution(mesh):
    return jax.shard_map(
        per_device,
        mesh=mesh,
        in_specs=(
            P("ang", None, "slab"),
            P("ang", "slab"),
            P("ang", "slab"),
            P("slab", None, None),
            P("ang", "slab", None, None),
        ),
        out_specs=(P("slab", None, None), P("ang", "slab", None, None)),
        check_vma=False,
    )
```

```python
import jax
import jax.numpy as jnp
from jax import lax
from jax.experimental import pallas as pl
from jax.experimental.pallas import tpu as pltpu
from jax.sharding import PartitionSpec as P

TILE = 8
LANES = 128
HALO = 2


def from_behind(block, axis, distance):
    devices = range(lax.axis_size(axis))
    route = [(i - distance, i) for i in devices if i - distance in devices]
    return lax.ppermute(block, axis, route)


def ring_groups():
    count = lax.axis_size("ang")
    return [list(range(0, count, 2)), list(range(1, count, 2))]


def from_far(block):
    return lax.ppermute(block, "ang", [(a, a ^ 1) for a in range(lax.axis_size("ang"))])


def over_ring(pieces):
    return lax.all_to_all(
        pieces, "ang", split_axis=0, concat_axis=0, axis_index_groups=ring_groups()
    )


ROW = 16


def route(pairs):
    count, slabs = lax.axis_size("ang"), lax.axis_size("slab")
    return [
        (a * slabs + s, (a if s // ROW == t // ROW else a ^ 1) * slabs + t)
        for a in range(count)
        for s, t in pairs
        if 0 <= t < slabs
    ]


def to_next(block):
    pairs = [(s, s + 1) for s in range(lax.axis_size("slab"))]
    return lax.ppermute(block, ("ang", "slab"), route(pairs))


def to_previous(block):
    pairs = [(s, s - 1) for s in range(lax.axis_size("slab"))]
    return lax.ppermute(block, ("ang", "slab"), route(pairs))


VMEM = pl.BlockSpec(memory_space=pltpu.VMEM)
SMEM = pl.BlockSpec(memory_space=pltpu.SMEM)
ANY = pl.BlockSpec(memory_space=pl.ANY)


def pack_kernel(window_ref, measured_ref, out_ref):
    angles, rows, height, columns = measured_ref.shape
    for a in range(angles):
        for r in range(rows):
            row = (a * rows + r) * height
            out_ref[row : row + height, :] = measured_ref[a, r].astype(jnp.float32)
    out_ref[angles * rows * height :, :] = window_ref[...]


def pack(window, measured):
    angles, rows, height, columns = measured.shape
    return pl.pallas_call(
        pack_kernel,
        in_specs=[VMEM, VMEM],
        out_specs=VMEM,
        out_shape=jax.ShapeDtypeStruct((angles * rows * height + TILE, columns), jnp.float32),
        compiler_params=pltpu.CompilerParams(vmem_limit_bytes=8 * 2**20),
        name="pack",
    )(window, measured)


def spread_kernel(coef_ref, sums_ref, own_ref, next_ref, out_ref):
    count, layers = coef_ref.shape
    ring = out_ref.shape[0]
    columns = own_ref.shape[1]
    height = (own_ref.shape[0] - TILE) // (count // 2)
    depth = height // ring
    ytiles, xtiles = depth // TILE, columns // LANES
    coefs = [[coef_ref[k, z] for z in range(layers)] for k in range(count)]
    body = layers * ytiles * xtiles * TILE

    def chunk(i, carry):
        top = pl.multiple_of(i * depth, depth)
        for t in range(xtiles):
            lanes = pl.ds(t * LANES, LANES)
            planes = [
                ref[pl.ds(k * height + top, depth), lanes]
                for ref in (own_ref, next_ref)
                for k in range(count // 2)
            ]
            for z in range(layers):
                total = planes[0] * coefs[0][z]
                for k in range(1, count):
                    total = total + planes[k] * coefs[k][z]
                for j in range(ytiles):
                    row = ((z * ytiles + j) * xtiles + t) * TILE
                    out_ref[i, row : row + TILE, :] = total[j * TILE : (j + 1) * TILE]
        out_ref[i, body : body + TILE, :] = sums_ref[...]
        return carry

    lax.fori_loop(0, ring, chunk, 0)


def spread(coefs, sums, own, following, height, ring):
    layers, columns = coefs.shape[1], own.shape[1]
    length = layers * (height // ring) * columns // LANES + TILE
    return pl.pallas_call(
        spread_kernel,
        in_specs=[SMEM, VMEM, VMEM, VMEM],
        out_specs=VMEM,
        out_shape=jax.ShapeDtypeStruct((ring, length, LANES), jnp.float32),
        compiler_params=pltpu.CompilerParams(vmem_limit_bytes=8 * 2**20),
        name="spread",
    )(coefs, sums, own, following)


def gather_kernel(parts_ref, after_ref, mine_ref):
    ring, length, _ = parts_ref.shape
    step = next(n for n in (5 * TILE, 3 * TILE, TILE) if length % n == 0)

    def add(i, carry):
        rows = pl.ds(pl.multiple_of(i * step, TILE), step)
        total = parts_ref[0, rows, :]
        for part in range(1, ring):
            total = total + parts_ref[part, rows, :]
        mine_ref[rows, :] = total
        return carry

    lax.fori_loop(0, length // step, add, 0)


def gather(parts, after):
    return pl.pallas_call(
        gather_kernel,
        in_specs=[VMEM, ANY],
        out_specs=VMEM,
        out_shape=jax.ShapeDtypeStruct(parts.shape[1:], jnp.float32),
        compiler_params=pltpu.CompilerParams(vmem_limit_bytes=8 * 2**20),
        name="gather",
    )(parts, after)


def late_kernel(place_ref, volume_ref, earlier_ref, whole_ref, piece_ref):
    layers, depth, _ = piece_ref.shape
    top = pl.multiple_of(place_ref[0] * depth, depth)
    for z in range(layers):
        whole_ref[z] = volume_ref[z]
        piece_ref[z] = volume_ref[z, pl.ds(top, depth), :]


def late(place, volume, earlier, depth):
    layers, _, columns = volume.shape
    return pl.pallas_call(
        late_kernel,
        in_specs=[SMEM, VMEM, ANY],
        out_specs=[VMEM, VMEM],
        out_shape=[
            jax.ShapeDtypeStruct(volume.shape, jnp.float32),
            jax.ShapeDtypeStruct((layers, depth, columns), jnp.float32),
        ],
        compiler_params=pltpu.CompilerParams(vmem_limit_bytes=8 * 2**20),
        cost_estimate=pl.CostEstimate(flops=0, bytes_accessed=32 * 2**20, transcendentals=0),
        name="late",
    )(place, volume, earlier)


def residual_kernel(coef_ref, before_ref, volume_ref, measured_ref, out_ref, done_ref):
    done_ref[...] = jnp.zeros_like(done_ref)
    angles, rows, depth, columns = measured_ref.shape
    layers = volume_ref.shape[0]
    coefs = [[coef_ref[k, z] for z in range(2 * layers)] for k in range(angles * rows)]
    for t in range(columns // LANES):
        lanes = pl.ds(t * LANES, LANES)
        planes = [ref[z, :, lanes] for ref in (before_ref, volume_ref) for z in range(layers)]
        for a in range(angles):
            for r in range(rows):
                total = planes[0] * coefs[a * rows + r][0]
                for k in range(1, len(planes)):
                    total = total + planes[k] * coefs[a * rows + r][k]
                out_ref[a, r, :, lanes] = (
                    measured_ref[a, r, :, lanes].astype(jnp.float32) - total
                )


def residual_of(coefs, before, volume, measured):
    angles, rows, height, columns = measured.shape
    layers = volume.shape[0]
    depth = 2 * TILE
    slab = pl.BlockSpec((layers, depth, columns), lambda i: (0, i, 0))
    block = pl.BlockSpec((angles, rows, depth, columns), lambda i: (0, 0, i, 0))
    return pl.pallas_call(
        residual_kernel,
        grid=(height // depth,),
        in_specs=[SMEM, slab, slab, block],
        out_specs=[block, pl.BlockSpec((TILE, LANES), lambda i: (0, 0))],
        out_shape=[
            jax.ShapeDtypeStruct(measured.shape, jnp.float32),
            jax.ShapeDtypeStruct((TILE, LANES), jnp.float32),
        ],
        compiler_params=pltpu.CompilerParams(vmem_limit_bytes=8 * 2**20),
        name="residual",
    )(coefs, before, volume, measured)


def update_kernel(
    place_ref, mine_ref, far_ref, before_ref, piece_ref, after_ref, earlier_ref, out_ref
):
    layers, depth, columns = piece_ref.shape
    ytiles, xtiles = depth // TILE, columns // LANES
    body = layers * ytiles * xtiles * TILE
    top = pl.multiple_of(place_ref[0] * depth, depth)
    sums = mine_ref[body : body + TILE, :] + far_ref[body : body + TILE, :]
    share = 1.0 / sums[:, 3 * layers : 3 * layers + 1]
    sums = sums * share

    def splat(value):
        return jnp.broadcast_to(value, (TILE, LANES))

    shares = [splat(share[z : z + 1, :]) for z in range(layers)]
    coefs = [
        [splat(sums[z : z + 1, k : k + 1]) for k in range(3 * layers)] for z in range(layers)
    ]
    for t in range(xtiles):
        lanes = pl.ds(t * LANES, LANES)
        for j in range(ytiles):
            rows = pl.ds(j * TILE, TILE)
            planes = [before_ref[z, pl.ds(top + j * TILE, TILE), lanes] for z in range(layers)]
            planes += [ref[z, rows, lanes] for ref in (piece_ref, after_ref) for z in range(layers)]
            for z in range(layers):
                row = ((z * ytiles + j) * xtiles + t) * TILE
                total = (mine_ref[row : row + TILE, :] + far_ref[row : row + TILE, :]) * shares[z]
                for k in range(3 * layers):
                    total = total - planes[k] * coefs[z][k]
                value = planes[layers + z] + total
                for copy in range(out_ref.shape[0]):
                    out_ref[copy, z, rows, lanes] = value


def update(place, mine, far, before, piece, after, earlier, ring):
    return pl.pallas_call(
        update_kernel,
        in_specs=[SMEM] + [VMEM] * 5 + [ANY],
        out_specs=VMEM,
        out_shape=jax.ShapeDtypeStruct((ring,) + piece.shape, jnp.float32),
        compiler_params=pltpu.CompilerParams(vmem_limit_bytes=8 * 2**20),
        name="update",
    )(place, mine, far, before, piece, after, earlier)


def sweep(source, target, edge, lowest, highest):
    tall, columns = source.shape[1:]
    height = tall - TILE
    xtiles = columns // LANES
    lane = lax.broadcasted_iota(jnp.int32, (TILE, LANES), 1)
    level = lax.broadcasted_iota(jnp.int32, (TILE, LANES), 0)
    last_lane, first_lane = lane == LANES - 1, lane == 0
    last_row, first_row = level == TILE - 1, level == 0
    spans = [pl.ds(t * LANES, LANES) for t in range(xtiles)]
    for z in range(lowest, highest + 1):
        edge[z, :, :] = jnp.zeros((TILE, columns), jnp.float32)

    def band(i, carry):
        top = pl.multiple_of(i * TILE, TILE)
        rows = pl.ds(top, TILE)
        below = pl.ds(top + TILE, 1)
        upper = [source[lowest - 1, rows, span] for span in spans]
        flow_z = None
        for z in range(lowest - 1, highest + 1):
            base, upper = upper, [source[z + 1, rows, span] for span in spans]
            turned = [pltpu.roll(b, LANES - 1, 1) for b in base]
            grad_z, along, scaled = [], [], []
            for t in range(xtiles):
                rise = upper[t] - base[t]
                nearby = jnp.where(
                    last_row,
                    jnp.broadcast_to(source[z, below, spans[t]], (TILE, LANES)),
                    pltpu.roll(base[t], TILE - 1, 0),
                )
                down = nearby - base[t]
                right = jnp.where(
                    last_lane, turned[t + 1] if t + 1 < xtiles else base[t], turned[t]
                )
                across = right - base[t]
                scale = lax.rsqrt(rise * rise + down * down + across * across + 0.01)
                grad_z.append(rise * scale)
                along.append(down * scale)
                scaled.append(across * scale)
            if z >= lowest:
                moved = [pltpu.roll(p, 1, 1) for p in scaled]
                for t in range(xtiles):
                    left = jnp.where(first_lane, moved[t - 1] if t else 0.0, moved[t])
                    above = jnp.where(
                        first_row,
                        jnp.broadcast_to(edge[z, TILE - 1 : TILE, spans[t]], (TILE, LANES)),
                        pltpu.roll(along[t], 1, 0),
                    )
                    edge[z, :, spans[t]] = along[t]
                    div = (grad_z[t] - flow_z[t]) + (along[t] - above) + (scaled[t] - left)
                    target(z, rows, spans[t], base[t] + 0.05 * div)
            flow_z = grad_z
        return carry

    lax.fori_loop(0, height // TILE, band, 0)


def smooth_kernel(place_ref, own_ref, low_ref, high_ref, out_ref, field, middle, edge):
    ring, layers, depth, columns = own_ref.shape
    height = ring * depth
    keep_low = place_ref[1].astype(jnp.float32)
    keep_high = place_ref[2].astype(jnp.float32)

    def fill(i, carry):
        top = pl.multiple_of(i * depth, depth)
        for z in range(HALO):
            field[z, pl.ds(top, depth), :] = low_ref[i, z]
            field[HALO + layers + z, pl.ds(top, depth), :] = high_ref[i, z]
        for z in range(layers):
            field[HALO + z, pl.ds(top, depth), :] = own_ref[i, z]
        return carry

    lax.fori_loop(0, ring, fill, 0)
    for z in range(layers + 2 * HALO):
        field[z, height : height + 1, :] = field[z, height - 1 : height, :]

    def keep(z, rows, span, value):
        if z == HALO - 1:
            value = value * keep_low
        if z == HALO + layers:
            value = value * keep_high
        middle[z, rows, span] = value

    def finish(z, rows, span, value):
        out_ref[z - HALO, rows, span] = value

    sweep(field, keep, edge, HALO - 1, HALO + layers)
    for z in range(HALO - 1, HALO + layers + 1):
        middle[z, height : height + 1, :] = middle[z, height - 1 : height, :]
    sweep(middle, finish, edge, HALO, HALO + layers - 1)


def smooth(place, own, low, high):
    ring, layers, depth, columns = own.shape
    deep, height = layers + 2 * HALO, ring * depth
    return pl.pallas_call(
        smooth_kernel,
        in_specs=[SMEM, VMEM, VMEM, VMEM],
        out_specs=VMEM,
        out_shape=jax.ShapeDtypeStruct((layers, height, columns), jnp.float32),
        scratch_shapes=[
            pltpu.VMEM((deep, height + TILE, columns), jnp.float32),
            pltpu.VMEM((deep, height + TILE, columns), jnp.float32),
            pltpu.VMEM((deep, TILE, columns), jnp.float32),
        ],
        compiler_params=pltpu.CompilerParams(vmem_limit_bytes=16 * 2**20),
        name="smooth",
    )(place, own, low, high)


def windows(weights, shifts, bands):
    band_rows = weights.shape[1]
    rows_i = jnp.arange(band_rows, dtype=jnp.int32)[:, None]
    rows_j = jnp.arange(band_rows, dtype=jnp.int32)[None, :]
    placer = ((rows_i == rows_j + shifts[0, 0]) & (rows_j < bands[0, 0])).astype(jnp.float32)
    return jnp.sum(placer[None, :, :, None] * weights[:, None, :, :], axis=2)


def per_device(weights, shifts, bands, volume, measured):
    layers, height, columns = volume.shape
    own_rows = measured.shape[1]
    ring = lax.axis_size("ang") // 2
    depth = height // ring
    slab = lax.axis_index("slab")
    last_slab = lax.axis_size("slab") - 1
    place = jnp.stack(
        [lax.axis_index("ang") // 2, slab > 0, slab < last_slab]
    ).astype(jnp.int32)

    window = windows(weights, shifts, bands)
    line = jnp.pad(window.reshape(1, -1), ((0, TILE - 1), (0, columns - window.size)))
    back = pack(line, measured)
    following = from_behind(back, "slab", -1)
    window_before = from_behind(window, "slab", 1)
    window_after = following[-TILE, : window.size].reshape(window.shape)

    low, high = window[:, :own_rows], window[:, own_rows:]
    low_after, high_before = window_after[:, :own_rows], window_before[:, own_rows:]
    total_own = jnp.sum(low, axis=2) + jnp.sum(high_before, axis=2)
    total_next = jnp.sum(low_after, axis=2) + jnp.sum(high, axis=2)
    share_own = 1.0 / jnp.maximum(total_own, 1.0)
    share_next = jnp.where(slab < last_slab, 1.0 / jnp.maximum(total_next, 1.0), 0.0)
    count = low.shape[0] * own_rows
    back_coefs = jnp.concatenate(
        [
            (low * share_own[:, :, None]).reshape(count, layers),
            (high * share_next[:, :, None]).reshape(count, layers),
        ]
    )
    nothing = jnp.zeros((count, layers), jnp.float32)
    flat = lambda block: block.reshape(count, layers)
    own_coefs = jnp.concatenate([flat(high_before), flat(low)], axis=1)
    forward_coefs = jnp.concatenate(
        [
            jnp.concatenate([own_coefs, nothing], axis=1),
            jnp.concatenate([nothing, flat(high), flat(low_after)], axis=1),
        ]
    )
    normal = jnp.sum(back_coefs[:, :, None] * forward_coefs[:, None, :], axis=0)
    column_part = jnp.sum(window, axis=(0, 1))
    sums = jnp.concatenate([normal, column_part[:, None]], axis=1)
    sums = jnp.pad(sums, ((0, TILE - layers), (0, LANES - 3 * layers - 1)))

    sent = spread(back_coefs, sums, back, following, height, ring)
    whole, piece = late(place, volume, sent, depth)
    before, after = to_next(whole), to_previous(piece)
    mine = gather(over_ring(sent), after)
    far = from_far(mine)
    residual, done = residual_of(own_coefs, before, volume, measured)
    field = over_ring(update(place, mine, far, before, piece, after, done, ring))
    halo_low = to_next(field[:, layers - HALO :])
    halo_high = to_previous(field[:, :HALO])
    updated = smooth(place, field, halo_low, halo_high)
    return (updated, residual)


def solution(mesh):
    return jax.shard_map(
        per_device,
        mesh=mesh,
        in_specs=(
            P("ang", None, "slab"),
            P("ang", "slab"),
            P("ang", "slab"),
            P("slab", None, None),
            P("ang", "slab", None, None),
        ),
        out_specs=(P("slab", None, None), P("ang", "slab", None, None)),
        check_vma=False,
    )
```

```python
import jax
import jax.numpy as jnp
from jax import lax
from jax.experimental import pallas as pl
from jax.experimental.pallas import tpu as pltpu
from jax.sharding import PartitionSpec as P

TILE = 8
LANES = 128
HALO = 2


def from_behind(block, axis, distance):
    devices = range(lax.axis_size(axis))
    route = [(i - distance, i) for i in devices if i - distance in devices]
    return lax.ppermute(block, axis, route)


def ring_groups():
    count = lax.axis_size("ang")
    return [list(range(0, count, 2)), list(range(1, count, 2))]


def over_ring(pieces):
    return lax.all_to_all(
        pieces, "ang", split_axis=0, concat_axis=0, axis_index_groups=ring_groups()
    )


ROW = 16


def route(pairs):
    count, slabs = lax.axis_size("ang"), lax.axis_size("slab")
    return [
        (a * slabs + s, (a if s // ROW == t // ROW else a ^ 1) * slabs + t)
        for a in range(count)
        for s, t in pairs
        if 0 <= t < slabs
    ]


def down_column(block, distance):
    count, slabs = lax.axis_size("ang"), lax.axis_size("slab")
    pairs = []
    for a in range(count):
        for t in range(slabs):
            z = (a % 2 * ROW + t % ROW) // 2
            there = (z - distance) % ROW
            to_ang = a - a % 2 + there * 2 // ROW
            to_slab = t - t % ROW + there * 2 % ROW + t % 2
            pairs.append((a * slabs + t, to_ang * slabs + to_slab))
    return lax.ppermute(block, ("ang", "slab"), pairs)


def from_far(low, high):
    high = down_column(high, ROW // 2 - 1)
    low = down_column(low, ROW // 2)
    return low, down_column(high, 1)


def to_next(block):
    pairs = [(s, s + 1) for s in range(lax.axis_size("slab"))]
    return lax.ppermute(block, ("ang", "slab"), route(pairs))


def to_previous(block):
    pairs = [(s, s - 1) for s in range(lax.axis_size("slab"))]
    return lax.ppermute(block, ("ang", "slab"), route(pairs))


VMEM = pl.BlockSpec(memory_space=pltpu.VMEM)
SMEM = pl.BlockSpec(memory_space=pltpu.SMEM)
ANY = pl.BlockSpec(memory_space=pl.ANY)


def pack_kernel(coef_ref, window_ref, volume_ref, measured_ref, out_ref):
    angles, rows, height, columns = measured_ref.shape
    layers = volume_ref.shape[0]
    depth = 2 * TILE
    coefs = [[coef_ref[k, z] for z in range(layers)] for k in range(angles * rows)]

    def chunk(i, carry):
        top = pl.multiple_of(i * depth, depth)
        for t in range(columns // LANES):
            lanes = pl.ds(t * LANES, LANES)
            planes = [volume_ref[z, pl.ds(top, depth), lanes] for z in range(layers)]
            for a in range(angles):
                for r in range(rows):
                    k = a * rows + r
                    total = planes[0] * coefs[k][0]
                    for z in range(1, layers):
                        total = total + planes[z] * coefs[k][z]
                    out_ref[pl.ds(pl.multiple_of(k * height + top, depth), depth), lanes] = (
                        measured_ref[a, r, pl.ds(top, depth), lanes].astype(jnp.float32) - total
                    )
        return carry

    lax.fori_loop(0, height // depth, chunk, 0)
    out_ref[angles * rows * height :, :] = window_ref[...]


def pack(coefs, window, volume, measured):
    angles, rows, height, columns = measured.shape
    return pl.pallas_call(
        pack_kernel,
        in_specs=[SMEM, VMEM, VMEM, VMEM],
        out_specs=VMEM,
        out_shape=jax.ShapeDtypeStruct((angles * rows * height + TILE, columns), jnp.float32),
        compiler_params=pltpu.CompilerParams(vmem_limit_bytes=8 * 2**20),
        name="pack",
    )(coefs, window, volume, measured)


def spread_kernel(coef_ref, sums_ref, own_ref, next_ref, out_ref):
    count, layers = coef_ref.shape
    ring = out_ref.shape[0]
    columns = own_ref.shape[1]
    height = (own_ref.shape[0] - TILE) // (count // 2)
    depth = height // ring
    ytiles, xtiles = depth // TILE, columns // LANES
    coefs = [[coef_ref[k, z] for z in range(layers)] for k in range(count)]
    body = layers * ytiles * xtiles * TILE

    def chunk(i, carry):
        top = pl.multiple_of(i * depth, depth)
        for t in range(xtiles):
            lanes = pl.ds(t * LANES, LANES)
            planes = [
                ref[pl.ds(k * height + top, depth), lanes]
                for ref in (own_ref, next_ref)
                for k in range(count // 2)
            ]
            for z in range(layers):
                total = planes[0] * coefs[0][z]
                for k in range(1, count):
                    total = total + planes[k] * coefs[k][z]
                for j in range(ytiles):
                    row = ((z * ytiles + j) * xtiles + t) * TILE
                    out_ref[i, row : row + TILE, :] = total[j * TILE : (j + 1) * TILE]
        out_ref[i, body : body + TILE, :] = sums_ref[...]
        return carry

    lax.fori_loop(0, ring, chunk, 0)


def spread(coefs, sums, own, following, height, ring):
    layers, columns = coefs.shape[1], own.shape[1]
    length = layers * (height // ring) * columns // LANES + TILE
    return pl.pallas_call(
        spread_kernel,
        in_specs=[SMEM, VMEM, VMEM, VMEM],
        out_specs=VMEM,
        out_shape=jax.ShapeDtypeStruct((ring, length, LANES), jnp.float32),
        compiler_params=pltpu.CompilerParams(vmem_limit_bytes=8 * 2**20),
        name="spread",
    )(coefs, sums, own, following)


def gather_kernel(parts_ref, low_ref, high_ref):
    ring = parts_ref.shape[0]
    half = high_ref.shape[0]
    step = 4 * TILE

    def total(start, size):
        value = parts_ref[0, pl.ds(start, size), :]
        for part in range(1, ring):
            value = value + parts_ref[part, pl.ds(start, size), :]
        return value

    def add(i, carry):
        row = pl.multiple_of(i * step, step)
        low_ref[pl.ds(row, step), :] = total(row, step)
        high_ref[pl.ds(row, step), :] = total(half + row, step)
        return carry

    lax.fori_loop(0, half // step, add, 0)
    low_ref[half:, :] = total(2 * half, TILE)


def gather(parts):
    half = (parts.shape[1] - TILE) // 2
    shape = lambda rows: jax.ShapeDtypeStruct((rows, LANES), jnp.float32)
    return pl.pallas_call(
        gather_kernel,
        in_specs=[VMEM],
        out_specs=[VMEM, VMEM],
        out_shape=[shape(half + TILE), shape(half)],
        compiler_params=pltpu.CompilerParams(vmem_limit_bytes=8 * 2**20),
        name="gather",
    )(parts)


def late_kernel(volume_ref, earlier_ref, whole_ref):
    for z in range(volume_ref.shape[0]):
        whole_ref[z] = volume_ref[z]


def late(volume, earlier):
    return pl.pallas_call(
        late_kernel,
        in_specs=[VMEM, ANY],
        out_specs=VMEM,
        out_shape=jax.ShapeDtypeStruct(volume.shape, jnp.float32),
        compiler_params=pltpu.CompilerParams(vmem_limit_bytes=8 * 2**20),
        cost_estimate=pl.CostEstimate(flops=0, bytes_accessed=32 * 2**20, transcendentals=0),
        name="late",
    )(volume, earlier)


def residual_kernel(coef_ref, before_ref, own_ref, out_ref, done_ref):
    done_ref[...] = jnp.zeros_like(done_ref)
    angles, rows, height, columns = out_ref.shape
    layers = before_ref.shape[0]
    depth = 2 * TILE
    coefs = [[coef_ref[k, z] for z in range(layers)] for k in range(angles * rows)]

    def chunk(i, carry):
        top = pl.multiple_of(i * depth, depth)
        for t in range(columns // LANES):
            lanes = pl.ds(t * LANES, LANES)
            planes = [before_ref[z, pl.ds(top, depth), lanes] for z in range(layers)]
            for a in range(angles):
                for r in range(rows):
                    k = a * rows + r
                    total = planes[0] * coefs[k][0]
                    for z in range(1, layers):
                        total = total + planes[z] * coefs[k][z]
                    row = pl.multiple_of(k * height + top, depth)
                    out_ref[a, r, pl.ds(top, depth), lanes] = (
                        own_ref[pl.ds(row, depth), lanes] - total
                    )
        return carry

    lax.fori_loop(0, height // depth, chunk, 0)


def residual_of(coefs, before, own, shape):
    return pl.pallas_call(
        residual_kernel,
        in_specs=[SMEM, VMEM, VMEM],
        out_specs=[VMEM, VMEM],
        out_shape=[
            jax.ShapeDtypeStruct(shape, jnp.float32),
            jax.ShapeDtypeStruct((TILE, LANES), jnp.float32),
        ],
        compiler_params=pltpu.CompilerParams(vmem_limit_bytes=8 * 2**20),
        name="residual",
    )(coefs, before, own)


def update_kernel(
    place_ref, low_ref, high_ref, far_low_ref, far_high_ref, before_ref, volume_ref, earlier_ref, out_ref
):
    copies, layers, depth, columns = out_ref.shape
    ytiles, xtiles = depth // TILE, columns // LANES
    half = high_ref.shape[0]
    top = pl.multiple_of(place_ref[0] * depth, depth)
    sums = low_ref[half:, :] + far_low_ref[half:, :]
    share = 1.0 / sums[:, 2 * layers : 2 * layers + 1]
    sums = sums * share

    def splat(value):
        return jnp.broadcast_to(value, (TILE, LANES))

    shares = [splat(share[z : z + 1, :]) for z in range(layers)]
    coefs = [
        [splat(sums[z : z + 1, k : k + 1]) for k in range(2 * layers)] for z in range(layers)
    ]
    for t in range(xtiles):
        lanes = pl.ds(t * LANES, LANES)
        for j in range(ytiles):
            rows = pl.ds(pl.multiple_of(top + j * TILE, TILE), TILE)
            planes = [ref[z, rows, lanes] for ref in (before_ref, volume_ref) for z in range(layers)]
            for z in range(layers):
                near, far = (low_ref, far_low_ref) if z < layers // 2 else (high_ref, far_high_ref)
                row = ((z % (layers // 2) * ytiles + j) * xtiles + t) * TILE
                total = (near[row : row + TILE, :] + far[row : row + TILE, :]) * shares[z]
                for k in range(2 * layers):
                    total = total - planes[k] * coefs[z][k]
                value = planes[layers + z] + total
                for copy in range(copies):
                    out_ref[copy, z, pl.ds(j * TILE, TILE), lanes] = value


def update(place, low, high, far_low, far_high, before, volume, earlier, ring):
    layers, height, columns = volume.shape
    return pl.pallas_call(
        update_kernel,
        in_specs=[SMEM] + [VMEM] * 6 + [ANY],
        out_specs=VMEM,
        out_shape=jax.ShapeDtypeStruct((ring, layers, height // ring, columns), jnp.float32),
        compiler_params=pltpu.CompilerParams(vmem_limit_bytes=8 * 2**20),
        name="update",
    )(place, low, high, far_low, far_high, before, volume, earlier)


def sweep(source, target, edge, lowest, highest):
    tall, columns = source.shape[1:]
    height = tall - TILE
    xtiles = columns // LANES
    lane = lax.broadcasted_iota(jnp.int32, (TILE, LANES), 1)
    level = lax.broadcasted_iota(jnp.int32, (TILE, LANES), 0)
    last_lane, first_lane = lane == LANES - 1, lane == 0
    last_row, first_row = level == TILE - 1, level == 0
    spans = [pl.ds(t * LANES, LANES) for t in range(xtiles)]
    for z in range(lowest, highest + 1):
        edge[z, :, :] = jnp.zeros((TILE, columns), jnp.float32)

    def band(i, carry):
        top = pl.multiple_of(i * TILE, TILE)
        rows = pl.ds(top, TILE)
        below = pl.ds(top + TILE, 1)
        upper = [source[lowest - 1, rows, span] for span in spans]
        flow_z = None
        for z in range(lowest - 1, highest + 1):
            base, upper = upper, [source[z + 1, rows, span] for span in spans]
            turned = [pltpu.roll(b, LANES - 1, 1) for b in base]
            grad_z, along, scaled = [], [], []
            for t in range(xtiles):
                rise = upper[t] - base[t]
                nearby = jnp.where(
                    last_row,
                    jnp.broadcast_to(source[z, below, spans[t]], (TILE, LANES)),
                    pltpu.roll(base[t], TILE - 1, 0),
                )
                down = nearby - base[t]
                right = jnp.where(
                    last_lane, turned[t + 1] if t + 1 < xtiles else base[t], turned[t]
                )
                across = right - base[t]
                scale = lax.rsqrt(rise * rise + down * down + across * across + 0.01)
                grad_z.append(rise * scale)
                along.append(down * scale)
                scaled.append(across * scale)
            if z >= lowest:
                moved = [pltpu.roll(p, 1, 1) for p in scaled]
                for t in range(xtiles):
                    left = jnp.where(first_lane, moved[t - 1] if t else 0.0, moved[t])
                    above = jnp.where(
                        first_row,
                        jnp.broadcast_to(edge[z, TILE - 1 : TILE, spans[t]], (TILE, LANES)),
                        pltpu.roll(along[t], 1, 0),
                    )
                    edge[z, :, spans[t]] = along[t]
                    div = (grad_z[t] - flow_z[t]) + (along[t] - above) + (scaled[t] - left)
                    target(z, rows, spans[t], base[t] + 0.05 * div)
            flow_z = grad_z
        return carry

    lax.fori_loop(0, height // TILE, band, 0)


def smooth_kernel(place_ref, own_ref, low_ref, high_ref, out_ref, field, middle, edge):
    ring, layers, depth, columns = own_ref.shape
    height = ring * depth
    keep_low = place_ref[1].astype(jnp.float32)
    keep_high = place_ref[2].astype(jnp.float32)

    def fill(i, carry):
        top = pl.multiple_of(i * depth, depth)
        for z in range(HALO):
            field[z, pl.ds(top, depth), :] = low_ref[i, z]
            field[HALO + layers + z, pl.ds(top, depth), :] = high_ref[i, z]
        for z in range(layers):
            field[HALO + z, pl.ds(top, depth), :] = own_ref[i, z]
        return carry

    lax.fori_loop(0, ring, fill, 0)
    for z in range(layers + 2 * HALO):
        field[z, height : height + 1, :] = field[z, height - 1 : height, :]

    def keep(z, rows, span, value):
        if z == HALO - 1:
            value = value * keep_low
        if z == HALO + layers:
            value = value * keep_high
        middle[z, rows, span] = value

    def finish(z, rows, span, value):
        out_ref[z - HALO, rows, span] = value

    sweep(field, keep, edge, HALO - 1, HALO + layers)
    for z in range(HALO - 1, HALO + layers + 1):
        middle[z, height : height + 1, :] = middle[z, height - 1 : height, :]
    sweep(middle, finish, edge, HALO, HALO + layers - 1)


def smooth(place, own, low, high):
    ring, layers, depth, columns = own.shape
    deep, height = layers + 2 * HALO, ring * depth
    return pl.pallas_call(
        smooth_kernel,
        in_specs=[SMEM, VMEM, VMEM, VMEM],
        out_specs=VMEM,
        out_shape=jax.ShapeDtypeStruct((layers, height, columns), jnp.float32),
        scratch_shapes=[
            pltpu.VMEM((deep, height + TILE, columns), jnp.float32),
            pltpu.VMEM((deep, height + TILE, columns), jnp.float32),
            pltpu.VMEM((deep, TILE, columns), jnp.float32),
        ],
        compiler_params=pltpu.CompilerParams(vmem_limit_bytes=16 * 2**20),
        name="smooth",
    )(place, own, low, high)


def windows(weights, shifts, bands):
    band_rows = weights.shape[1]
    rows_i = jnp.arange(band_rows, dtype=jnp.int32)[:, None]
    rows_j = jnp.arange(band_rows, dtype=jnp.int32)[None, :]
    placer = ((rows_i == rows_j + shifts[0, 0]) & (rows_j < bands[0, 0])).astype(jnp.float32)
    return jnp.sum(placer[None, :, :, None] * weights[:, None, :, :], axis=2)


def per_device(weights, shifts, bands, volume, measured):
    layers, height, columns = volume.shape
    own_rows = measured.shape[1]
    ring = lax.axis_size("ang") // 2
    depth = height // ring
    slab = lax.axis_index("slab")
    last_slab = lax.axis_size("slab") - 1
    place = jnp.stack(
        [lax.axis_index("ang") // 2, slab > 0, slab < last_slab]
    ).astype(jnp.int32)

    window = windows(weights, shifts, bands)
    low, high = window[:, :own_rows], window[:, own_rows:]
    count = window.shape[0] * own_rows
    flat = lambda block: block.reshape(count, layers)
    line = jnp.pad(window.reshape(1, -1), ((0, TILE - 1), (0, columns - window.size)))
    back = pack(flat(low), line, volume, measured)
    following = from_behind(back, "slab", -1)
    window_before = from_behind(window, "slab", 1)
    window_after = following[-TILE, : window.size].reshape(window.shape)

    low_after, high_before = window_after[:, :own_rows], window_before[:, own_rows:]
    total_own = jnp.sum(low, axis=2) + jnp.sum(high_before, axis=2)
    total_next = jnp.sum(low_after, axis=2) + jnp.sum(high, axis=2)
    share_own = 1.0 / jnp.maximum(total_own, 1.0)
    share_next = jnp.where(slab < last_slab, 1.0 / jnp.maximum(total_next, 1.0), 0.0)
    coefs_own = flat(low) * share_own.reshape(count, 1)
    coefs_next = flat(high) * share_next.reshape(count, 1)
    back_coefs = jnp.concatenate([coefs_own, coefs_next])
    normal_before = jnp.sum(coefs_own[:, :, None] * flat(high_before)[:, None, :], axis=0)
    normal_own = jnp.sum(coefs_next[:, :, None] * flat(high)[:, None, :], axis=0)
    column_part = jnp.sum(window, axis=(0, 1))
    sums = jnp.concatenate([normal_before, normal_own, column_part[:, None]], axis=1)
    sums = jnp.pad(sums, ((0, TILE - layers), (0, LANES - 2 * layers - 1)))

    sent = spread(back_coefs, sums, back, following, height, ring)
    before = to_next(late(volume, sent))
    near = gather(over_ring(sent))
    far = from_far(*near)
    residual, done = residual_of(flat(high_before), before, back, measured.shape)
    field = over_ring(update(place, *near, *far, before, volume, done, ring))
    halo_low = to_next(field[:, layers - HALO :])
    halo_high = to_previous(field[:, :HALO])
    updated = smooth(place, field, halo_low, halo_high)
    return (updated, residual)


def solution(mesh):
    return jax.shard_map(
        per_device,
        mesh=mesh,
        in_specs=(
            P("ang", None, "slab"),
            P("ang", "slab"),
            P("ang", "slab"),
            P("slab", None, None),
            P("ang", "slab", None, None),
        ),
        out_specs=(P("slab", None, None), P("ang", "slab", None, None)),
        check_vma=False,
    )
```

```python
import jax
import jax.numpy as jnp
from jax import lax
from jax.experimental import pallas as pl
from jax.experimental.pallas import tpu as pltpu
from jax.sharding import PartitionSpec as P

TILE = 8
LANES = 128
HALO = 2


def from_behind(block, axis, distance):
    devices = range(lax.axis_size(axis))
    route = [(i - distance, i) for i in devices if i - distance in devices]
    return lax.ppermute(block, axis, route)


def ring_groups():
    count = lax.axis_size("ang")
    return [list(range(0, count, 2)), list(range(1, count, 2))]


def over_ring(pieces):
    return lax.all_to_all(
        pieces, "ang", split_axis=0, concat_axis=0, axis_index_groups=ring_groups()
    )


ROW = 16


def route(pairs):
    count, slabs = lax.axis_size("ang"), lax.axis_size("slab")
    return [
        (a * slabs + s, (a if s // ROW == t // ROW else a ^ 1) * slabs + t)
        for a in range(count)
        for s, t in pairs
        if 0 <= t < slabs
    ]


def from_far(block):
    return lax.ppermute(block, "ang", [(a, a ^ 1) for a in range(lax.axis_size("ang"))])


def within_chip(block):
    return lax.ppermute(block, "slab", [(s, s ^ 1) for s in range(lax.axis_size("slab"))])


def across_chips(block):
    pairs = [(s, s + 1 if s % 2 else s - 1) for s in range(lax.axis_size("slab"))]
    return lax.ppermute(block, ("ang", "slab"), route(pairs))


def to_next(block):
    pairs = [(s, s + 1) for s in range(lax.axis_size("slab"))]
    return lax.ppermute(block, ("ang", "slab"), route(pairs))


def over_ring(pieces):
    return lax.all_to_all(
        pieces, "ang", split_axis=0, concat_axis=0, axis_index_groups=ring_groups()
    )


ROW = 16


def route(pairs):
    count, slabs = lax.axis_size("ang"), lax.axis_size("slab")
    return [
        (a * slabs + s, (a if s // ROW == t // ROW else a ^ 1) * slabs + t)
        for a in range(count)
        for s, t in pairs
        if 0 <= t < slabs
    ]


def from_far(block):
    return lax.ppermute(block, "ang", [(a, a ^ 1) for a in range(lax.axis_size("ang"))])


def within_chip(block):
    return lax.ppermute(block, "slab", [(s, s ^ 1) for s in range(lax.axis_size("slab"))])


def across_chips(block):
    pairs = [(s, s + 1 if s % 2 else s - 1) for s in range(lax.axis_size("slab"))]
    return lax.ppermute(block, ("ang", "slab"), route(pairs))


def to_next(block):
    pairs = [(s, s + 1) for s in range(lax.axis_size("slab"))]
    return lax.ppermute(block, ("ang", "slab"), route(pairs))


def to_previous(block):
    pairs = [(s, s - 1) for s in range(lax.axis_size("slab"))]
    return lax.ppermute(block, ("ang", "slab"), route(pairs))


VMEM = pl.BlockSpec(memory_space=pltpu.VMEM)
SMEM = pl.BlockSpec(memory_space=pltpu.SMEM)
ANY = pl.BlockSpec(memory_space=pl.ANY)


def splats(ref):
    rows, columns = ref.shape
    return [[jnp.full((TILE, LANES), ref[k, z]) for z in range(columns)] for k in range(rows)]


def combine(planes, coefs):
    total = planes[0] * coefs[0]
    for plane, coef in zip(planes[1:], coefs[1:]):
        total = total + plane * coef
    return total


def pack_kernel(coef_ref, window_ref, volume_ref, measured_ref, out_ref):
    angles, rows, height, columns = measured_ref.shape
    layers = volume_ref.shape[0]
    depth = 2 * TILE
    coefs = splats(coef_ref)
    out_ref[angles * rows * height :, :] = window_ref[...]

    def chunk(i, carry):
        top = pl.multiple_of(i * depth, depth)
        for t in range(columns // LANES):
            lanes = pl.ds(t * LANES, LANES)
            planes = [volume_ref[z, pl.ds(top, depth), lanes] for z in range(layers)]
            for a in range(angles):
                for r in range(rows):
                    k = a * rows + r
                    value = measured_ref[a, r, pl.ds(top, depth), lanes].astype(jnp.float32)
                    for j in range(depth // TILE):
                        tile = slice(j * TILE, (j + 1) * TILE)
                        row = pl.multiple_of(k * height + top + j * TILE, TILE)
                        out_ref[pl.ds(row, TILE), lanes] = value[tile] - combine(
                            [plane[tile] for plane in planes], coefs[k]
                        )
        return carry

    lax.fori_loop(0, height // depth, chunk, 0)


def pack(coefs, window, volume, measured):
    angles, rows, height, columns = measured.shape
    return pl.pallas_call(
        pack_kernel,
        in_specs=[SMEM, VMEM, VMEM, VMEM],
        out_specs=VMEM,
        out_shape=jax.ShapeDtypeStruct((angles * rows * height + TILE, columns), jnp.float32),
        compiler_params=pltpu.CompilerParams(vmem_limit_bytes=8 * 2**20),
        name="pack",
    )(coefs, window, volume, measured)


def spread_kernel(coef_ref, sums_ref, own_ref, next_ref, out_ref):
    count, layers = coef_ref.shape
    ring = out_ref.shape[0]
    columns = own_ref.shape[1]
    height = (own_ref.shape[0] - TILE) // (count // 2)
    depth = height // ring
    ytiles, xtiles = depth // TILE, columns // LANES
    coefs = splats(coef_ref)
    body = layers * ytiles * xtiles * TILE

    def chunk(i, carry):
        top = i * depth
        for t in range(xtiles):
            lanes = pl.ds(t * LANES, LANES)
            for j in range(ytiles):
                planes = [
                    ref[pl.ds(pl.multiple_of(k * height + top + j * TILE, TILE), TILE), lanes]
                    for ref in (own_ref, next_ref)
                    for k in range(count // 2)
                ]
                for z in range(layers):
                    row = ((z * ytiles + j) * xtiles + t) * TILE
                    out_ref[i, row : row + TILE, :] = combine(planes, [c[z] for c in coefs])
        out_ref[i, body : body + TILE, :] = sums_ref[...]
        return carry

    lax.fori_loop(0, ring, chunk, 0)


def spread(coefs, sums, own, following, height, ring):
    layers, columns = coefs.shape[1], own.shape[1]
    length = layers * (height // ring) * columns // LANES + TILE
    return pl.pallas_call(
        spread_kernel,
        in_specs=[SMEM, VMEM, VMEM, VMEM],
        out_specs=VMEM,
        out_shape=jax.ShapeDtypeStruct((ring, length, LANES), jnp.float32),
        compiler_params=pltpu.CompilerParams(vmem_limit_bytes=8 * 2**20),
        name="spread",
    )(coefs, sums, own, following)


def gather_kernel(parts_ref, mine_ref):
    ring, length, _ = parts_ref.shape
    step = next(n for n in (5 * TILE, 3 * TILE, TILE) if length % n == 0)

    def add(i, carry):
        rows = pl.ds(pl.multiple_of(i * step, TILE), step)
        total = parts_ref[0, rows, :]
        for part in range(1, ring):
            total = total + parts_ref[part, rows, :]
        mine_ref[rows, :] = total
        return carry

    lax.fori_loop(0, length // step, add, 0)


def gather(parts):
    return pl.pallas_call(
        gather_kernel,
        in_specs=[VMEM],
        out_specs=VMEM,
        out_shape=jax.ShapeDtypeStruct(parts.shape[1:], jnp.float32),
        compiler_params=pltpu.CompilerParams(vmem_limit_bytes=8 * 2**20),
        name="gather",
    )(parts)


def copies_kernel(block_ref, out_ref):
    for z in range(block_ref.shape[0]):
        block = block_ref[z]
        for copy in range(out_ref.shape[0]):
            out_ref[copy, z] = block


def copies_of(block, count):
    return pl.pallas_call(
        copies_kernel,
        in_specs=[VMEM],
        out_specs=VMEM,
        out_shape=jax.ShapeDtypeStruct((count,) + block.shape, jnp.float32),
        compiler_params=pltpu.CompilerParams(vmem_limit_bytes=8 * 2**20),
        name="copies",
    )(block)


def facing_kernel(place_ref, field_ref, earlier_ref, out_ref):
    ring, layers = field_ref.shape[:2]
    first = (1 - place_ref[1]) * (layers - HALO)
    for i in range(ring):
        for z in range(HALO):
            out_ref[i, z] = field_ref[i, first + z]


def facing(place, field, earlier):
    ring, _, depth, columns = field.shape
    return pl.pallas_call(
        facing_kernel,
        in_specs=[SMEM, VMEM, ANY],
        out_specs=VMEM,
        out_shape=jax.ShapeDtypeStruct((ring, HALO, depth, columns), jnp.float32),
        compiler_params=pltpu.CompilerParams(vmem_limit_bytes=8 * 2**20),
        name="facing",
    )(place, field, earlier)


def late_kernel(volume_ref, earlier_ref, whole_ref):
    for z in range(volume_ref.shape[0]):
        whole_ref[z] = volume_ref[z]


def late(volume, earlier):
    return pl.pallas_call(
        late_kernel,
        in_specs=[VMEM, ANY],
        out_specs=VMEM,
        out_shape=jax.ShapeDtypeStruct(volume.shape, jnp.float32),
        compiler_params=pltpu.CompilerParams(vmem_limit_bytes=8 * 2**20),
        cost_estimate=pl.CostEstimate(flops=0, bytes_accessed=32 * 2**20, transcendentals=0),
        name="late",
    )(volume, earlier)


def residual_kernel(coef_ref, before_ref, own_ref, out_ref, done_ref):
    done_ref[...] = jnp.zeros_like(done_ref)
    angles, rows, height, columns = out_ref.shape
    layers = before_ref.shape[0]
    depth = 2 * TILE
    coefs = [[coef_ref[k, z] for z in range(layers)] for k in range(angles * rows)]

    def chunk(i, carry):
        top = pl.multiple_of(i * depth, depth)
        for t in range(columns // LANES):
            lanes = pl.ds(t * LANES, LANES)
            planes = [before_ref[z, pl.ds(top, depth), lanes] for z in range(layers)]
            for a in range(angles):
                for r in range(rows):
                    k = a * rows + r
                    total = planes[0] * coefs[k][0]
                    for z in range(1, layers):
                        total = total + planes[z] * coefs[k][z]
                    row = pl.multiple_of(k * height + top, depth)
                    out_ref[a, r, pl.ds(top, depth), lanes] = (
                        own_ref[pl.ds(row, depth), lanes] - total
                    )
        return carry

    lax.fori_loop(0, height // depth, chunk, 0)


def residual_of(coefs, before, own, shape):
    return pl.pallas_call(
        residual_kernel,
        in_specs=[SMEM, VMEM, VMEM],
        out_specs=[VMEM, VMEM],
        out_shape=[
            jax.ShapeDtypeStruct(shape, jnp.float32),
            jax.ShapeDtypeStruct((TILE, LANES), jnp.float32),
        ],
        compiler_params=pltpu.CompilerParams(vmem_limit_bytes=8 * 2**20),
        name="residual",
    )(coefs, before, own)


def update_kernel(
    place_ref, near_ref, far_ref, before_ref, volume_ref, earlier_ref, out_ref, cross_ref
):
    copies, layers, depth, columns = out_ref.shape
    ytiles, xtiles = depth // TILE, columns // LANES
    body = layers * ytiles * xtiles * TILE
    top = pl.multiple_of(place_ref[0] * depth, depth)
    odd = place_ref[1] == 1
    sums = near_ref[body:, :] + far_ref[body:, :]
    share = 1.0 / sums[:, 2 * layers : 2 * layers + 1]
    sums = sums * share

    def splat(value):
        return jnp.broadcast_to(value, (TILE, LANES))

    shares = [splat(share[z : z + 1, :]) for z in range(layers)]
    coefs = [
        [splat(sums[z : z + 1, k : k + 1]) for k in range(2 * layers)] for z in range(layers)
    ]
    for t in range(xtiles):
        lanes = pl.ds(t * LANES, LANES)
        for j in range(ytiles):
            part = pl.ds(j * TILE, TILE)
            rows = pl.ds(pl.multiple_of(top + j * TILE, TILE), TILE)
            planes = [ref[z, rows, lanes] for ref in (before_ref, volume_ref) for z in range(layers)]
            values = []
            for z in range(layers):
                row = ((z * ytiles + j) * xtiles + t) * TILE
                total = (near_ref[row : row + TILE, :] + far_ref[row : row + TILE, :]) * shares[z]
                values.append(planes[layers + z] + (total - combine(planes, coefs[z])))
                for copy in range(copies):
                    out_ref[copy, z, part, lanes] = values[z]
            for z in range(HALO):
                cross_ref[z, part, lanes] = jnp.where(odd, values[layers - HALO + z], values[z])


def update(place, near, far, before, volume, earlier, ring):
    layers, height, columns = volume.shape
    shape = lambda *sizes: jax.ShapeDtypeStruct(sizes + (height // ring, columns), jnp.float32)
    return pl.pallas_call(
        update_kernel,
        in_specs=[SMEM] + [VMEM] * 4 + [ANY],
        out_specs=[VMEM, VMEM],
        out_shape=[shape(ring, layers), shape(HALO)],
        compiler_params=pltpu.CompilerParams(vmem_limit_bytes=8 * 2**20),
        name="update",
    )(place, near, far, before, volume, earlier)


def sweep(source, target, edge, lowest, highest):
    tall, columns = source.shape[1:]
    height = tall - TILE
    xtiles = columns // LANES
    lane = lax.broadcasted_iota(jnp.int32, (TILE, LANES), 1)
    level = lax.broadcasted_iota(jnp.int32, (TILE, LANES), 0)
    last_lane, first_lane = lane == LANES - 1, lane == 0
    last_row, first_row = level == TILE - 1, level == 0
    spans = [pl.ds(t * LANES, LANES) for t in range(xtiles)]
    for z in range(lowest, highest + 1):
        edge[z, :, :] = jnp.zeros((TILE, columns), jnp.float32)

    def band(i, carry):
        top = pl.multiple_of(i * TILE, TILE)
        rows = pl.ds(top, TILE)
        below = pl.ds(top + TILE, 1)
        upper = [source[lowest - 1, rows, span] for span in spans]
        flow_z = None
        for z in range(lowest - 1, highest + 1):
            base, upper = upper, [source[z + 1, rows, span] for span in spans]
            turned = [pltpu.roll(b, LANES - 1, 1) for b in base]
            grad_z, along, scaled = [], [], []
            for t in range(xtiles):
                rise = upper[t] - base[t]
                nearby = jnp.where(
                    last_row,
                    jnp.broadcast_to(source[z, below, spans[t]], (TILE, LANES)),
                    pltpu.roll(base[t], TILE - 1, 0),
                )
                down = nearby - base[t]
                right = jnp.where(
                    last_lane, turned[t + 1] if t + 1 < xtiles else base[t], turned[t]
                )
                across = right - base[t]
                scale = lax.rsqrt(rise * rise + down * down + across * across + 0.01)
                grad_z.append(rise * scale)
                along.append(down * scale)
                scaled.append(across * scale)
            if z >= lowest:
                moved = [pltpu.roll(p, 1, 1) for p in scaled]
                for t in range(xtiles):
                    left = jnp.where(first_lane, moved[t - 1] if t else 0.0, moved[t])
                    above = jnp.where(
                        first_row,
                        jnp.broadcast_to(edge[z, TILE - 1 : TILE, spans[t]], (TILE, LANES)),
                        pltpu.roll(along[t], 1, 0),
                    )
                    edge[z, :, spans[t]] = along[t]
                    div = (grad_z[t] - flow_z[t]) + (along[t] - above) + (scaled[t] - left)
                    target(z, rows, spans[t], base[t] + 0.05 * div)
            flow_z = grad_z
        return carry

    lax.fori_loop(0, height // TILE, band, 0)


def smooth_kernel(place_ref, own_ref, cross_ref, inner_ref, out_ref, field, middle, edge):
    ring, layers, depth, columns = own_ref.shape
    height = ring * depth
    odd = place_ref[1] == 1
    keep_low = place_ref[2].astype(jnp.float32)
    keep_high = place_ref[3].astype(jnp.float32)

    def fill(i, carry):
        rows = pl.ds(pl.multiple_of(i * depth, depth), depth)
        for z in range(HALO):
            cross, inner = cross_ref[i, z], inner_ref[i, z]
            field[z, rows, :] = jnp.where(odd, inner, cross)
            field[HALO + layers + z, rows, :] = jnp.where(odd, cross, inner)
        for z in range(layers):
            field[HALO + z, rows, :] = own_ref[i, z]
        return carry

    lax.fori_loop(0, ring, fill, 0)
    for z in range(layers + 2 * HALO):
        field[z, height : height + 1, :] = field[z, height - 1 : height, :]

    def keep(z, rows, span, value):
        if z == HALO - 1:
            value = value * keep_low
        if z == HALO + layers:
            value = value * keep_high
        middle[z, rows, span] = value

    def finish(z, rows, span, value):
        out_ref[z - HALO, rows, span] = value

    sweep(field, keep, edge, HALO - 1, HALO + layers)
    for z in range(HALO - 1, HALO + layers + 1):
        middle[z, height : height + 1, :] = middle[z, height - 1 : height, :]
    sweep(middle, finish, edge, HALO, HALO + layers - 1)


def smooth(place, own, cross, inner):
    ring, layers, depth, columns = own.shape
    deep, height = layers + 2 * HALO, ring * depth
    return pl.pallas_call(
        smooth_kernel,
        in_specs=[SMEM, VMEM, VMEM, VMEM],
        out_specs=VMEM,
        out_shape=jax.ShapeDtypeStruct((layers, height, columns), jnp.float32),
        scratch_shapes=[
            pltpu.VMEM((deep, height + TILE, columns), jnp.float32),
            pltpu.VMEM((deep, height + TILE, columns), jnp.float32),
            pltpu.VMEM((deep, TILE, columns), jnp.float32),
        ],
        compiler_params=pltpu.CompilerParams(vmem_limit_bytes=16 * 2**20),
        name="smooth",
    )(place, own, cross, inner)


def windows(weights, shifts, bands):
    band_rows = weights.shape[1]
    rows_i = jnp.arange(band_rows, dtype=jnp.int32)[:, None]
    rows_j = jnp.arange(band_rows, dtype=jnp.int32)[None, :]
    placer = ((rows_i == rows_j + shifts[0, 0]) & (rows_j < bands[0, 0])).astype(jnp.float32)
    return jnp.sum(placer[None, :, :, None] * weights[:, None, :, :], axis=2)


def per_device(weights, shifts, bands, volume, measured):
    layers, height, columns = volume.shape
    own_rows = measured.shape[1]
    ring = lax.axis_size("ang") // 2
    depth = height // ring
    slab = lax.axis_index("slab")
    last_slab = lax.axis_size("slab") - 1
    place = jnp.stack(
        [lax.axis_index("ang") // 2, slab % 2, slab > 0, slab < last_slab]
    ).astype(jnp.int32)

    window = windows(weights, shifts, bands)
    low, high = window[:, :own_rows], window[:, own_rows:]
    count = window.shape[0] * own_rows
    flat = lambda block: block.reshape(count, layers)
    line = jnp.pad(window.reshape(1, -1), ((0, TILE - 1), (0, columns - window.size)))
    back = pack(flat(low), line, volume, measured)
    following = from_behind(back, "slab", -1)
    window_before = from_behind(window, "slab", 1)
    window_after = following[-TILE, : window.size].reshape(window.shape)

    low_after, high_before = window_after[:, :own_rows], window_before[:, own_rows:]
    total_own = jnp.sum(low, axis=2) + jnp.sum(high_before, axis=2)
    total_next = jnp.sum(low_after, axis=2) + jnp.sum(high, axis=2)
    share_own = 1.0 / jnp.maximum(total_own, 1.0)
    share_next = jnp.where(slab < last_slab, 1.0 / jnp.maximum(total_next, 1.0), 0.0)
    coefs_own = flat(low) * share_own.reshape(count, 1)
    coefs_next = flat(high) * share_next.reshape(count, 1)
    back_coefs = jnp.concatenate([coefs_own, coefs_next])
    normal_before = jnp.sum(coefs_own[:, :, None] * flat(high_before)[:, None, :], axis=0)
    normal_own = jnp.sum(coefs_next[:, :, None] * flat(high)[:, None, :], axis=0)
    column_part = jnp.sum(window, axis=(0, 1))
    sums = jnp.concatenate([normal_before, normal_own, column_part[:, None]], axis=1)
    sums = jnp.pad(sums, ((0, TILE - layers), (0, LANES - 2 * layers - 1)))

    sent = spread(back_coefs, sums, back, following, height, ring)
    before = to_next(late(volume, sent))
    near = gather(over_ring(sent))
    far = from_far(near)
    residual, done = residual_of(flat(high_before), before, back, measured.shape)
    pieces, cross = update(place, near, far, before, volume, done, ring)
    field = over_ring(pieces)
    cross = copies_of(across_chips(cross), ring)
    inner = within_chip(facing(place, field, cross))
    updated = smooth(place, field, over_ring(cross), inner)
    return (updated, residual)


def solution(mesh):
    return jax.shard_map(
        per_device,
        mesh=mesh,
        in_specs=(
            P("ang", None, "slab"),
            P("ang", "slab"),
            P("ang", "slab"),
            P("slab", None, None),
            P("ang", "slab", None, None),
        ),
        out_specs=(P("slab", None, None), P("ang", "slab", None, None)),
        check_vma=False,
    )
```

```python
import jax
import jax.numpy as jnp
from jax import lax
from jax.experimental import pallas as pl
from jax.experimental.pallas import tpu as pltpu
from jax.sharding import PartitionSpec as P

TILE = 8
LANES = 128
HALO = 2


def from_behind(block, axis, distance):
    devices = range(lax.axis_size(axis))
    route = [(i - distance, i) for i in devices if i - distance in devices]
    return lax.ppermute(block, axis, route)


def ring_groups():
    count = lax.axis_size("ang")
    return [list(range(0, count, 2)), list(range(1, count, 2))]


def over_ring(pieces):
    return lax.all_to_all(
        pieces, "ang", split_axis=0, concat_axis=0, axis_index_groups=ring_groups()
    )


ROW = 16


def route(pairs):
    count, slabs = lax.axis_size("ang"), lax.axis_size("slab")
    return [
        (a * slabs + s, (a if s // ROW == t // ROW else a ^ 1) * slabs + t)
        for a in range(count)
        for s, t in pairs
        if 0 <= t < slabs
    ]


def from_far(block):
    return lax.ppermute(block, "ang", [(a, a ^ 1) for a in range(lax.axis_size("ang"))])


def to_next(block):
    pairs = [(s, s + 1) for s in range(lax.axis_size("slab"))]
    return lax.ppermute(block, ("ang", "slab"), route(pairs))


def over_ring(pieces):
    return lax.all_to_all(
        pieces, "ang", split_axis=0, concat_axis=0, axis_index_groups=ring_groups()
    )


ROW = 16


def route(pairs):
    count, slabs = lax.axis_size("ang"), lax.axis_size("slab")
    return [
        (a * slabs + s, (a if s // ROW == t // ROW else a ^ 1) * slabs + t)
        for a in range(count)
        for s, t in pairs
        if 0 <= t < slabs
    ]


def from_far(block):
    return lax.ppermute(block, "ang", [(a, a ^ 1) for a in range(lax.axis_size("ang"))])


def within_chip(block):
    return lax.ppermute(block, "slab", [(s, s ^ 1) for s in range(lax.axis_size("slab"))])


def across_chips(block):
    pairs = [(s, s + 1 if s % 2 else s - 1) for s in range(lax.axis_size("slab"))]
    return lax.ppermute(block, ("ang", "slab"), route(pairs))


def to_next(block):
    pairs = [(s, s + 1) for s in range(lax.axis_size("slab"))]
    return lax.ppermute(block, ("ang", "slab"), route(pairs))


def to_previous(block):
    pairs = [(s, s - 1) for s in range(lax.axis_size("slab"))]
    return lax.ppermute(block, ("ang", "slab"), route(pairs))


VMEM = pl.BlockSpec(memory_space=pltpu.VMEM)
SMEM = pl.BlockSpec(memory_space=pltpu.SMEM)
ANY = pl.BlockSpec(memory_space=pl.ANY)


def splats(ref):
    rows, columns = ref.shape
    return [[jnp.full((TILE, LANES), ref[k, z]) for z in range(columns)] for k in range(rows)]


def combine(planes, coefs):
    total = planes[0] * coefs[0]
    for plane, coef in zip(planes[1:], coefs[1:]):
        total = total + plane * coef
    return total


def pack_kernel(coef_ref, window_ref, volume_ref, measured_ref, out_ref):
    angles, rows, height, columns = measured_ref.shape
    layers = volume_ref.shape[0]
    depth = 2 * TILE
    coefs = splats(coef_ref)
    out_ref[angles * rows * height :, :] = window_ref[...]

    def chunk(i, carry):
        top = pl.multiple_of(i * depth, depth)
        for t in range(columns // LANES):
            lanes = pl.ds(t * LANES, LANES)
            planes = [volume_ref[z, pl.ds(top, depth), lanes] for z in range(layers)]
            for a in range(angles):
                for r in range(rows):
                    k = a * rows + r
                    value = measured_ref[a, r, pl.ds(top, depth), lanes].astype(jnp.float32)
                    for j in range(depth // TILE):
                        tile = slice(j * TILE, (j + 1) * TILE)
                        row = pl.multiple_of(k * height + top + j * TILE, TILE)
                        out_ref[pl.ds(row, TILE), lanes] = value[tile] - combine(
                            [plane[tile] for plane in planes], coefs[k]
                        )
        return carry

    lax.fori_loop(0, height // depth, chunk, 0)


def pack(coefs, window, volume, measured):
    angles, rows, height, columns = measured.shape
    return pl.pallas_call(
        pack_kernel,
        in_specs=[SMEM, VMEM, VMEM, VMEM],
        out_specs=VMEM,
        out_shape=jax.ShapeDtypeStruct((angles * rows * height + TILE, columns), jnp.float32),
        compiler_params=pltpu.CompilerParams(vmem_limit_bytes=8 * 2**20),
        name="pack",
    )(coefs, window, volume, measured)


def spread_kernel(coef_ref, sums_ref, own_ref, next_ref, earlier_ref, out_ref):
    count, layers = coef_ref.shape
    ring = out_ref.shape[0]
    columns = own_ref.shape[1]
    height = (own_ref.shape[0] - TILE) // (count // 2)
    depth = height // ring
    ytiles, xtiles = depth // TILE, columns // LANES
    coefs = splats(coef_ref)
    body = layers * ytiles * xtiles * TILE

    def chunk(i, carry):
        top = i * depth
        for t in range(xtiles):
            lanes = pl.ds(t * LANES, LANES)
            for j in range(ytiles):
                planes = [
                    ref[pl.ds(pl.multiple_of(k * height + top + j * TILE, TILE), TILE), lanes]
                    for ref in (own_ref, next_ref)
                    for k in range(count // 2)
                ]
                for z in range(layers):
                    row = ((z * ytiles + j) * xtiles + t) * TILE
                    out_ref[i, row : row + TILE, :] = combine(planes, [c[z] for c in coefs])
        out_ref[i, body : body + TILE, :] = sums_ref[...]
        return carry

    lax.fori_loop(0, ring, chunk, 0)


def spread(coefs, sums, own, following, earlier, height, ring):
    layers, columns = coefs.shape[1], own.shape[1]
    length = layers * (height // ring) * columns // LANES + TILE
    return pl.pallas_call(
        spread_kernel,
        in_specs=[SMEM, VMEM, VMEM, VMEM, ANY],
        out_specs=VMEM,
        out_shape=jax.ShapeDtypeStruct((ring, length, LANES), jnp.float32),
        compiler_params=pltpu.CompilerParams(vmem_limit_bytes=8 * 2**20),
        name="spread",
    )(coefs, sums, own, following, earlier)


def gather_kernel(parts_ref, mine_ref):
    ring, length, _ = parts_ref.shape
    step = next(n for n in (5 * TILE, 3 * TILE, TILE) if length % n == 0)

    def add(i, carry):
        rows = pl.ds(pl.multiple_of(i * step, TILE), step)
        total = parts_ref[0, rows, :]
        for part in range(1, ring):
            total = total + parts_ref[part, rows, :]
        mine_ref[rows, :] = total
        return carry

    lax.fori_loop(0, length // step, add, 0)


def gather(parts):
    return pl.pallas_call(
        gather_kernel,
        in_specs=[VMEM],
        out_specs=VMEM,
        out_shape=jax.ShapeDtypeStruct(parts.shape[1:], jnp.float32),
        compiler_params=pltpu.CompilerParams(vmem_limit_bytes=8 * 2**20),
        name="gather",
    )(parts)


def piece_kernel(place_ref, volume_ref, earlier_ref, out_ref):
    layers, depth, _ = out_ref.shape
    top = pl.multiple_of(place_ref[0] * depth, depth)
    for z in range(layers):
        out_ref[z] = volume_ref[z, pl.ds(top, depth), :]


def piece_of(place, volume, earlier, depth):
    layers, _, columns = volume.shape
    return pl.pallas_call(
        piece_kernel,
        in_specs=[SMEM, VMEM, ANY],
        out_specs=VMEM,
        out_shape=jax.ShapeDtypeStruct((layers, depth, columns), jnp.float32),
        compiler_params=pltpu.CompilerParams(vmem_limit_bytes=8 * 2**20),
        cost_estimate=pl.CostEstimate(flops=0, bytes_accessed=32 * 2**20, transcendentals=0),
        name="piece",
    )(place, volume, earlier)


def late_kernel(volume_ref, earlier_ref, whole_ref):
    for z in range(volume_ref.shape[0]):
        whole_ref[z] = volume_ref[z]


def late(volume, earlier):
    return pl.pallas_call(
        late_kernel,
        in_specs=[VMEM, ANY],
        out_specs=VMEM,
        out_shape=jax.ShapeDtypeStruct(volume.shape, jnp.float32),
        compiler_params=pltpu.CompilerParams(vmem_limit_bytes=8 * 2**20),
        cost_estimate=pl.CostEstimate(flops=0, bytes_accessed=32 * 2**20, transcendentals=0),
        name="late",
    )(volume, earlier)


def residual_kernel(coef_ref, before_ref, own_ref, out_ref, done_ref):
    done_ref[...] = jnp.zeros_like(done_ref)
    angles, rows, height, columns = out_ref.shape
    layers = before_ref.shape[0]
    depth = 2 * TILE
    coefs = [[coef_ref[k, z] for z in range(layers)] for k in range(angles * rows)]

    def chunk(i, carry):
        top = pl.multiple_of(i * depth, depth)
        for t in range(columns // LANES):
            lanes = pl.ds(t * LANES, LANES)
            planes = [before_ref[z, pl.ds(top, depth), lanes] for z in range(layers)]
            for a in range(angles):
                for r in range(rows):
                    k = a * rows + r
                    total = planes[0] * coefs[k][0]
                    for z in range(1, layers):
                        total = total + planes[z] * coefs[k][z]
                    row = pl.multiple_of(k * height + top, depth)
                    out_ref[a, r, pl.ds(top, depth), lanes] = (
                        own_ref[pl.ds(row, depth), lanes] - total
                    )
        return carry

    lax.fori_loop(0, height // depth, chunk, 0)


def residual_of(coefs, before, own, shape):
    return pl.pallas_call(
        residual_kernel,
        in_specs=[SMEM, VMEM, VMEM],
        out_specs=[VMEM, VMEM],
        out_shape=[
            jax.ShapeDtypeStruct(shape, jnp.float32),
            jax.ShapeDtypeStruct((TILE, LANES), jnp.float32),
        ],
        compiler_params=pltpu.CompilerParams(vmem_limit_bytes=8 * 2**20),
        cost_estimate=pl.CostEstimate(flops=0, bytes_accessed=16 * 2**20, transcendentals=0),
        name="residual",
    )(coefs, before, own)


def update_kernel(near_ref, far_ref, before_ref, piece_ref, out_ref):
    copies, layers, depth, columns = out_ref.shape
    ytiles, xtiles = depth // TILE, columns // LANES
    body = layers * ytiles * xtiles * TILE
    sums = near_ref[body:, :] + far_ref[body:, :]
    share = 1.0 / sums[:, 2 * layers : 2 * layers + 1]
    sums = sums * share

    def splat(value):
        return jnp.broadcast_to(value, (TILE, LANES))

    shares = [splat(share[z : z + 1, :]) for z in range(layers)]
    coefs = [
        [splat(sums[z : z + 1, k : k + 1]) for k in range(2 * layers)] for z in range(layers)
    ]
    for t in range(xtiles):
        lanes = pl.ds(t * LANES, LANES)
        for j in range(ytiles):
            rows = pl.ds(j * TILE, TILE)
            planes = [ref[z, rows, lanes] for ref in (before_ref, piece_ref) for z in range(layers)]
            for z in range(layers):
                row = ((z * ytiles + j) * xtiles + t) * TILE
                total = (near_ref[row : row + TILE, :] + far_ref[row : row + TILE, :]) * shares[z]
                value = planes[layers + z] + (total - combine(planes, coefs[z]))
                for copy in range(copies):
                    out_ref[copy, z, rows, lanes] = value


def update(near, far, before, piece, ring):
    return pl.pallas_call(
        update_kernel,
        in_specs=[VMEM] * 4,
        out_specs=VMEM,
        out_shape=jax.ShapeDtypeStruct((ring,) + piece.shape, jnp.float32),
        compiler_params=pltpu.CompilerParams(vmem_limit_bytes=8 * 2**20),
        name="update",
    )(near, far, before, piece)


def sweep(source, target, edge, lowest, highest):
    tall, columns = source.shape[1:]
    height = tall - TILE
    xtiles = columns // LANES
    lane = lax.broadcasted_iota(jnp.int32, (TILE, LANES), 1)
    level = lax.broadcasted_iota(jnp.int32, (TILE, LANES), 0)
    last_lane, first_lane = lane == LANES - 1, lane == 0
    last_row, first_row = level == TILE - 1, level == 0
    spans = [pl.ds(t * LANES, LANES) for t in range(xtiles)]
    for z in range(lowest, highest + 1):
        edge[z, :, :] = jnp.zeros((TILE, columns), jnp.float32)

    def band(i, carry):
        top = pl.multiple_of(i * TILE, TILE)
        rows = pl.ds(top, TILE)
        below = pl.ds(top + TILE, 1)
        upper = [source[lowest - 1, rows, span] for span in spans]
        flow_z = None
        for z in range(lowest - 1, highest + 1):
            base, upper = upper, [source[z + 1, rows, span] for span in spans]
            turned = [pltpu.roll(b, LANES - 1, 1) for b in base]
            grad_z, along, scaled = [], [], []
            for t in range(xtiles):
                rise = upper[t] - base[t]
                nearby = jnp.where(
                    last_row,
                    jnp.broadcast_to(source[z, below, spans[t]], (TILE, LANES)),
                    pltpu.roll(base[t], TILE - 1, 0),
                )
                down = nearby - base[t]
                right = jnp.where(
                    last_lane, turned[t + 1] if t + 1 < xtiles else base[t], turned[t]
                )
                across = right - base[t]
                scale = lax.rsqrt(rise * rise + down * down + across * across + 0.01)
                grad_z.append(rise * scale)
                along.append(down * scale)
                scaled.append(across * scale)
            if z >= lowest:
                moved = [pltpu.roll(p, 1, 1) for p in scaled]
                for t in range(xtiles):
                    left = jnp.where(first_lane, moved[t - 1] if t else 0.0, moved[t])
                    above = jnp.where(
                        first_row,
                        jnp.broadcast_to(edge[z, TILE - 1 : TILE, spans[t]], (TILE, LANES)),
                        pltpu.roll(along[t], 1, 0),
                    )
                    edge[z, :, spans[t]] = along[t]
                    div = (grad_z[t] - flow_z[t]) + (along[t] - above) + (scaled[t] - left)
                    target(z, rows, spans[t], base[t] + 0.05 * div)
            flow_z = grad_z
        return carry

    lax.fori_loop(0, height // TILE, band, 0)


def smooth_kernel(place_ref, earlier_ref, own_ref, low_ref, high_ref, out_ref, field, middle, edge):
    ring, layers, depth, columns = own_ref.shape
    height = ring * depth
    keep_low = place_ref[1].astype(jnp.float32)
    keep_high = place_ref[2].astype(jnp.float32)

    def fill(i, carry):
        top = pl.multiple_of(i * depth, depth)
        for z in range(HALO):
            field[z, pl.ds(top, depth), :] = low_ref[i, z]
            field[HALO + layers + z, pl.ds(top, depth), :] = high_ref[i, z]
        for z in range(layers):
            field[HALO + z, pl.ds(top, depth), :] = own_ref[i, z]
        return carry

    lax.fori_loop(0, ring, fill, 0)
    for z in range(layers + 2 * HALO):
        field[z, height : height + 1, :] = field[z, height - 1 : height, :]

    def keep(z, rows, span, value):
        if z == HALO - 1:
            value = value * keep_low
        if z == HALO + layers:
            value = value * keep_high
        middle[z, rows, span] = value

    def finish(z, rows, span, value):
        out_ref[z - HALO, rows, span] = value

    sweep(field, keep, edge, HALO - 1, HALO + layers)
    for z in range(HALO - 1, HALO + layers + 1):
        middle[z, height : height + 1, :] = middle[z, height - 1 : height, :]
    sweep(middle, finish, edge, HALO, HALO + layers - 1)


def smooth(place, earlier, own, low, high):
    ring, layers, depth, columns = own.shape
    deep, height = layers + 2 * HALO, ring * depth
    return pl.pallas_call(
        smooth_kernel,
        in_specs=[SMEM, ANY, VMEM, VMEM, VMEM],
        out_specs=VMEM,
        out_shape=jax.ShapeDtypeStruct((layers, height, columns), jnp.float32),
        scratch_shapes=[
            pltpu.VMEM((deep, height + TILE, columns), jnp.float32),
            pltpu.VMEM((deep, height + TILE, columns), jnp.float32),
            pltpu.VMEM((deep, TILE, columns), jnp.float32),
        ],
        compiler_params=pltpu.CompilerParams(vmem_limit_bytes=16 * 2**20),
        name="smooth",
    )(place, earlier, own, low, high)


def windows(weights, shifts, bands):
    band_rows = weights.shape[1]
    rows_i = jnp.arange(band_rows, dtype=jnp.int32)[:, None]
    rows_j = jnp.arange(band_rows, dtype=jnp.int32)[None, :]
    placer = ((rows_i == rows_j + shifts[0, 0]) & (rows_j < bands[0, 0])).astype(jnp.float32)
    return jnp.sum(placer[None, :, :, None] * weights[:, None, :, :], axis=2)


def per_device(weights, shifts, bands, volume, measured):
    layers, height, columns = volume.shape
    own_rows = measured.shape[1]
    ring = lax.axis_size("ang") // 2
    depth = height // ring
    slab = lax.axis_index("slab")
    last_slab = lax.axis_size("slab") - 1
    place = jnp.stack(
        [lax.axis_index("ang") // 2, slab > 0, slab < last_slab]
    ).astype(jnp.int32)

    window = windows(weights, shifts, bands)
    low, high = window[:, :own_rows], window[:, own_rows:]
    count = window.shape[0] * own_rows
    flat = lambda block: block.reshape(count, layers)
    line = jnp.pad(window.reshape(1, -1), ((0, TILE - 1), (0, columns - window.size)))
    back = pack(flat(low), line, volume, measured)
    following = from_behind(back, "slab", -1)
    window_before = from_behind(window, "slab", 1)
    piece = piece_of(place, volume, back, depth)
    before = to_next(piece)
    window_after = following[-TILE, : window.size].reshape(window.shape)

    low_after, high_before = window_after[:, :own_rows], window_before[:, own_rows:]
    total_own = jnp.sum(low, axis=2) + jnp.sum(high_before, axis=2)
    total_next = jnp.sum(low_after, axis=2) + jnp.sum(high, axis=2)
    share_own = 1.0 / jnp.maximum(total_own, 1.0)
    share_next = jnp.where(slab < last_slab, 1.0 / jnp.maximum(total_next, 1.0), 0.0)
    coefs_own = flat(low) * share_own.reshape(count, 1)
    coefs_next = flat(high) * share_next.reshape(count, 1)
    back_coefs = jnp.concatenate([coefs_own, coefs_next])
    normal_before = jnp.sum(coefs_own[:, :, None] * flat(high_before)[:, None, :], axis=0)
    normal_own = jnp.sum(coefs_next[:, :, None] * flat(high)[:, None, :], axis=0)
    column_part = jnp.sum(window, axis=(0, 1))
    sums = jnp.concatenate([normal_before, normal_own, column_part[:, None]], axis=1)
    sums = jnp.pad(sums, ((0, TILE - layers), (0, LANES - 2 * layers - 1)))

    sent = spread(back_coefs, sums, back, following, before, height, ring)
    near = gather(over_ring(sent))
    pieces = update(near, from_far(near), before, piece, ring)
    field = over_ring(pieces)
    volume_before = to_next(late(volume, pieces))
    residual, done = residual_of(flat(high_before), volume_before, back, measured.shape)
    halo_low = to_next(field[:, layers - HALO :])
    halo_high = to_previous(field[:, :HALO])
    updated = smooth(place, done, field, halo_low, halo_high)
    return (updated, residual)


def solution(mesh):
    return jax.shard_map(
        per_device,
        mesh=mesh,
        in_specs=(
            P("ang", None, "slab"),
            P("ang", "slab"),
            P("ang", "slab"),
            P("slab", None, None),
            P("ang", "slab", None, None),
        ),
        out_specs=(P("slab", None, None), P("ang", "slab", None, None)),
        check_vma=False,
    )
```

```python
import jax
import jax.numpy as jnp
from jax import lax
from jax.experimental import pallas as pl
from jax.experimental.pallas import tpu as pltpu
from jax.sharding import PartitionSpec as P

TILE = 8
LANES = 128
HALO = 2


def from_behind(block, axis, distance):
    devices = range(lax.axis_size(axis))
    route = [(i - distance, i) for i in devices if i - distance in devices]
    return lax.ppermute(block, axis, route)


def ring_groups():
    count = lax.axis_size("ang")
    return [list(range(0, count, 2)), list(range(1, count, 2))]


def over_ring(pieces):
    return lax.all_to_all(
        pieces, "ang", split_axis=0, concat_axis=0, axis_index_groups=ring_groups()
    )


ROW = 16


def route(pairs):
    count, slabs = lax.axis_size("ang"), lax.axis_size("slab")
    return [
        (a * slabs + s, (a if s // ROW == t // ROW else a ^ 1) * slabs + t)
        for a in range(count)
        for s, t in pairs
        if 0 <= t < slabs
    ]


def from_far(block):
    return lax.ppermute(block, "ang", [(a, a ^ 1) for a in range(lax.axis_size("ang"))])


def to_next(block):
    pairs = [(s, s + 1) for s in range(lax.axis_size("slab"))]
    return lax.ppermute(block, ("ang", "slab"), route(pairs))


def over_ring(pieces):
    return lax.all_to_all(
        pieces, "ang", split_axis=0, concat_axis=0, axis_index_groups=ring_groups()
    )


ROW = 16


def route(pairs):
    count, slabs = lax.axis_size("ang"), lax.axis_size("slab")
    return [
        (a * slabs + s, (a if s // ROW == t // ROW else a ^ 1) * slabs + t)
        for a in range(count)
        for s, t in pairs
        if 0 <= t < slabs
    ]


def from_far(block):
    return lax.ppermute(block, "ang", [(a, a ^ 1) for a in range(lax.axis_size("ang"))])


def within_chip(block):
    return lax.ppermute(block, "slab", [(s, s ^ 1) for s in range(lax.axis_size("slab"))])


def across_chips(block):
    pairs = [(s, s + 1 if s % 2 else s - 1) for s in range(lax.axis_size("slab"))]
    return lax.ppermute(block, ("ang", "slab"), route(pairs))


def to_next(block):
    pairs = [(s, s + 1) for s in range(lax.axis_size("slab"))]
    return lax.ppermute(block, ("ang", "slab"), route(pairs))


def to_previous(block):
    pairs = [(s, s - 1) for s in range(lax.axis_size("slab"))]
    return lax.ppermute(block, ("ang", "slab"), route(pairs))


VMEM = pl.BlockSpec(memory_space=pltpu.VMEM)
SMEM = pl.BlockSpec(memory_space=pltpu.SMEM)
ANY = pl.BlockSpec(memory_space=pl.ANY)


def splats(ref):
    rows, columns = ref.shape
    return [[jnp.full((TILE, LANES), ref[k, z]) for z in range(columns)] for k in range(rows)]


def combine(planes, coefs):
    total = planes[0] * coefs[0]
    for plane, coef in zip(planes[1:], coefs[1:]):
        total = total + plane * coef
    return total


def pack_kernel(coef_ref, window_ref, volume_ref, measured_ref, out_ref):
    angles, rows, height, columns = measured_ref.shape
    layers = volume_ref.shape[0]
    depth = 2 * TILE
    coefs = splats(coef_ref)
    out_ref[angles * rows * height :, :] = window_ref[...]

    def chunk(i, carry):
        top = pl.multiple_of(i * depth, depth)
        for t in range(columns // LANES):
            lanes = pl.ds(t * LANES, LANES)
            planes = [volume_ref[z, pl.ds(top, depth), lanes] for z in range(layers)]
            for a in range(angles):
                for r in range(rows):
                    k = a * rows + r
                    value = measured_ref[a, r, pl.ds(top, depth), lanes].astype(jnp.float32)
                    for j in range(depth // TILE):
                        tile = slice(j * TILE, (j + 1) * TILE)
                        row = pl.multiple_of(k * height + top + j * TILE, TILE)
                        out_ref[pl.ds(row, TILE), lanes] = value[tile] - combine(
                            [plane[tile] for plane in planes], coefs[k]
                        )
        return carry

    lax.fori_loop(0, height // depth, chunk, 0)


def pack(coefs, window, volume, measured):
    angles, rows, height, columns = measured.shape
    return pl.pallas_call(
        pack_kernel,
        in_specs=[SMEM, VMEM, VMEM, VMEM],
        out_specs=VMEM,
        out_shape=jax.ShapeDtypeStruct((angles * rows * height + TILE, columns), jnp.float32),
        compiler_params=pltpu.CompilerParams(vmem_limit_bytes=8 * 2**20),
        name="pack",
    )(coefs, window, volume, measured)


def spread_kernel(coef_ref, sums_ref, own_ref, next_ref, earlier_ref, out_ref):
    count, layers = coef_ref.shape
    ring = out_ref.shape[0]
    columns = own_ref.shape[1]
    height = (own_ref.shape[0] - TILE) // (count // 2)
    depth = height // ring
    ytiles, xtiles = depth // TILE, columns // LANES
    coefs = splats(coef_ref)
    body = layers * ytiles * xtiles * TILE

    def chunk(i, carry):
        top = i * depth
        for t in range(xtiles):
            lanes = pl.ds(t * LANES, LANES)
            for j in range(ytiles):
                planes = [
                    ref[pl.ds(pl.multiple_of(k * height + top + j * TILE, TILE), TILE), lanes]
                    for ref in (own_ref, next_ref)
                    for k in range(count // 2)
                ]
                for z in range(layers):
                    row = ((z * ytiles + j) * xtiles + t) * TILE
                    out_ref[i, row : row + TILE, :] = combine(planes, [c[z] for c in coefs])
        out_ref[i, body : body + TILE, :] = sums_ref[...]
        return carry

    lax.fori_loop(0, ring, chunk, 0)


def spread(coefs, sums, own, following, earlier, height, ring):
    layers, columns = coefs.shape[1], own.shape[1]
    length = layers * (height // ring) * columns // LANES + TILE
    return pl.pallas_call(
        spread_kernel,
        in_specs=[SMEM, VMEM, VMEM, VMEM, ANY],
        out_specs=VMEM,
        out_shape=jax.ShapeDtypeStruct((ring, length, LANES), jnp.float32),
        compiler_params=pltpu.CompilerParams(vmem_limit_bytes=8 * 2**20),
        name="spread",
    )(coefs, sums, own, following, earlier)


def gather_kernel(parts_ref, mine_ref):
    ring, length, _ = parts_ref.shape
    step = next(n for n in (5 * TILE, 3 * TILE, TILE) if length % n == 0)

    def add(i, carry):
        rows = pl.ds(pl.multiple_of(i * step, TILE), step)
        total = parts_ref[0, rows, :]
        for part in range(1, ring):
            total = total + parts_ref[part, rows, :]
        mine_ref[rows, :] = total
        return carry

    lax.fori_loop(0, length // step, add, 0)


def gather(parts):
    return pl.pallas_call(
        gather_kernel,
        in_specs=[VMEM],
        out_specs=VMEM,
        out_shape=jax.ShapeDtypeStruct(parts.shape[1:], jnp.float32),
        compiler_params=pltpu.CompilerParams(vmem_limit_bytes=8 * 2**20),
        name="gather",
    )(parts)


def piece_kernel(place_ref, volume_ref, earlier_ref, out_ref):
    layers, depth, _ = out_ref.shape
    top = pl.multiple_of(place_ref[0] * depth, depth)
    for z in range(layers):
        out_ref[z] = volume_ref[z, pl.ds(top, depth), :]


def piece_of(place, volume, earlier, depth):
    layers, _, columns = volume.shape
    return pl.pallas_call(
        piece_kernel,
        in_specs=[SMEM, VMEM, ANY],
        out_specs=VMEM,
        out_shape=jax.ShapeDtypeStruct((layers, depth, columns), jnp.float32),
        compiler_params=pltpu.CompilerParams(vmem_limit_bytes=8 * 2**20),
        cost_estimate=pl.CostEstimate(flops=0, bytes_accessed=32 * 2**20, transcendentals=0),
        name="piece",
    )(place, volume, earlier)


def late_kernel(volume_ref, earlier_ref, whole_ref):
    for z in range(volume_ref.shape[0]):
        whole_ref[z] = volume_ref[z]


def late(volume, earlier):
    return pl.pallas_call(
        late_kernel,
        in_specs=[VMEM, ANY],
        out_specs=VMEM,
        out_shape=jax.ShapeDtypeStruct(volume.shape, jnp.float32),
        compiler_params=pltpu.CompilerParams(vmem_limit_bytes=8 * 2**20),
        cost_estimate=pl.CostEstimate(flops=0, bytes_accessed=32 * 2**20, transcendentals=0),
        name="late",
    )(volume, earlier)


def residual_kernel(coef_ref, before_ref, own_ref, earlier_ref, out_ref, done_ref):
    done_ref[...] = jnp.zeros_like(done_ref)
    angles, rows, height, columns = out_ref.shape
    layers = before_ref.shape[0]
    depth = 2 * TILE
    coefs = [[coef_ref[k, z] for z in range(layers)] for k in range(angles * rows)]

    def chunk(i, carry):
        top = pl.multiple_of(i * depth, depth)
        for t in range(columns // LANES):
            lanes = pl.ds(t * LANES, LANES)
            planes = [before_ref[z, pl.ds(top, depth), lanes] for z in range(layers)]
            for a in range(angles):
                for r in range(rows):
                    k = a * rows + r
                    total = planes[0] * coefs[k][0]
                    for z in range(1, layers):
                        total = total + planes[z] * coefs[k][z]
                    row = pl.multiple_of(k * height + top, depth)
                    out_ref[a, r, pl.ds(top, depth), lanes] = (
                        own_ref[pl.ds(row, depth), lanes] - total
                    )
        return carry

    lax.fori_loop(0, height // depth, chunk, 0)


def residual_of(coefs, before, own, earlier, shape):
    return pl.pallas_call(
        residual_kernel,
        in_specs=[SMEM, VMEM, VMEM, ANY],
        out_specs=[VMEM, VMEM],
        out_shape=[
            jax.ShapeDtypeStruct(shape, jnp.float32),
            jax.ShapeDtypeStruct((TILE, LANES), jnp.float32),
        ],
        compiler_params=pltpu.CompilerParams(vmem_limit_bytes=8 * 2**20),
        cost_estimate=pl.CostEstimate(flops=0, bytes_accessed=16 * 2**20, transcendentals=0),
        name="residual",
    )(coefs, before, own, earlier)


def update_kernel(near_ref, far_ref, before_ref, piece_ref, out_ref):
    copies, layers, depth, columns = out_ref.shape
    ytiles, xtiles = depth // TILE, columns // LANES
    body = layers * ytiles * xtiles * TILE
    sums = near_ref[body:, :] + far_ref[body:, :]
    share = 1.0 / sums[:, 2 * layers : 2 * layers + 1]
    sums = sums * share

    def splat(value):
        return jnp.broadcast_to(value, (TILE, LANES))

    shares = [splat(share[z : z + 1, :]) for z in range(layers)]
    coefs = [
        [splat(sums[z : z + 1, k : k + 1]) for k in range(2 * layers)] for z in range(layers)
    ]
    for t in range(xtiles):
        lanes = pl.ds(t * LANES, LANES)
        for j in range(ytiles):
            rows = pl.ds(j * TILE, TILE)
            planes = [ref[z, rows, lanes] for ref in (before_ref, piece_ref) for z in range(layers)]
            for z in range(layers):
                row = ((z * ytiles + j) * xtiles + t) * TILE
                total = (near_ref[row : row + TILE, :] + far_ref[row : row + TILE, :]) * shares[z]
                value = planes[layers + z] + (total - combine(planes, coefs[z]))
                for copy in range(copies):
                    out_ref[copy, z, rows, lanes] = value


def update(near, far, before, piece, ring):
    return pl.pallas_call(
        update_kernel,
        in_specs=[VMEM] * 4,
        out_specs=VMEM,
        out_shape=jax.ShapeDtypeStruct((ring,) + piece.shape, jnp.float32),
        compiler_params=pltpu.CompilerParams(vmem_limit_bytes=8 * 2**20),
        name="update",
    )(near, far, before, piece)


def sweep(source, target, edge, lowest, highest):
    tall, columns = source.shape[1:]
    height = tall - TILE
    xtiles = columns // LANES
    lane = lax.broadcasted_iota(jnp.int32, (TILE, LANES), 1)
    level = lax.broadcasted_iota(jnp.int32, (TILE, LANES), 0)
    last_lane, first_lane = lane == LANES - 1, lane == 0
    last_row, first_row = level == TILE - 1, level == 0
    spans = [pl.ds(t * LANES, LANES) for t in range(xtiles)]
    for z in range(lowest, highest + 1):
        edge[z, :, :] = jnp.zeros((TILE, columns), jnp.float32)

    def band(i, carry):
        top = pl.multiple_of(i * TILE, TILE)
        rows = pl.ds(top, TILE)
        below = pl.ds(top + TILE, 1)
        upper = [source[lowest - 1, rows, span] for span in spans]
        flow_z = None
        for z in range(lowest - 1, highest + 1):
            base, upper = upper, [source[z + 1, rows, span] for span in spans]
            turned = [pltpu.roll(b, LANES - 1, 1) for b in base]
            grad_z, along, scaled = [], [], []
            for t in range(xtiles):
                rise = upper[t] - base[t]
                nearby = jnp.where(
                    last_row,
                    jnp.broadcast_to(source[z, below, spans[t]], (TILE, LANES)),
                    pltpu.roll(base[t], TILE - 1, 0),
                )
                down = nearby - base[t]
                right = jnp.where(
                    last_lane, turned[t + 1] if t + 1 < xtiles else base[t], turned[t]
                )
                across = right - base[t]
                scale = lax.rsqrt(rise * rise + down * down + across * across + 0.01)
                grad_z.append(rise * scale)
                along.append(down * scale)
                scaled.append(across * scale)
            if z >= lowest:
                moved = [pltpu.roll(p, 1, 1) for p in scaled]
                for t in range(xtiles):
                    left = jnp.where(first_lane, moved[t - 1] if t else 0.0, moved[t])
                    above = jnp.where(
                        first_row,
                        jnp.broadcast_to(edge[z, TILE - 1 : TILE, spans[t]], (TILE, LANES)),
                        pltpu.roll(along[t], 1, 0),
                    )
                    edge[z, :, spans[t]] = along[t]
                    div = (grad_z[t] - flow_z[t]) + (along[t] - above) + (scaled[t] - left)
                    target(z, rows, spans[t], base[t] + 0.05 * div)
            flow_z = grad_z
        return carry

    lax.fori_loop(0, height // TILE, band, 0)


def smooth_kernel(place_ref, earlier_ref, own_ref, low_ref, high_ref, out_ref, field, middle, edge):
    ring, layers, depth, columns = own_ref.shape
    height = ring * depth
    keep_low = place_ref[1].astype(jnp.float32)
    keep_high = place_ref[2].astype(jnp.float32)

    def fill(i, carry):
        top = pl.multiple_of(i * depth, depth)
        for z in range(HALO):
            field[z, pl.ds(top, depth), :] = low_ref[i, z]
            field[HALO + layers + z, pl.ds(top, depth), :] = high_ref[i, z]
        for z in range(layers):
            field[HALO + z, pl.ds(top, depth), :] = own_ref[i, z]
        return carry

    lax.fori_loop(0, ring, fill, 0)
    for z in range(layers + 2 * HALO):
        field[z, height : height + 1, :] = field[z, height - 1 : height, :]

    def keep(z, rows, span, value):
        if z == HALO - 1:
            value = value * keep_low
        if z == HALO + layers:
            value = value * keep_high
        middle[z, rows, span] = value

    def finish(z, rows, span, value):
        out_ref[z - HALO, rows, span] = value

    sweep(field, keep, edge, HALO - 1, HALO + layers)
    for z in range(HALO - 1, HALO + layers + 1):
        middle[z, height : height + 1, :] = middle[z, height - 1 : height, :]
    sweep(middle, finish, edge, HALO, HALO + layers - 1)


def smooth(place, earlier, own, low, high):
    ring, layers, depth, columns = own.shape
    deep, height = layers + 2 * HALO, ring * depth
    return pl.pallas_call(
        smooth_kernel,
        in_specs=[SMEM, ANY, VMEM, VMEM, VMEM],
        out_specs=VMEM,
        out_shape=jax.ShapeDtypeStruct((layers, height, columns), jnp.float32),
        scratch_shapes=[
            pltpu.VMEM((deep, height + TILE, columns), jnp.float32),
            pltpu.VMEM((deep, height + TILE, columns), jnp.float32),
            pltpu.VMEM((deep, TILE, columns), jnp.float32),
        ],
        compiler_params=pltpu.CompilerParams(vmem_limit_bytes=16 * 2**20),
        name="smooth",
    )(place, earlier, own, low, high)


def windows(weights, shifts, bands):
    band_rows = weights.shape[1]
    rows_i = jnp.arange(band_rows, dtype=jnp.int32)[:, None]
    rows_j = jnp.arange(band_rows, dtype=jnp.int32)[None, :]
    placer = ((rows_i == rows_j + shifts[0, 0]) & (rows_j < bands[0, 0])).astype(jnp.float32)
    return jnp.sum(placer[None, :, :, None] * weights[:, None, :, :], axis=2)


def per_device(weights, shifts, bands, volume, measured):
    layers, height, columns = volume.shape
    own_rows = measured.shape[1]
    ring = lax.axis_size("ang") // 2
    depth = height // ring
    slab = lax.axis_index("slab")
    last_slab = lax.axis_size("slab") - 1
    place = jnp.stack(
        [lax.axis_index("ang") // 2, slab > 0, slab < last_slab]
    ).astype(jnp.int32)

    window = windows(weights, shifts, bands)
    low, high = window[:, :own_rows], window[:, own_rows:]
    count = window.shape[0] * own_rows
    flat = lambda block: block.reshape(count, layers)
    line = jnp.pad(window.reshape(1, -1), ((0, TILE - 1), (0, columns - window.size)))
    back = pack(flat(low), line, volume, measured)
    following = from_behind(back, "slab", -1)
    window_before = from_behind(window, "slab", 1)
    piece = piece_of(place, volume, back, depth)
    before = to_next(piece)
    window_after = following[-TILE, : window.size].reshape(window.shape)

    low_after, high_before = window_after[:, :own_rows], window_before[:, own_rows:]
    total_own = jnp.sum(low, axis=2) + jnp.sum(high_before, axis=2)
    total_next = jnp.sum(low_after, axis=2) + jnp.sum(high, axis=2)
    share_own = 1.0 / jnp.maximum(total_own, 1.0)
    share_next = jnp.where(slab < last_slab, 1.0 / jnp.maximum(total_next, 1.0), 0.0)
    coefs_own = flat(low) * share_own.reshape(count, 1)
    coefs_next = flat(high) * share_next.reshape(count, 1)
    back_coefs = jnp.concatenate([coefs_own, coefs_next])
    normal_before = jnp.sum(coefs_own[:, :, None] * flat(high_before)[:, None, :], axis=0)
    normal_own = jnp.sum(coefs_next[:, :, None] * flat(high)[:, None, :], axis=0)
    column_part = jnp.sum(window, axis=(0, 1))
    sums = jnp.concatenate([normal_before, normal_own, column_part[:, None]], axis=1)
    sums = jnp.pad(sums, ((0, TILE - layers), (0, LANES - 2 * layers - 1)))

    sent = spread(back_coefs, sums, back, following, before, height, ring)
    volume_before = to_next(late(volume, sent))
    near = gather(over_ring(sent))
    pieces = update(near, from_far(near), before, piece, ring)
    field = over_ring(pieces)
    residual, done = residual_of(
        flat(high_before), volume_before, back, pieces, measured.shape
    )
    halo_low = to_next(field[:, layers - HALO :])
    halo_high = to_previous(field[:, :HALO])
    updated = smooth(place, done, field, halo_low, halo_high)
    return (updated, residual)


def solution(mesh):
    return jax.shard_map(
        per_device,
        mesh=mesh,
        in_specs=(
            P("ang", None, "slab"),
            P("ang", "slab"),
            P("ang", "slab"),
            P("slab", None, None),
            P("ang", "slab", None, None),
        ),
        out_specs=(P("slab", None, None), P("ang", "slab", None, None)),
        check_vma=False,
    )
```

```python
import jax
import jax.numpy as jnp
from jax import lax
from jax.experimental import pallas as pl
from jax.experimental.pallas import tpu as pltpu
from jax.sharding import PartitionSpec as P

TILE = 8
LANES = 128
HALO = 2


def from_behind(block, axis, distance):
    devices = range(lax.axis_size(axis))
    route = [(i - distance, i) for i in devices if i - distance in devices]
    return lax.ppermute(block, axis, route)


def ring_groups():
    count = lax.axis_size("ang")
    return [list(range(0, count, 2)), list(range(1, count, 2))]


def over_ring(pieces):
    return lax.all_to_all(
        pieces, "ang", split_axis=0, concat_axis=0, axis_index_groups=ring_groups()
    )


ROW = 16


def route(pairs):
    count, slabs = lax.axis_size("ang"), lax.axis_size("slab")
    return [
        (a * slabs + s, (a if s // ROW == t // ROW else a ^ 1) * slabs + t)
        for a in range(count)
        for s, t in pairs
        if 0 <= t < slabs
    ]


def from_far(block):
    return lax.ppermute(block, "ang", [(a, a ^ 1) for a in range(lax.axis_size("ang"))])


def to_next(block):
    pairs = [(s, s + 1) for s in range(lax.axis_size("slab"))]
    return lax.ppermute(block, ("ang", "slab"), route(pairs))


def over_ring(pieces):
    return lax.all_to_all(
        pieces, "ang", split_axis=0, concat_axis=0, axis_index_groups=ring_groups()
    )


ROW = 16


def route(pairs):
    count, slabs = lax.axis_size("ang"), lax.axis_size("slab")
    return [
        (a * slabs + s, (a if s // ROW == t // ROW else a ^ 1) * slabs + t)
        for a in range(count)
        for s, t in pairs
        if 0 <= t < slabs
    ]


def from_far(block):
    return lax.ppermute(block, "ang", [(a, a ^ 1) for a in range(lax.axis_size("ang"))])


def within_chip(block):
    return lax.ppermute(block, "slab", [(s, s ^ 1) for s in range(lax.axis_size("slab"))])


def across_chips(block):
    pairs = [(s, s + 1 if s % 2 else s - 1) for s in range(lax.axis_size("slab"))]
    return lax.ppermute(block, ("ang", "slab"), route(pairs))


def to_next(block):
    pairs = [(s, s + 1) for s in range(lax.axis_size("slab"))]
    return lax.ppermute(block, ("ang", "slab"), route(pairs))


def to_previous(block):
    pairs = [(s, s - 1) for s in range(lax.axis_size("slab"))]
    return lax.ppermute(block, ("ang", "slab"), route(pairs))


VMEM = pl.BlockSpec(memory_space=pltpu.VMEM)
SMEM = pl.BlockSpec(memory_space=pltpu.SMEM)
ANY = pl.BlockSpec(memory_space=pl.ANY)


def splats(ref):
    rows, columns = ref.shape
    return [[jnp.full((TILE, LANES), ref[k, z]) for z in range(columns)] for k in range(rows)]


def combine(planes, coefs):
    total = planes[0] * coefs[0]
    for plane, coef in zip(planes[1:], coefs[1:]):
        total = total + plane * coef
    return total


def pack_kernel(coef_ref, volume_ref, measured_ref, out_ref):
    angles, rows, height, columns = measured_ref.shape
    layers = volume_ref.shape[0]
    depth = 2 * TILE
    coefs = splats(coef_ref)

    def chunk(i, carry):
        top = pl.multiple_of(i * depth, depth)
        for t in range(columns // LANES):
            lanes = pl.ds(t * LANES, LANES)
            planes = [volume_ref[z, pl.ds(top, depth), lanes] for z in range(layers)]
            for a in range(angles):
                for r in range(rows):
                    k = a * rows + r
                    value = measured_ref[a, r, pl.ds(top, depth), lanes].astype(jnp.float32)
                    for j in range(depth // TILE):
                        tile = slice(j * TILE, (j + 1) * TILE)
                        row = pl.multiple_of(k * height + top + j * TILE, TILE)
                        out_ref[pl.ds(row, TILE), lanes] = value[tile] - combine(
                            [plane[tile] for plane in planes], coefs[k]
                        )
        return carry

    lax.fori_loop(0, height // depth, chunk, 0)


def pack(coefs, volume, measured):
    angles, rows, height, columns = measured.shape
    return pl.pallas_call(
        pack_kernel,
        in_specs=[SMEM, VMEM, VMEM],
        out_specs=VMEM,
        out_shape=jax.ShapeDtypeStruct((angles * rows * height, columns), jnp.float32),
        compiler_params=pltpu.CompilerParams(vmem_limit_bytes=8 * 2**20),
        name="pack",
    )(coefs, volume, measured)


def spread_kernel(coef_ref, sums_ref, own_ref, next_ref, earlier_ref, out_ref):
    count, layers = coef_ref.shape
    ring = out_ref.shape[0]
    columns = own_ref.shape[1]
    height = own_ref.shape[0] // (count // 2)
    depth = height // ring
    ytiles, xtiles = depth // TILE, columns // LANES
    coefs = splats(coef_ref)
    body = layers * ytiles * xtiles * TILE

    def chunk(i, carry):
        top = i * depth
        for t in range(xtiles):
            lanes = pl.ds(t * LANES, LANES)
            for j in range(ytiles):
                planes = [
                    ref[pl.ds(pl.multiple_of(k * height + top + j * TILE, TILE), TILE), lanes]
                    for ref in (own_ref, next_ref)
                    for k in range(count // 2)
                ]
                for z in range(layers):
                    row = ((z * ytiles + j) * xtiles + t) * TILE
                    out_ref[i, row : row + TILE, :] = combine(planes, [c[z] for c in coefs])
        out_ref[i, body : body + TILE, :] = sums_ref[...]
        return carry

    lax.fori_loop(0, ring, chunk, 0)


def spread(coefs, sums, own, following, earlier, height, ring):
    layers, columns = coefs.shape[1], own.shape[1]
    length = layers * (height // ring) * columns // LANES + TILE
    return pl.pallas_call(
        spread_kernel,
        in_specs=[SMEM, VMEM, VMEM, VMEM, ANY],
        out_specs=VMEM,
        out_shape=jax.ShapeDtypeStruct((ring, length, LANES), jnp.float32),
        compiler_params=pltpu.CompilerParams(vmem_limit_bytes=8 * 2**20),
        name="spread",
    )(coefs, sums, own, following, earlier)


def gather_kernel(parts_ref, mine_ref):
    ring, length, _ = parts_ref.shape
    step = next(n for n in (5 * TILE, 3 * TILE, TILE) if length % n == 0)

    def add(i, carry):
        rows = pl.ds(pl.multiple_of(i * step, TILE), step)
        total = parts_ref[0, rows, :]
        for part in range(1, ring):
            total = total + parts_ref[part, rows, :]
        mine_ref[rows, :] = total
        return carry

    lax.fori_loop(0, length // step, add, 0)


def gather(parts):
    return pl.pallas_call(
        gather_kernel,
        in_specs=[VMEM],
        out_specs=VMEM,
        out_shape=jax.ShapeDtypeStruct(parts.shape[1:], jnp.float32),
        compiler_params=pltpu.CompilerParams(vmem_limit_bytes=8 * 2**20),
        name="gather",
    )(parts)


def late_kernel(volume_ref, earlier_ref, whole_ref):
    for z in range(volume_ref.shape[0]):
        whole_ref[z] = volume_ref[z]


def late(volume, earlier):
    return pl.pallas_call(
        late_kernel,
        in_specs=[VMEM, ANY],
        out_specs=VMEM,
        out_shape=jax.ShapeDtypeStruct(volume.shape, jnp.float32),
        compiler_params=pltpu.CompilerParams(vmem_limit_bytes=8 * 2**20),
        cost_estimate=pl.CostEstimate(flops=0, bytes_accessed=32 * 2**20, transcendentals=0),
        name="late",
    )(volume, earlier)


def residual_kernel(coef_ref, before_ref, own_ref, out_ref, done_ref):
    done_ref[...] = jnp.zeros_like(done_ref)
    angles, rows, height, columns = out_ref.shape
    layers = before_ref.shape[0]
    depth = 2 * TILE
    coefs = [[coef_ref[k, z] for z in range(layers)] for k in range(angles * rows)]

    def chunk(i, carry):
        top = pl.multiple_of(i * depth, depth)
        for t in range(columns // LANES):
            lanes = pl.ds(t * LANES, LANES)
            planes = [before_ref[z, pl.ds(top, depth), lanes] for z in range(layers)]
            for a in range(angles):
                for r in range(rows):
                    k = a * rows + r
                    total = planes[0] * coefs[k][0]
                    for z in range(1, layers):
                        total = total + planes[z] * coefs[k][z]
                    row = pl.multiple_of(k * height + top, depth)
                    out_ref[a, r, pl.ds(top, depth), lanes] = (
                        own_ref[pl.ds(row, depth), lanes] - total
                    )
        return carry

    lax.fori_loop(0, height // depth, chunk, 0)


def residual_of(coefs, before, own, shape):
    return pl.pallas_call(
        residual_kernel,
        in_specs=[SMEM, VMEM, VMEM],
        out_specs=[VMEM, VMEM],
        out_shape=[
            jax.ShapeDtypeStruct(shape, jnp.float32),
            jax.ShapeDtypeStruct((TILE, LANES), jnp.float32),
        ],
        compiler_params=pltpu.CompilerParams(vmem_limit_bytes=8 * 2**20),
        cost_estimate=pl.CostEstimate(flops=0, bytes_accessed=16 * 2**20, transcendentals=0),
        name="residual",
    )(coefs, before, own)


def update_kernel(place_ref, near_ref, far_ref, before_ref, volume_ref, out_ref):
    copies, layers, depth, columns = out_ref.shape
    ytiles, xtiles = depth // TILE, columns // LANES
    body = layers * ytiles * xtiles * TILE
    top = pl.multiple_of(place_ref[0] * depth, depth)
    sums = near_ref[body:, :] + far_ref[body:, :]
    share = 1.0 / sums[:, 2 * layers : 2 * layers + 1]
    sums = sums * share

    def splat(value):
        return jnp.broadcast_to(value, (TILE, LANES))

    shares = [splat(share[z : z + 1, :]) for z in range(layers)]
    coefs = [
        [splat(sums[z : z + 1, k : k + 1]) for k in range(2 * layers)] for z in range(layers)
    ]
    for t in range(xtiles):
        lanes = pl.ds(t * LANES, LANES)
        for j in range(ytiles):
            rows = pl.ds(pl.multiple_of(top + j * TILE, TILE), TILE)
            planes = [ref[z, rows, lanes] for ref in (before_ref, volume_ref) for z in range(layers)]
            for z in range(layers):
                row = ((z * ytiles + j) * xtiles + t) * TILE
                total = (near_ref[row : row + TILE, :] + far_ref[row : row + TILE, :]) * shares[z]
                value = planes[layers + z] + (total - combine(planes, coefs[z]))
                for copy in range(copies):
                    out_ref[copy, z, pl.ds(j * TILE, TILE), lanes] = value


def update(place, near, far, before, volume, ring):
    layers, height, columns = volume.shape
    return pl.pallas_call(
        update_kernel,
        in_specs=[SMEM] + [VMEM] * 4,
        out_specs=VMEM,
        out_shape=jax.ShapeDtypeStruct((ring, layers, height // ring, columns), jnp.float32),
        compiler_params=pltpu.CompilerParams(vmem_limit_bytes=8 * 2**20),
        name="update",
    )(place, near, far, before, volume)


def sweep(source, target, edge, lowest, highest):
    tall, columns = source.shape[1:]
    height = tall - TILE
    xtiles = columns // LANES
    lane = lax.broadcasted_iota(jnp.int32, (TILE, LANES), 1)
    level = lax.broadcasted_iota(jnp.int32, (TILE, LANES), 0)
    last_lane, first_lane = lane == LANES - 1, lane == 0
    last_row, first_row = level == TILE - 1, level == 0
    spans = [pl.ds(t * LANES, LANES) for t in range(xtiles)]
    for z in range(lowest, highest + 1):
        edge[z, :, :] = jnp.zeros((TILE, columns), jnp.float32)

    def band(i, carry):
        top = pl.multiple_of(i * TILE, TILE)
        rows = pl.ds(top, TILE)
        below = pl.ds(top + TILE, 1)
        upper = [source[lowest - 1, rows, span] for span in spans]
        flow_z = None
        for z in range(lowest - 1, highest + 1):
            base, upper = upper, [source[z + 1, rows, span] for span in spans]
            turned = [pltpu.roll(b, LANES - 1, 1) for b in base]
            grad_z, along, scaled = [], [], []
            for t in range(xtiles):
                rise = upper[t] - base[t]
                nearby = jnp.where(
                    last_row,
                    jnp.broadcast_to(source[z, below, spans[t]], (TILE, LANES)),
                    pltpu.roll(base[t], TILE - 1, 0),
                )
                down = nearby - base[t]
                right = jnp.where(
                    last_lane, turned[t + 1] if t + 1 < xtiles else base[t], turned[t]
                )
                across = right - base[t]
                scale = lax.rsqrt(rise * rise + down * down + across * across + 0.01)
                grad_z.append(rise * scale)
                along.append(down * scale)
                scaled.append(across * scale)
            if z >= lowest:
                moved = [pltpu.roll(p, 1, 1) for p in scaled]
                for t in range(xtiles):
                    left = jnp.where(first_lane, moved[t - 1] if t else 0.0, moved[t])
                    above = jnp.where(
                        first_row,
                        jnp.broadcast_to(edge[z, TILE - 1 : TILE, spans[t]], (TILE, LANES)),
                        pltpu.roll(along[t], 1, 0),
                    )
                    edge[z, :, spans[t]] = along[t]
                    div = (grad_z[t] - flow_z[t]) + (along[t] - above) + (scaled[t] - left)
                    target(z, rows, spans[t], base[t] + 0.05 * div)
            flow_z = grad_z
        return carry

    lax.fori_loop(0, height // TILE, band, 0)


def smooth_kernel(place_ref, earlier_ref, own_ref, low_ref, high_ref, out_ref, field, middle, edge):
    ring, layers, depth, columns = own_ref.shape
    height = ring * depth
    keep_low = place_ref[1].astype(jnp.float32)
    keep_high = place_ref[2].astype(jnp.float32)

    def fill(i, carry):
        top = pl.multiple_of(i * depth, depth)
        for z in range(HALO):
            field[z, pl.ds(top, depth), :] = low_ref[i, z]
            field[HALO + layers + z, pl.ds(top, depth), :] = high_ref[i, z]
        for z in range(layers):
            field[HALO + z, pl.ds(top, depth), :] = own_ref[i, z]
        return carry

    lax.fori_loop(0, ring, fill, 0)
    for z in range(layers + 2 * HALO):
        field[z, height : height + 1, :] = field[z, height - 1 : height, :]

    def keep(z, rows, span, value):
        if z == HALO - 1:
            value = value * keep_low
        if z == HALO + layers:
            value = value * keep_high
        middle[z, rows, span] = value

    def finish(z, rows, span, value):
        out_ref[z - HALO, rows, span] = value

    sweep(field, keep, edge, HALO - 1, HALO + layers)
    for z in range(HALO - 1, HALO + layers + 1):
        middle[z, height : height + 1, :] = middle[z, height - 1 : height, :]
    sweep(middle, finish, edge, HALO, HALO + layers - 1)


def smooth(place, earlier, own, low, high):
    ring, layers, depth, columns = own.shape
    deep, height = layers + 2 * HALO, ring * depth
    return pl.pallas_call(
        smooth_kernel,
        in_specs=[SMEM, ANY, VMEM, VMEM, VMEM],
        out_specs=VMEM,
        out_shape=jax.ShapeDtypeStruct((layers, height, columns), jnp.float32),
        scratch_shapes=[
            pltpu.VMEM((deep, height + TILE, columns), jnp.float32),
            pltpu.VMEM((deep, height + TILE, columns), jnp.float32),
            pltpu.VMEM((deep, TILE, columns), jnp.float32),
        ],
        compiler_params=pltpu.CompilerParams(vmem_limit_bytes=16 * 2**20),
        name="smooth",
    )(place, earlier, own, low, high)


def windows(weights, shifts, bands):
    band_rows = weights.shape[1]
    rows_i = jnp.arange(band_rows, dtype=jnp.int32)[:, None]
    rows_j = jnp.arange(band_rows, dtype=jnp.int32)[None, :]
    placer = ((rows_i == rows_j + shifts[0, 0]) & (rows_j < bands[0, 0])).astype(jnp.float32)
    return jnp.sum(placer[None, :, :, None] * weights[:, None, :, :], axis=2)


def per_device(weights, shifts, bands, volume, measured):
    layers, height, columns = volume.shape
    own_rows = measured.shape[1]
    ring = lax.axis_size("ang") // 2
    depth = height // ring
    slab = lax.axis_index("slab")
    last_slab = lax.axis_size("slab") - 1
    place = jnp.stack(
        [lax.axis_index("ang") // 2, slab > 0, slab < last_slab]
    ).astype(jnp.int32)

    window = windows(weights, shifts, bands)
    low = window[:, :own_rows]
    count = window.shape[0] * own_rows
    flat = lambda block: block.reshape(count, layers)
    window_before = from_behind(window, "slab", 1)
    back = pack(flat(low), volume, measured)
    following = to_previous(back)
    before = to_next(late(volume, back))

    high_before = window_before[:, own_rows:]
    total_own = jnp.sum(low, axis=2) + jnp.sum(high_before, axis=2)
    share_own = (1.0 / jnp.maximum(total_own, 1.0)).reshape(count, 1)
    coefs_own = flat(low) * share_own
    arrived = to_previous(
        jnp.concatenate([flat(high_before) * share_own, flat(high_before)], axis=1)
    )
    coefs_next, high_next = arrived[:, :layers], arrived[:, layers:]
    back_coefs = jnp.concatenate([coefs_own, coefs_next])
    normal_before = jnp.sum(coefs_own[:, :, None] * flat(high_before)[:, None, :], axis=0)
    normal_own = jnp.sum(coefs_next[:, :, None] * high_next[:, None, :], axis=0)
    column_part = jnp.sum(window, axis=(0, 1))
    sums = jnp.concatenate([normal_before, normal_own, column_part[:, None]], axis=1)
    sums = jnp.pad(sums, ((0, TILE - layers), (0, LANES - 2 * layers - 1)))

    sent = spread(back_coefs, sums, back, following, before, height, ring)
    near = gather(over_ring(sent))
    field = over_ring(update(place, near, from_far(near), before, volume, ring))
    residual, done = residual_of(flat(high_before), before, back, measured.shape)
    halo_low = to_next(field[:, layers - HALO :])
    halo_high = to_previous(field[:, :HALO])
    updated = smooth(place, done, field, halo_low, halo_high)
    return (updated, residual)


def solution(mesh):
    return jax.shard_map(
        per_device,
        mesh=mesh,
        in_specs=(
            P("ang", None, "slab"),
            P("ang", "slab"),
            P("ang", "slab"),
            P("slab", None, None),
            P("ang", "slab", None, None),
        ),
        out_specs=(P("slab", None, None), P("ang", "slab", None, None)),
        check_vma=False,
    )
```

```python
import jax
import jax.numpy as jnp
from jax import lax
from jax.experimental import pallas as pl
from jax.experimental.pallas import tpu as pltpu
from jax.sharding import PartitionSpec as P

TILE = 8
LANES = 128
HALO = 2


def from_behind(block, axis, distance):
    devices = range(lax.axis_size(axis))
    route = [(i - distance, i) for i in devices if i - distance in devices]
    return lax.ppermute(block, axis, route)


def ring_groups():
    count = lax.axis_size("ang")
    return [list(range(0, count, 2)), list(range(1, count, 2))]


def over_ring(pieces):
    return lax.all_to_all(
        pieces, "ang", split_axis=0, concat_axis=0, axis_index_groups=ring_groups()
    )


ROW = 16


def route(pairs):
    count, slabs = lax.axis_size("ang"), lax.axis_size("slab")
    return [
        (a * slabs + s, (a if s // ROW == t // ROW else a ^ 1) * slabs + t)
        for a in range(count)
        for s, t in pairs
        if 0 <= t < slabs
    ]


def from_far(block):
    return lax.ppermute(block, "ang", [(a, a ^ 1) for a in range(lax.axis_size("ang"))])


def from_far_at_row_ends(block):
    count, slabs = lax.axis_size("ang"), lax.axis_size("slab")
    ends = range(ROW - 1, slabs, ROW)
    pairs = [(a * slabs + t, (a ^ 1) * slabs + t) for a in range(count) for t in ends]
    return lax.ppermute(block, ("ang", "slab"), pairs)


def to_next(block):
    pairs = [(s, s + 1) for s in range(lax.axis_size("slab"))]
    return lax.ppermute(block, ("ang", "slab"), route(pairs))


def over_ring(pieces):
    return lax.all_to_all(
        pieces, "ang", split_axis=0, concat_axis=0, axis_index_groups=ring_groups()
    )


ROW = 16


def route(pairs):
    count, slabs = lax.axis_size("ang"), lax.axis_size("slab")
    return [
        (a * slabs + s, (a if s // ROW == t // ROW else a ^ 1) * slabs + t)
        for a in range(count)
        for s, t in pairs
        if 0 <= t < slabs
    ]


def from_far(block):
    return lax.ppermute(block, "ang", [(a, a ^ 1) for a in range(lax.axis_size("ang"))])


def within_chip(block):
    return lax.ppermute(block, "slab", [(s, s ^ 1) for s in range(lax.axis_size("slab"))])


def across_chips(block):
    pairs = [(s, s + 1 if s % 2 else s - 1) for s in range(lax.axis_size("slab"))]
    return lax.ppermute(block, ("ang", "slab"), route(pairs))


def from_far_at_row_ends(block):
    count, slabs = lax.axis_size("ang"), lax.axis_size("slab")
    ends = range(ROW - 1, slabs, ROW)
    pairs = [(a * slabs + t, (a ^ 1) * slabs + t) for a in range(count) for t in ends]
    return lax.ppermute(block, ("ang", "slab"), pairs)


def to_next(block):
    pairs = [(s, s + 1) for s in range(lax.axis_size("slab"))]
    return lax.ppermute(block, ("ang", "slab"), route(pairs))


def to_previous(block):
    pairs = [(s, s - 1) for s in range(lax.axis_size("slab"))]
    return lax.ppermute(block, ("ang", "slab"), route(pairs))


VMEM = pl.BlockSpec(memory_space=pltpu.VMEM)
SMEM = pl.BlockSpec(memory_space=pltpu.SMEM)
ANY = pl.BlockSpec(memory_space=pl.ANY)


def splats(ref):
    rows, columns = ref.shape
    return [[jnp.full((TILE, LANES), ref[k, z]) for z in range(columns)] for k in range(rows)]


def combine(planes, coefs):
    total = planes[0] * coefs[0]
    for plane, coef in zip(planes[1:], coefs[1:]):
        total = total + plane * coef
    return total


def pack_kernel(coef_ref, window_ref, volume_ref, measured_ref, out_ref):
    angles, rows, height, columns = measured_ref.shape
    layers = volume_ref.shape[0]
    depth = 2 * TILE
    coefs = splats(coef_ref)
    out_ref[angles * rows * height :, :] = window_ref[...]

    def chunk(i, carry):
        top = pl.multiple_of(i * depth, depth)
        for t in range(columns // LANES):
            lanes = pl.ds(t * LANES, LANES)
            planes = [volume_ref[z, pl.ds(top, depth), lanes] for z in range(layers)]
            for a in range(angles):
                for r in range(rows):
                    k = a * rows + r
                    value = measured_ref[a, r, pl.ds(top, depth), lanes].astype(jnp.float32)
                    for j in range(depth // TILE):
                        tile = slice(j * TILE, (j + 1) * TILE)
                        row = pl.multiple_of(k * height + top + j * TILE, TILE)
                        out_ref[pl.ds(row, TILE), lanes] = value[tile] - combine(
                            [plane[tile] for plane in planes], coefs[k]
                        )
        return carry

    lax.fori_loop(0, height // depth, chunk, 0)


def pack(coefs, window, volume, measured):
    angles, rows, height, columns = measured.shape
    return pl.pallas_call(
        pack_kernel,
        in_specs=[SMEM, VMEM, VMEM, VMEM],
        out_specs=VMEM,
        out_shape=jax.ShapeDtypeStruct((angles * rows * height + TILE, columns), jnp.float32),
        compiler_params=pltpu.CompilerParams(vmem_limit_bytes=8 * 2**20),
        name="pack",
    )(coefs, window, volume, measured)


def spread_kernel(coef_ref, sums_ref, own_ref, next_ref, earlier_ref, out_ref):
    count, layers = coef_ref.shape
    ring = out_ref.shape[0]
    columns = own_ref.shape[1]
    height = (own_ref.shape[0] - TILE) // (count // 2)
    depth = height // ring
    ytiles, xtiles = depth // TILE, columns // LANES
    coefs = splats(coef_ref)
    body = layers * ytiles * xtiles * TILE

    def chunk(i, carry):
        top = i * depth
        for t in range(xtiles):
            lanes = pl.ds(t * LANES, LANES)
            for j in range(ytiles):
                planes = [
                    ref[pl.ds(pl.multiple_of(k * height + top + j * TILE, TILE), TILE), lanes]
                    for ref in (own_ref, next_ref)
                    for k in range(count // 2)
                ]
                for z in range(layers):
                    row = ((z * ytiles + j) * xtiles + t) * TILE
                    out_ref[i, row : row + TILE, :] = combine(planes, [c[z] for c in coefs])
        out_ref[i, body : body + TILE, :] = sums_ref[...]
        return carry

    lax.fori_loop(0, ring, chunk, 0)


def spread(coefs, sums, own, following, earlier, height, ring):
    layers, columns = coefs.shape[1], own.shape[1]
    length = layers * (height // ring) * columns // LANES + TILE
    return pl.pallas_call(
        spread_kernel,
        in_specs=[SMEM, VMEM, VMEM, VMEM, ANY],
        out_specs=VMEM,
        out_shape=jax.ShapeDtypeStruct((ring, length, LANES), jnp.float32),
        compiler_params=pltpu.CompilerParams(vmem_limit_bytes=8 * 2**20),
        name="spread",
    )(coefs, sums, own, following, earlier)


def gather_kernel(parts_ref, mine_ref):
    ring, length, _ = parts_ref.shape
    step = next(n for n in (5 * TILE, 3 * TILE, TILE) if length % n == 0)

    def add(i, carry):
        rows = pl.ds(pl.multiple_of(i * step, TILE), step)
        total = parts_ref[0, rows, :]
        for part in range(1, ring):
            total = total + parts_ref[part, rows, :]
        mine_ref[rows, :] = total
        return carry

    lax.fori_loop(0, length // step, add, 0)


def gather(parts):
    return pl.pallas_call(
        gather_kernel,
        in_specs=[VMEM],
        out_specs=VMEM,
        out_shape=jax.ShapeDtypeStruct(parts.shape[1:], jnp.float32),
        compiler_params=pltpu.CompilerParams(vmem_limit_bytes=8 * 2**20),
        name="gather",
    )(parts)


def late_kernel(volume_ref, window_ref, earlier_ref, whole_ref, window_out_ref):
    window_out_ref[...] = window_ref[...]
    for z in range(volume_ref.shape[0]):
        whole_ref[z] = volume_ref[z]


def late(volume, window, earlier):
    return pl.pallas_call(
        late_kernel,
        in_specs=[VMEM, VMEM, ANY],
        out_specs=[VMEM, VMEM],
        out_shape=[
            jax.ShapeDtypeStruct(volume.shape, jnp.float32),
            jax.ShapeDtypeStruct(window.shape, jnp.float32),
        ],
        compiler_params=pltpu.CompilerParams(vmem_limit_bytes=8 * 2**20),
        cost_estimate=pl.CostEstimate(flops=0, bytes_accessed=32 * 2**20, transcendentals=0),
        name="late",
    )(volume, window, earlier)


def residual_kernel(coef_ref, before_ref, own_ref, out_ref, done_ref):
    done_ref[...] = jnp.zeros_like(done_ref)
    angles, rows, height, columns = out_ref.shape
    layers = before_ref.shape[0]
    depth = 2 * TILE
    coefs = [[coef_ref[k, z] for z in range(layers)] for k in range(angles * rows)]

    def chunk(i, carry):
        top = pl.multiple_of(i * depth, depth)
        for t in range(columns // LANES):
            lanes = pl.ds(t * LANES, LANES)
            planes = [before_ref[z, pl.ds(top, depth), lanes] for z in range(layers)]
            for a in range(angles):
                for r in range(rows):
                    k = a * rows + r
                    total = planes[0] * coefs[k][0]
                    for z in range(1, layers):
                        total = total + planes[z] * coefs[k][z]
                    row = pl.multiple_of(k * height + top, depth)
                    out_ref[a, r, pl.ds(top, depth), lanes] = (
                        own_ref[pl.ds(row, depth), lanes] - total
                    )
        return carry

    lax.fori_loop(0, height // depth, chunk, 0)


def residual_of(coefs, before, own, shape):
    return pl.pallas_call(
        residual_kernel,
        in_specs=[SMEM, VMEM, VMEM],
        out_specs=[VMEM, VMEM],
        out_shape=[
            jax.ShapeDtypeStruct(shape, jnp.float32),
            jax.ShapeDtypeStruct((TILE, LANES), jnp.float32),
        ],
        compiler_params=pltpu.CompilerParams(vmem_limit_bytes=8 * 2**20),
        cost_estimate=pl.CostEstimate(flops=0, bytes_accessed=16 * 2**20, transcendentals=0),
        name="residual",
    )(coefs, before, own)


def update_kernel(place_ref, near_ref, far_ref, before_ref, volume_ref, out_ref):
    copies, layers, depth, columns = out_ref.shape
    ytiles, xtiles = depth // TILE, columns // LANES
    body = layers * ytiles * xtiles * TILE
    top = pl.multiple_of(place_ref[0] * depth, depth)
    sums = near_ref[body:, :] + far_ref[body:, :]
    share = 1.0 / sums[:, 2 * layers : 2 * layers + 1]
    sums = sums * share

    def splat(value):
        return jnp.broadcast_to(value, (TILE, LANES))

    shares = [splat(share[z : z + 1, :]) for z in range(layers)]
    coefs = [
        [splat(sums[z : z + 1, k : k + 1]) for k in range(2 * layers)] for z in range(layers)
    ]
    for t in range(xtiles):
        lanes = pl.ds(t * LANES, LANES)
        for j in range(ytiles):
            rows = pl.ds(pl.multiple_of(top + j * TILE, TILE), TILE)
            planes = [ref[z, rows, lanes] for ref in (before_ref, volume_ref) for z in range(layers)]
            for z in range(layers):
                row = ((z * ytiles + j) * xtiles + t) * TILE
                total = (near_ref[row : row + TILE, :] + far_ref[row : row + TILE, :]) * shares[z]
                value = planes[layers + z] + (total - combine(planes, coefs[z]))
                for copy in range(copies):
                    out_ref[copy, z, pl.ds(j * TILE, TILE), lanes] = value


def update(place, near, far, before, volume, ring):
    layers, height, columns = volume.shape
    return pl.pallas_call(
        update_kernel,
        in_specs=[SMEM] + [VMEM] * 4,
        out_specs=VMEM,
        out_shape=jax.ShapeDtypeStruct((ring, layers, height // ring, columns), jnp.float32),
        compiler_params=pltpu.CompilerParams(vmem_limit_bytes=8 * 2**20),
        name="update",
    )(place, near, far, before, volume)


def sweep(source, target, edge, lowest, highest):
    tall, columns = source.shape[1:]
    height = tall - TILE
    xtiles = columns // LANES
    lane = lax.broadcasted_iota(jnp.int32, (TILE, LANES), 1)
    level = lax.broadcasted_iota(jnp.int32, (TILE, LANES), 0)
    last_lane, first_lane = lane == LANES - 1, lane == 0
    last_row, first_row = level == TILE - 1, level == 0
    spans = [pl.ds(t * LANES, LANES) for t in range(xtiles)]
    for z in range(lowest, highest + 1):
        edge[z, :, :] = jnp.zeros((TILE, columns), jnp.float32)

    def band(i, carry):
        top = pl.multiple_of(i * TILE, TILE)
        rows = pl.ds(top, TILE)
        below = pl.ds(top + TILE, 1)
        upper = [source[lowest - 1, rows, span] for span in spans]
        flow_z = None
        for z in range(lowest - 1, highest + 1):
            base, upper = upper, [source[z + 1, rows, span] for span in spans]
            turned = [pltpu.roll(b, LANES - 1, 1) for b in base]
            grad_z, along, scaled = [], [], []
            for t in range(xtiles):
                rise = upper[t] - base[t]
                nearby = jnp.where(
                    last_row,
                    jnp.broadcast_to(source[z, below, spans[t]], (TILE, LANES)),
                    pltpu.roll(base[t], TILE - 1, 0),
                )
                down = nearby - base[t]
                right = jnp.where(
                    last_lane, turned[t + 1] if t + 1 < xtiles else base[t], turned[t]
                )
                across = right - base[t]
                scale = lax.rsqrt(rise * rise + down * down + across * across + 0.01)
                grad_z.append(rise * scale)
                along.append(down * scale)
                scaled.append(across * scale)
            if z >= lowest:
                moved = [pltpu.roll(p, 1, 1) for p in scaled]
                for t in range(xtiles):
                    left = jnp.where(first_lane, moved[t - 1] if t else 0.0, moved[t])
                    above = jnp.where(
                        first_row,
                        jnp.broadcast_to(edge[z, TILE - 1 : TILE, spans[t]], (TILE, LANES)),
                        pltpu.roll(along[t], 1, 0),
                    )
                    edge[z, :, spans[t]] = along[t]
                    div = (grad_z[t] - flow_z[t]) + (along[t] - above) + (scaled[t] - left)
                    target(z, rows, spans[t], base[t] + 0.05 * div)
            flow_z = grad_z
        return carry

    lax.fori_loop(0, height // TILE, band, 0)


def smooth_kernel(place_ref, earlier_ref, own_ref, low_ref, high_ref, out_ref, field, middle, edge):
    ring, layers, depth, columns = own_ref.shape
    height = ring * depth
    keep_low = place_ref[1].astype(jnp.float32)
    keep_high = place_ref[2].astype(jnp.float32)

    def fill(i, carry):
        top = pl.multiple_of(i * depth, depth)
        for z in range(HALO):
            field[z, pl.ds(top, depth), :] = low_ref[i, z]
            field[HALO + layers + z, pl.ds(top, depth), :] = high_ref[i, z]
        for z in range(layers):
            field[HALO + z, pl.ds(top, depth), :] = own_ref[i, z]
        return carry

    lax.fori_loop(0, ring, fill, 0)
    for z in range(layers + 2 * HALO):
        field[z, height : height + 1, :] = field[z, height - 1 : height, :]

    def keep(z, rows, span, value):
        if z == HALO - 1:
            value = value * keep_low
        if z == HALO + layers:
            value = value * keep_high
        middle[z, rows, span] = value

    def finish(z, rows, span, value):
        out_ref[z - HALO, rows, span] = value

    sweep(field, keep, edge, HALO - 1, HALO + layers)
    for z in range(HALO - 1, HALO + layers + 1):
        middle[z, height : height + 1, :] = middle[z, height - 1 : height, :]
    sweep(middle, finish, edge, HALO, HALO + layers - 1)


def smooth(place, earlier, own, low, high):
    ring, layers, depth, columns = own.shape
    deep, height = layers + 2 * HALO, ring * depth
    return pl.pallas_call(
        smooth_kernel,
        in_specs=[SMEM, ANY, VMEM, VMEM, VMEM],
        out_specs=VMEM,
        out_shape=jax.ShapeDtypeStruct((layers, height, columns), jnp.float32),
        scratch_shapes=[
            pltpu.VMEM((deep, height + TILE, columns), jnp.float32),
            pltpu.VMEM((deep, height + TILE, columns), jnp.float32),
            pltpu.VMEM((deep, TILE, columns), jnp.float32),
        ],
        compiler_params=pltpu.CompilerParams(vmem_limit_bytes=16 * 2**20),
        name="smooth",
    )(place, earlier, own, low, high)


def windows(weights, shifts, bands):
    band_rows = weights.shape[1]
    rows_i = jnp.arange(band_rows, dtype=jnp.int32)[:, None]
    rows_j = jnp.arange(band_rows, dtype=jnp.int32)[None, :]
    placer = ((rows_i == rows_j + shifts[0, 0]) & (rows_j < bands[0, 0])).astype(jnp.float32)
    return jnp.sum(placer[None, :, :, None] * weights[:, None, :, :], axis=2)


def per_device(weights, shifts, bands, volume, measured):
    layers, height, columns = volume.shape
    own_rows = measured.shape[1]
    ring = lax.axis_size("ang") // 2
    depth = height // ring
    slab = lax.axis_index("slab")
    last_slab = lax.axis_size("slab") - 1
    place = jnp.stack(
        [lax.axis_index("ang") // 2, slab > 0, slab < last_slab]
    ).astype(jnp.int32)

    window = windows(weights, shifts, bands)
    low = window[:, :own_rows]
    count = window.shape[0] * own_rows
    flat = lambda block: block.reshape(count, layers)
    line = jnp.pad(window.reshape(1, -1), ((0, TILE - 1), (0, columns - window.size)))
    back = pack(flat(low), line, volume, measured)
    following = to_previous(back)
    window_before = from_behind(window, "slab", 1)
    whole, window_late = late(volume, window, back)
    before = to_next(whole)
    other = from_far_at_row_ends(window_late)
    high_next = jnp.where(slab % ROW == ROW - 1, other, window)[:, own_rows:]

    window_after = following[-TILE, : window.size].reshape(window.shape)
    low_after, high_before = window_after[:, :own_rows], window_before[:, own_rows:]
    total_own = jnp.sum(low, axis=2) + jnp.sum(high_before, axis=2)
    total_next = jnp.sum(low_after, axis=2) + jnp.sum(high_next, axis=2)
    share_own = 1.0 / jnp.maximum(total_own, 1.0)
    share_next = jnp.where(slab < last_slab, 1.0 / jnp.maximum(total_next, 1.0), 0.0)
    coefs_own = flat(low) * share_own.reshape(count, 1)
    coefs_next = flat(high_next) * share_next.reshape(count, 1)
    back_coefs = jnp.concatenate([coefs_own, coefs_next])
    normal_before = jnp.sum(coefs_own[:, :, None] * flat(high_before)[:, None, :], axis=0)
    normal_own = jnp.sum(coefs_next[:, :, None] * flat(high_next)[:, None, :], axis=0)
    column_part = jnp.sum(window, axis=(0, 1))
    sums = jnp.concatenate([normal_before, normal_own, column_part[:, None]], axis=1)
    sums = jnp.pad(sums, ((0, TILE - layers), (0, LANES - 2 * layers - 1)))

    sent = spread(back_coefs, sums, back, following, before, height, ring)
    near = gather(over_ring(sent))
    field = over_ring(update(place, near, from_far(near), before, volume, ring))
    residual, done = residual_of(flat(high_before), before, back, measured.shape)
    halo_low = to_next(field[:, layers - HALO :])
    halo_high = to_previous(field[:, :HALO])
    updated = smooth(place, done, field, halo_low, halo_high)
    return (updated, residual)


def solution(mesh):
    return jax.shard_map(
        per_device,
        mesh=mesh,
        in_specs=(
            P("ang", None, "slab"),
            P("ang", "slab"),
            P("ang", "slab"),
            P("slab", None, None),
            P("ang", "slab", None, None),
        ),
        out_specs=(P("slab", None, None), P("ang", "slab", None, None)),
        check_vma=False,
    )
```

```python
import jax
import jax.numpy as jnp
from jax import lax
from jax.experimental import pallas as pl
from jax.experimental.pallas import tpu as pltpu
from jax.sharding import PartitionSpec as P

TILE = 8
LANES = 128
HALO = 2


def from_behind(block, axis, distance):
    devices = range(lax.axis_size(axis))
    route = [(i - distance, i) for i in devices if i - distance in devices]
    return lax.ppermute(block, axis, route)


def ring_groups():
    count = lax.axis_size("ang")
    return [list(range(0, count, 2)), list(range(1, count, 2))]


def over_ring(pieces):
    return lax.all_to_all(
        pieces, "ang", split_axis=0, concat_axis=0, axis_index_groups=ring_groups()
    )


ROW = 16


def route(pairs):
    count, slabs = lax.axis_size("ang"), lax.axis_size("slab")
    return [
        (a * slabs + s, (a if s // ROW == t // ROW else a ^ 1) * slabs + t)
        for a in range(count)
        for s, t in pairs
        if 0 <= t < slabs
    ]


def from_far(block):
    return lax.ppermute(block, "ang", [(a, a ^ 1) for a in range(lax.axis_size("ang"))])


def from_far_at_row_ends(block):
    count, slabs = lax.axis_size("ang"), lax.axis_size("slab")
    ends = range(ROW - 1, slabs, ROW)
    pairs = [(a * slabs + t, (a ^ 1) * slabs + t) for a in range(count) for t in ends]
    return lax.ppermute(block, ("ang", "slab"), pairs)


def to_next(block):
    pairs = [(s, s + 1) for s in range(lax.axis_size("slab"))]
    return lax.ppermute(block, ("ang", "slab"), route(pairs))


def over_ring(pieces):
    return lax.all_to_all(
        pieces, "ang", split_axis=0, concat_axis=0, axis_index_groups=ring_groups()
    )


ROW = 16


def route(pairs):
    count, slabs = lax.axis_size("ang"), lax.axis_size("slab")
    return [
        (a * slabs + s, (a if s // ROW == t // ROW else a ^ 1) * slabs + t)
        for a in range(count)
        for s, t in pairs
        if 0 <= t < slabs
    ]


def from_far(block):
    return lax.ppermute(block, "ang", [(a, a ^ 1) for a in range(lax.axis_size("ang"))])


def within_chip(block):
    return lax.ppermute(block, "slab", [(s, s ^ 1) for s in range(lax.axis_size("slab"))])


def across_chips(block):
    pairs = [(s, s + 1 if s % 2 else s - 1) for s in range(lax.axis_size("slab"))]
    return lax.ppermute(block, ("ang", "slab"), route(pairs))


def from_far_at_row_ends(block):
    count, slabs = lax.axis_size("ang"), lax.axis_size("slab")
    ends = range(ROW - 1, slabs, ROW)
    pairs = [(a * slabs + t, (a ^ 1) * slabs + t) for a in range(count) for t in ends]
    return lax.ppermute(block, ("ang", "slab"), pairs)


def to_next(block):
    pairs = [(s, s + 1) for s in range(lax.axis_size("slab"))]
    return lax.ppermute(block, ("ang", "slab"), route(pairs))


def to_previous(block):
    pairs = [(s, s - 1) for s in range(lax.axis_size("slab"))]
    return lax.ppermute(block, ("ang", "slab"), route(pairs))


VMEM = pl.BlockSpec(memory_space=pltpu.VMEM)
SMEM = pl.BlockSpec(memory_space=pltpu.SMEM)
ANY = pl.BlockSpec(memory_space=pl.ANY)


def splats(ref):
    rows, columns = ref.shape
    return [[jnp.full((TILE, LANES), ref[k, z]) for z in range(columns)] for k in range(rows)]


def combine(planes, coefs):
    total = planes[0] * coefs[0]
    for plane, coef in zip(planes[1:], coefs[1:]):
        total = total + plane * coef
    return total


def pack_kernel(coef_ref, window_ref, volume_ref, measured_ref, out_ref):
    angles, rows, height, columns = measured_ref.shape
    layers = volume_ref.shape[0]
    depth = 2 * TILE
    coefs = splats(coef_ref)
    out_ref[angles * rows * height :, :] = window_ref[...]

    def chunk(i, carry):
        top = pl.multiple_of(i * depth, depth)
        for t in range(columns // LANES):
            lanes = pl.ds(t * LANES, LANES)
            planes = [volume_ref[z, pl.ds(top, depth), lanes] for z in range(layers)]
            for a in range(angles):
                for r in range(rows):
                    k = a * rows + r
                    value = measured_ref[a, r, pl.ds(top, depth), lanes].astype(jnp.float32)
                    for j in range(depth // TILE):
                        tile = slice(j * TILE, (j + 1) * TILE)
                        row = pl.multiple_of(k * height + top + j * TILE, TILE)
                        out_ref[pl.ds(row, TILE), lanes] = value[tile] - combine(
                            [plane[tile] for plane in planes], coefs[k]
                        )
        return carry

    lax.fori_loop(0, height // depth, chunk, 0)


def pack(coefs, window, volume, measured):
    angles, rows, height, columns = measured.shape
    return pl.pallas_call(
        pack_kernel,
        in_specs=[SMEM, VMEM, VMEM, VMEM],
        out_specs=VMEM,
        out_shape=jax.ShapeDtypeStruct((angles * rows * height + TILE, columns), jnp.float32),
        compiler_params=pltpu.CompilerParams(vmem_limit_bytes=8 * 2**20),
        name="pack",
    )(coefs, window, volume, measured)


def spread_kernel(coef_ref, sums_ref, own_ref, next_ref, out_ref):
    count, layers = coef_ref.shape
    ring = out_ref.shape[0]
    columns = own_ref.shape[1]
    height = (own_ref.shape[0] - TILE) // (count // 2)
    depth = height // ring
    ytiles, xtiles = depth // TILE, columns // LANES
    coefs = splats(coef_ref)
    body = layers * ytiles * xtiles * TILE

    def chunk(i, carry):
        top = i * depth
        for t in range(xtiles):
            lanes = pl.ds(t * LANES, LANES)
            for j in range(ytiles):
                planes = [
                    ref[pl.ds(pl.multiple_of(k * height + top + j * TILE, TILE), TILE), lanes]
                    for ref in (own_ref, next_ref)
                    for k in range(count // 2)
                ]
                for z in range(layers):
                    row = ((z * ytiles + j) * xtiles + t) * TILE
                    out_ref[i, row : row + TILE, :] = combine(planes, [c[z] for c in coefs])
        out_ref[i, body : body + TILE, :] = sums_ref[...]
        return carry

    lax.fori_loop(0, ring, chunk, 0)


def spread(coefs, sums, own, following, height, ring):
    layers, columns = coefs.shape[1], own.shape[1]
    length = layers * (height // ring) * columns // LANES + TILE
    return pl.pallas_call(
        spread_kernel,
        in_specs=[SMEM, VMEM, VMEM, VMEM],
        out_specs=VMEM,
        out_shape=jax.ShapeDtypeStruct((ring, length, LANES), jnp.float32),
        compiler_params=pltpu.CompilerParams(vmem_limit_bytes=8 * 2**20),
        name="spread",
    )(coefs, sums, own, following)


def gather_kernel(parts_ref, earlier_ref, mine_ref):
    ring, length, _ = parts_ref.shape
    step = next(n for n in (5 * TILE, 3 * TILE, TILE) if length % n == 0)

    def add(i, carry):
        rows = pl.ds(pl.multiple_of(i * step, TILE), step)
        total = parts_ref[0, rows, :]
        for part in range(1, ring):
            total = total + parts_ref[part, rows, :]
        mine_ref[rows, :] = total
        return carry

    lax.fori_loop(0, length // step, add, 0)


def gather(parts, earlier):
    return pl.pallas_call(
        gather_kernel,
        in_specs=[VMEM, ANY],
        out_specs=VMEM,
        out_shape=jax.ShapeDtypeStruct(parts.shape[1:], jnp.float32),
        compiler_params=pltpu.CompilerParams(vmem_limit_bytes=8 * 2**20),
        name="gather",
    )(parts, earlier)


def late_kernel(volume_ref, window_ref, earlier_ref, whole_ref, window_out_ref):
    window_out_ref[...] = window_ref[...]
    for z in range(volume_ref.shape[0]):
        whole_ref[z] = volume_ref[z]


def late(volume, window, earlier):
    return pl.pallas_call(
        late_kernel,
        in_specs=[VMEM, VMEM, ANY],
        out_specs=[VMEM, VMEM],
        out_shape=[
            jax.ShapeDtypeStruct(volume.shape, jnp.float32),
            jax.ShapeDtypeStruct(window.shape, jnp.float32),
        ],
        compiler_params=pltpu.CompilerParams(vmem_limit_bytes=8 * 2**20),
        cost_estimate=pl.CostEstimate(flops=0, bytes_accessed=32 * 2**20, transcendentals=0),
        name="late",
    )(volume, window, earlier)


def residual_kernel(coef_ref, before_ref, own_ref, out_ref, done_ref):
    done_ref[...] = jnp.zeros_like(done_ref)
    angles, rows, height, columns = out_ref.shape
    layers = before_ref.shape[0]
    depth = 2 * TILE
    coefs = [[coef_ref[k, z] for z in range(layers)] for k in range(angles * rows)]

    def chunk(i, carry):
        top = pl.multiple_of(i * depth, depth)
        for t in range(columns // LANES):
            lanes = pl.ds(t * LANES, LANES)
            planes = [before_ref[z, pl.ds(top, depth), lanes] for z in range(layers)]
            for a in range(angles):
                for r in range(rows):
                    k = a * rows + r
                    total = planes[0] * coefs[k][0]
                    for z in range(1, layers):
                        total = total + planes[z] * coefs[k][z]
                    row = pl.multiple_of(k * height + top, depth)
                    out_ref[a, r, pl.ds(top, depth), lanes] = (
                        own_ref[pl.ds(row, depth), lanes] - total
                    )
        return carry

    lax.fori_loop(0, height // depth, chunk, 0)


def residual_of(coefs, before, own, shape):
    return pl.pallas_call(
        residual_kernel,
        in_specs=[SMEM, VMEM, VMEM],
        out_specs=[VMEM, VMEM],
        out_shape=[
            jax.ShapeDtypeStruct(shape, jnp.float32),
            jax.ShapeDtypeStruct((TILE, LANES), jnp.float32),
        ],
        compiler_params=pltpu.CompilerParams(vmem_limit_bytes=8 * 2**20),
        cost_estimate=pl.CostEstimate(flops=0, bytes_accessed=16 * 2**20, transcendentals=0),
        name="residual",
    )(coefs, before, own)


def update_kernel(place_ref, near_ref, far_ref, before_ref, volume_ref, out_ref):
    copies, layers, depth, columns = out_ref.shape
    ytiles, xtiles = depth // TILE, columns // LANES
    body = layers * ytiles * xtiles * TILE
    top = pl.multiple_of(place_ref[0] * depth, depth)
    sums = near_ref[body:, :] + far_ref[body:, :]
    share = 1.0 / sums[:, 2 * layers : 2 * layers + 1]
    sums = sums * share

    def splat(value):
        return jnp.broadcast_to(value, (TILE, LANES))

    shares = [splat(share[z : z + 1, :]) for z in range(layers)]
    coefs = [
        [splat(sums[z : z + 1, k : k + 1]) for k in range(2 * layers)] for z in range(layers)
    ]
    for t in range(xtiles):
        lanes = pl.ds(t * LANES, LANES)
        for j in range(ytiles):
            rows = pl.ds(pl.multiple_of(top + j * TILE, TILE), TILE)
            planes = [ref[z, rows, lanes] for ref in (before_ref, volume_ref) for z in range(layers)]
            for z in range(layers):
                row = ((z * ytiles + j) * xtiles + t) * TILE
                total = (near_ref[row : row + TILE, :] + far_ref[row : row + TILE, :]) * shares[z]
                value = planes[layers + z] + (total - combine(planes, coefs[z]))
                for copy in range(copies):
                    out_ref[copy, z, pl.ds(j * TILE, TILE), lanes] = value


def update(place, near, far, before, volume, ring):
    layers, height, columns = volume.shape
    return pl.pallas_call(
        update_kernel,
        in_specs=[SMEM] + [VMEM] * 4,
        out_specs=VMEM,
        out_shape=jax.ShapeDtypeStruct((ring, layers, height // ring, columns), jnp.float32),
        compiler_params=pltpu.CompilerParams(vmem_limit_bytes=8 * 2**20),
        name="update",
    )(place, near, far, before, volume)


def sweep(source, target, edge, lowest, highest):
    tall, columns = source.shape[1:]
    height = tall - TILE
    xtiles = columns // LANES
    lane = lax.broadcasted_iota(jnp.int32, (TILE, LANES), 1)
    level = lax.broadcasted_iota(jnp.int32, (TILE, LANES), 0)
    last_lane, first_lane = lane == LANES - 1, lane == 0
    last_row, first_row = level == TILE - 1, level == 0
    spans = [pl.ds(t * LANES, LANES) for t in range(xtiles)]
    for z in range(lowest, highest + 1):
        edge[z, :, :] = jnp.zeros((TILE, columns), jnp.float32)

    def band(i, carry):
        top = pl.multiple_of(i * TILE, TILE)
        rows = pl.ds(top, TILE)
        below = pl.ds(top + TILE, 1)
        upper = [source[lowest - 1, rows, span] for span in spans]
        flow_z = None
        for z in range(lowest - 1, highest + 1):
            base, upper = upper, [source[z + 1, rows, span] for span in spans]
            turned = [pltpu.roll(b, LANES - 1, 1) for b in base]
            grad_z, along, scaled = [], [], []
            for t in range(xtiles):
                rise = upper[t] - base[t]
                nearby = jnp.where(
                    last_row,
                    jnp.broadcast_to(source[z, below, spans[t]], (TILE, LANES)),
                    pltpu.roll(base[t], TILE - 1, 0),
                )
                down = nearby - base[t]
                right = jnp.where(
                    last_lane, turned[t + 1] if t + 1 < xtiles else base[t], turned[t]
                )
                across = right - base[t]
                scale = lax.rsqrt(rise * rise + down * down + across * across + 0.01)
                grad_z.append(rise * scale)
                along.append(down * scale)
                scaled.append(across * scale)
            if z >= lowest:
                moved = [pltpu.roll(p, 1, 1) for p in scaled]
                for t in range(xtiles):
                    left = jnp.where(first_lane, moved[t - 1] if t else 0.0, moved[t])
                    above = jnp.where(
                        first_row,
                        jnp.broadcast_to(edge[z, TILE - 1 : TILE, spans[t]], (TILE, LANES)),
                        pltpu.roll(along[t], 1, 0),
                    )
                    edge[z, :, spans[t]] = along[t]
                    div = (grad_z[t] - flow_z[t]) + (along[t] - above) + (scaled[t] - left)
                    target(z, rows, spans[t], base[t] + 0.05 * div)
            flow_z = grad_z
        return carry

    lax.fori_loop(0, height // TILE, band, 0)


def smooth_kernel(place_ref, earlier_ref, own_ref, low_ref, high_ref, out_ref, field, middle, edge):
    ring, layers, depth, columns = own_ref.shape
    height = ring * depth
    keep_low = place_ref[1].astype(jnp.float32)
    keep_high = place_ref[2].astype(jnp.float32)

    def fill(i, carry):
        top = pl.multiple_of(i * depth, depth)
        for z in range(HALO):
            field[z, pl.ds(top, depth), :] = low_ref[i, z]
            field[HALO + layers + z, pl.ds(top, depth), :] = high_ref[i, z]
        for z in range(layers):
            field[HALO + z, pl.ds(top, depth), :] = own_ref[i, z]
        return carry

    lax.fori_loop(0, ring, fill, 0)
    for z in range(layers + 2 * HALO):
        field[z, height : height + 1, :] = field[z, height - 1 : height, :]

    def keep(z, rows, span, value):
        if z == HALO - 1:
            value = value * keep_low
        if z == HALO + layers:
            value = value * keep_high
        middle[z, rows, span] = value

    def finish(z, rows, span, value):
        out_ref[z - HALO, rows, span] = value

    sweep(field, keep, edge, HALO - 1, HALO + layers)
    for z in range(HALO - 1, HALO + layers + 1):
        middle[z, height : height + 1, :] = middle[z, height - 1 : height, :]
    sweep(middle, finish, edge, HALO, HALO + layers - 1)


def smooth(place, earlier, own, low, high):
    ring, layers, depth, columns = own.shape
    deep, height = layers + 2 * HALO, ring * depth
    return pl.pallas_call(
        smooth_kernel,
        in_specs=[SMEM, ANY, VMEM, VMEM, VMEM],
        out_specs=VMEM,
        out_shape=jax.ShapeDtypeStruct((layers, height, columns), jnp.float32),
        scratch_shapes=[
            pltpu.VMEM((deep, height + TILE, columns), jnp.float32),
            pltpu.VMEM((deep, height + TILE, columns), jnp.float32),
            pltpu.VMEM((deep, TILE, columns), jnp.float32),
        ],
        compiler_params=pltpu.CompilerParams(vmem_limit_bytes=16 * 2**20),
        name="smooth",
    )(place, earlier, own, low, high)


def windows(weights, shifts, bands):
    band_rows = weights.shape[1]
    rows_i = jnp.arange(band_rows, dtype=jnp.int32)[:, None]
    rows_j = jnp.arange(band_rows, dtype=jnp.int32)[None, :]
    placer = ((rows_i == rows_j + shifts[0, 0]) & (rows_j < bands[0, 0])).astype(jnp.float32)
    return jnp.sum(placer[None, :, :, None] * weights[:, None, :, :], axis=2)


def per_device(weights, shifts, bands, volume, measured):
    layers, height, columns = volume.shape
    own_rows = measured.shape[1]
    ring = lax.axis_size("ang") // 2
    depth = height // ring
    slab = lax.axis_index("slab")
    last_slab = lax.axis_size("slab") - 1
    place = jnp.stack(
        [lax.axis_index("ang") // 2, slab > 0, slab < last_slab]
    ).astype(jnp.int32)

    window = windows(weights, shifts, bands)
    low = window[:, :own_rows]
    count = window.shape[0] * own_rows
    flat = lambda block: block.reshape(count, layers)
    line = jnp.pad(window.reshape(1, -1), ((0, TILE - 1), (0, columns - window.size)))
    back = pack(flat(low), line, volume, measured)
    following = to_previous(back)
    window_before = from_behind(window, "slab", 1)
    whole, window_late = late(volume, window, back)
    before = to_next(whole)
    other = from_far_at_row_ends(window_late)
    high_next = jnp.where(slab % ROW == ROW - 1, other, window)[:, own_rows:]

    window_after = following[-TILE, : window.size].reshape(window.shape)
    low_after, high_before = window_after[:, :own_rows], window_before[:, own_rows:]
    total_own = jnp.sum(low, axis=2) + jnp.sum(high_before, axis=2)
    total_next = jnp.sum(low_after, axis=2) + jnp.sum(high_next, axis=2)
    share_own = 1.0 / jnp.maximum(total_own, 1.0)
    share_next = jnp.where(slab < last_slab, 1.0 / jnp.maximum(total_next, 1.0), 0.0)
    coefs_own = flat(low) * share_own.reshape(count, 1)
    coefs_next = flat(high_next) * share_next.reshape(count, 1)
    back_coefs = jnp.concatenate([coefs_own, coefs_next])
    normal_before = jnp.sum(coefs_own[:, :, None] * flat(high_before)[:, None, :], axis=0)
    normal_own = jnp.sum(coefs_next[:, :, None] * flat(high_next)[:, None, :], axis=0)
    column_part = jnp.sum(window, axis=(0, 1))
    sums = jnp.concatenate([normal_before, normal_own, column_part[:, None]], axis=1)
    sums = jnp.pad(sums, ((0, TILE - layers), (0, LANES - 2 * layers - 1)))

    sent = spread(back_coefs, sums, back, following, height, ring)
    near = gather(over_ring(sent), before)
    field = over_ring(update(place, near, from_far(near), before, volume, ring))
    residual, done = residual_of(flat(high_before), before, back, measured.shape)
    halo_low = to_next(field[:, layers - HALO :])
    halo_high = to_previous(field[:, :HALO])
    updated = smooth(place, done, field, halo_low, halo_high)
    return (updated, residual)


def solution(mesh):
    return jax.shard_map(
        per_device,
        mesh=mesh,
        in_specs=(
            P("ang", None, "slab"),
            P("ang", "slab"),
            P("ang", "slab"),
            P("slab", None, None),
            P("ang", "slab", None, None),
        ),
        out_specs=(P("slab", None, None), P("ang", "slab", None, None)),
        check_vma=False,
    )
```

```python
import jax
import jax.numpy as jnp
from jax import lax
from jax.experimental import pallas as pl
from jax.experimental.pallas import tpu as pltpu
from jax.sharding import PartitionSpec as P

TILE = 8
LANES = 128
HALO = 2


def from_behind(block, axis, distance):
    devices = range(lax.axis_size(axis))
    route = [(i - distance, i) for i in devices if i - distance in devices]
    return lax.ppermute(block, axis, route)


def ring_groups():
    count = lax.axis_size("ang")
    return [list(range(0, count, 2)), list(range(1, count, 2))]


def over_ring(pieces):
    return lax.all_to_all(
        pieces, "ang", split_axis=0, concat_axis=0, axis_index_groups=ring_groups()
    )


ROW = 16


def route(pairs):
    count, slabs = lax.axis_size("ang"), lax.axis_size("slab")
    return [
        (a * slabs + s, (a if s // ROW == t // ROW else a ^ 1) * slabs + t)
        for a in range(count)
        for s, t in pairs
        if 0 <= t < slabs
    ]


def along_column(block, distance):
    count, slabs = lax.axis_size("ang"), lax.axis_size("slab")
    pairs = []
    for a in range(count):
        for t in range(slabs):
            there = ((a % 2 * ROW + t % ROW) // 2 + distance) % ROW
            to_ang = a - a % 2 + there * 2 // ROW
            to_slab = t - t % ROW + there * 2 % ROW + t % 2
            pairs.append((a * slabs + t, to_ang * slabs + to_slab))
    return lax.ppermute(block, ("ang", "slab"), pairs)


def from_far(block):
    half = (block.shape[0] // TILE + 1) // 2 * TILE
    most = ROW // 2 - 1
    up, down = along_column(block[:half], most), along_column(block[half:], -most)
    return jnp.concatenate([along_column(up, 1), along_column(down, -1)])


def from_far_at_row_ends(block):
    count, slabs = lax.axis_size("ang"), lax.axis_size("slab")
    ends = range(ROW - 1, slabs, ROW)
    pairs = [(a * slabs + t, (a ^ 1) * slabs + t) for a in range(count) for t in ends]
    return lax.ppermute(block, ("ang", "slab"), pairs)


def to_next(block):
    pairs = [(s, s + 1) for s in range(lax.axis_size("slab"))]
    return lax.ppermute(block, ("ang", "slab"), route(pairs))


def over_ring(pieces):
    return lax.all_to_all(
        pieces, "ang", split_axis=0, concat_axis=0, axis_index_groups=ring_groups()
    )


ROW = 16


def route(pairs):
    count, slabs = lax.axis_size("ang"), lax.axis_size("slab")
    return [
        (a * slabs + s, (a if s // ROW == t // ROW else a ^ 1) * slabs + t)
        for a in range(count)
        for s, t in pairs
        if 0 <= t < slabs
    ]


def from_far(block):
    return lax.ppermute(block, "ang", [(a, a ^ 1) for a in range(lax.axis_size("ang"))])


def within_chip(block):
    return lax.ppermute(block, "slab", [(s, s ^ 1) for s in range(lax.axis_size("slab"))])


def across_chips(block):
    pairs = [(s, s + 1 if s % 2 else s - 1) for s in range(lax.axis_size("slab"))]
    return lax.ppermute(block, ("ang", "slab"), route(pairs))


def from_far_at_row_ends(block):
    count, slabs = lax.axis_size("ang"), lax.axis_size("slab")
    ends = range(ROW - 1, slabs, ROW)
    pairs = [(a * slabs + t, (a ^ 1) * slabs + t) for a in range(count) for t in ends]
    return lax.ppermute(block, ("ang", "slab"), pairs)


def to_next(block):
    pairs = [(s, s + 1) for s in range(lax.axis_size("slab"))]
    return lax.ppermute(block, ("ang", "slab"), route(pairs))


def to_previous(block):
    pairs = [(s, s - 1) for s in range(lax.axis_size("slab"))]
    return lax.ppermute(block, ("ang", "slab"), route(pairs))


VMEM = pl.BlockSpec(memory_space=pltpu.VMEM)
SMEM = pl.BlockSpec(memory_space=pltpu.SMEM)
ANY = pl.BlockSpec(memory_space=pl.ANY)


def splats(ref):
    rows, columns = ref.shape
    return [[jnp.full((TILE, LANES), ref[k, z]) for z in range(columns)] for k in range(rows)]


def combine(planes, coefs):
    total = planes[0] * coefs[0]
    for plane, coef in zip(planes[1:], coefs[1:]):
        total = total + plane * coef
    return total


def pack_kernel(coef_ref, window_ref, volume_ref, measured_ref, out_ref):
    angles, rows, height, columns = measured_ref.shape
    layers = volume_ref.shape[0]
    depth = 2 * TILE
    coefs = splats(coef_ref)
    out_ref[angles * rows * height :, :] = window_ref[...]

    def chunk(i, carry):
        top = pl.multiple_of(i * depth, depth)
        for t in range(columns // LANES):
            lanes = pl.ds(t * LANES, LANES)
            planes = [volume_ref[z, pl.ds(top, depth), lanes] for z in range(layers)]
            for a in range(angles):
                for r in range(rows):
                    k = a * rows + r
                    value = measured_ref[a, r, pl.ds(top, depth), lanes].astype(jnp.float32)
                    for j in range(depth // TILE):
                        tile = slice(j * TILE, (j + 1) * TILE)
                        row = pl.multiple_of(k * height + top + j * TILE, TILE)
                        out_ref[pl.ds(row, TILE), lanes] = value[tile] - combine(
                            [plane[tile] for plane in planes], coefs[k]
                        )
        return carry

    lax.fori_loop(0, height // depth, chunk, 0)


def pack(coefs, window, volume, measured):
    angles, rows, height, columns = measured.shape
    return pl.pallas_call(
        pack_kernel,
        in_specs=[SMEM, VMEM, VMEM, VMEM],
        out_specs=VMEM,
        out_shape=jax.ShapeDtypeStruct((angles * rows * height + TILE, columns), jnp.float32),
        compiler_params=pltpu.CompilerParams(vmem_limit_bytes=8 * 2**20),
        name="pack",
    )(coefs, window, volume, measured)


def spread_kernel(coef_ref, sums_ref, own_ref, next_ref, out_ref):
    count, layers = coef_ref.shape
    ring = out_ref.shape[0]
    columns = own_ref.shape[1]
    height = (own_ref.shape[0] - TILE) // (count // 2)
    depth = height // ring
    ytiles, xtiles = depth // TILE, columns // LANES
    coefs = splats(coef_ref)
    body = layers * ytiles * xtiles * TILE

    def chunk(i, carry):
        top = i * depth
        for t in range(xtiles):
            lanes = pl.ds(t * LANES, LANES)
            for j in range(ytiles):
                planes = [
                    ref[pl.ds(pl.multiple_of(k * height + top + j * TILE, TILE), TILE), lanes]
                    for ref in (own_ref, next_ref)
                    for k in range(count // 2)
                ]
                for z in range(layers):
                    row = ((z * ytiles + j) * xtiles + t) * TILE
                    out_ref[i, row : row + TILE, :] = combine(planes, [c[z] for c in coefs])
        out_ref[i, body : body + TILE, :] = sums_ref[...]
        return carry

    lax.fori_loop(0, ring, chunk, 0)


def spread(coefs, sums, own, following, height, ring):
    layers, columns = coefs.shape[1], own.shape[1]
    length = layers * (height // ring) * columns // LANES + TILE
    return pl.pallas_call(
        spread_kernel,
        in_specs=[SMEM, VMEM, VMEM, VMEM],
        out_specs=VMEM,
        out_shape=jax.ShapeDtypeStruct((ring, length, LANES), jnp.float32),
        compiler_params=pltpu.CompilerParams(vmem_limit_bytes=8 * 2**20),
        name="spread",
    )(coefs, sums, own, following)


def gather_kernel(parts_ref, earlier_ref, mine_ref):
    ring, length, _ = parts_ref.shape
    step = next(n for n in (5 * TILE, 3 * TILE, TILE) if length % n == 0)

    def add(i, carry):
        rows = pl.ds(pl.multiple_of(i * step, TILE), step)
        total = parts_ref[0, rows, :]
        for part in range(1, ring):
            total = total + parts_ref[part, rows, :]
        mine_ref[rows, :] = total
        return carry

    lax.fori_loop(0, length // step, add, 0)


def gather(parts, earlier):
    return pl.pallas_call(
        gather_kernel,
        in_specs=[VMEM, ANY],
        out_specs=VMEM,
        out_shape=jax.ShapeDtypeStruct(parts.shape[1:], jnp.float32),
        compiler_params=pltpu.CompilerParams(vmem_limit_bytes=8 * 2**20),
        name="gather",
    )(parts, earlier)


def late_kernel(volume_ref, window_ref, earlier_ref, whole_ref, window_out_ref):
    window_out_ref[...] = window_ref[...]
    for z in range(volume_ref.shape[0]):
        whole_ref[z] = volume_ref[z]


def late(volume, window, earlier):
    return pl.pallas_call(
        late_kernel,
        in_specs=[VMEM, VMEM, ANY],
        out_specs=[VMEM, VMEM],
        out_shape=[
            jax.ShapeDtypeStruct(volume.shape, jnp.float32),
            jax.ShapeDtypeStruct(window.shape, jnp.float32),
        ],
        compiler_params=pltpu.CompilerParams(vmem_limit_bytes=8 * 2**20),
        cost_estimate=pl.CostEstimate(flops=0, bytes_accessed=32 * 2**20, transcendentals=0),
        name="late",
    )(volume, window, earlier)


def residual_kernel(coef_ref, before_ref, own_ref, out_ref, done_ref):
    done_ref[...] = jnp.zeros_like(done_ref)
    angles, rows, height, columns = out_ref.shape
    layers = before_ref.shape[0]
    depth = 2 * TILE
    coefs = [[coef_ref[k, z] for z in range(layers)] for k in range(angles * rows)]

    def chunk(i, carry):
        top = pl.multiple_of(i * depth, depth)
        for t in range(columns // LANES):
            lanes = pl.ds(t * LANES, LANES)
            planes = [before_ref[z, pl.ds(top, depth), lanes] for z in range(layers)]
            for a in range(angles):
                for r in range(rows):
                    k = a * rows + r
                    total = planes[0] * coefs[k][0]
                    for z in range(1, layers):
                        total = total + planes[z] * coefs[k][z]
                    row = pl.multiple_of(k * height + top, depth)
                    out_ref[a, r, pl.ds(top, depth), lanes] = (
                        own_ref[pl.ds(row, depth), lanes] - total
                    )
        return carry

    lax.fori_loop(0, height // depth, chunk, 0)


def residual_of(coefs, before, own, shape):
    return pl.pallas_call(
        residual_kernel,
        in_specs=[SMEM, VMEM, VMEM],
        out_specs=[VMEM, VMEM],
        out_shape=[
            jax.ShapeDtypeStruct(shape, jnp.float32),
            jax.ShapeDtypeStruct((TILE, LANES), jnp.float32),
        ],
        compiler_params=pltpu.CompilerParams(vmem_limit_bytes=8 * 2**20),
        cost_estimate=pl.CostEstimate(flops=0, bytes_accessed=16 * 2**20, transcendentals=0),
        name="residual",
    )(coefs, before, own)


def update_kernel(place_ref, near_ref, far_ref, before_ref, volume_ref, out_ref):
    copies, layers, depth, columns = out_ref.shape
    ytiles, xtiles = depth // TILE, columns // LANES
    body = layers * ytiles * xtiles * TILE
    top = pl.multiple_of(place_ref[0] * depth, depth)
    sums = near_ref[body:, :] + far_ref[body:, :]
    share = 1.0 / sums[:, 2 * layers : 2 * layers + 1]
    sums = sums * share

    def splat(value):
        return jnp.broadcast_to(value, (TILE, LANES))

    shares = [splat(share[z : z + 1, :]) for z in range(layers)]
    coefs = [
        [splat(sums[z : z + 1, k : k + 1]) for k in range(2 * layers)] for z in range(layers)
    ]
    for t in range(xtiles):
        lanes = pl.ds(t * LANES, LANES)
        for j in range(ytiles):
            rows = pl.ds(pl.multiple_of(top + j * TILE, TILE), TILE)
            planes = [ref[z, rows, lanes] for ref in (before_ref, volume_ref) for z in range(layers)]
            for z in range(layers):
                row = ((z * ytiles + j) * xtiles + t) * TILE
                total = (near_ref[row : row + TILE, :] + far_ref[row : row + TILE, :]) * shares[z]
                value = planes[layers + z] + (total - combine(planes, coefs[z]))
                for copy in range(copies):
                    out_ref[copy, z, pl.ds(j * TILE, TILE), lanes] = value


def update(place, near, far, before, volume, ring):
    layers, height, columns = volume.shape
    return pl.pallas_call(
        update_kernel,
        in_specs=[SMEM] + [VMEM] * 4,
        out_specs=VMEM,
        out_shape=jax.ShapeDtypeStruct((ring, layers, height // ring, columns), jnp.float32),
        compiler_params=pltpu.CompilerParams(vmem_limit_bytes=8 * 2**20),
        name="update",
    )(place, near, far, before, volume)


def sweep(source, target, edge, lowest, highest):
    tall, columns = source.shape[1:]
    height = tall - TILE
    xtiles = columns // LANES
    lane = lax.broadcasted_iota(jnp.int32, (TILE, LANES), 1)
    level = lax.broadcasted_iota(jnp.int32, (TILE, LANES), 0)
    last_lane, first_lane = lane == LANES - 1, lane == 0
    last_row, first_row = level == TILE - 1, level == 0
    spans = [pl.ds(t * LANES, LANES) for t in range(xtiles)]
    for z in range(lowest, highest + 1):
        edge[z, :, :] = jnp.zeros((TILE, columns), jnp.float32)

    def band(i, carry):
        top = pl.multiple_of(i * TILE, TILE)
        rows = pl.ds(top, TILE)
        below = pl.ds(top + TILE, 1)
        upper = [source[lowest - 1, rows, span] for span in spans]
        flow_z = None
        for z in range(lowest - 1, highest + 1):
            base, upper = upper, [source[z + 1, rows, span] for span in spans]
            turned = [pltpu.roll(b, LANES - 1, 1) for b in base]
            grad_z, along, scaled = [], [], []
            for t in range(xtiles):
                rise = upper[t] - base[t]
                nearby = jnp.where(
                    last_row,
                    jnp.broadcast_to(source[z, below, spans[t]], (TILE, LANES)),
                    pltpu.roll(base[t], TILE - 1, 0),
                )
                down = nearby - base[t]
                right = jnp.where(
                    last_lane, turned[t + 1] if t + 1 < xtiles else base[t], turned[t]
                )
                across = right - base[t]
                scale = lax.rsqrt(rise * rise + down * down + across * across + 0.01)
                grad_z.append(rise * scale)
                along.append(down * scale)
                scaled.append(across * scale)
            if z >= lowest:
                moved = [pltpu.roll(p, 1, 1) for p in scaled]
                for t in range(xtiles):
                    left = jnp.where(first_lane, moved[t - 1] if t else 0.0, moved[t])
                    above = jnp.where(
                        first_row,
                        jnp.broadcast_to(edge[z, TILE - 1 : TILE, spans[t]], (TILE, LANES)),
                        pltpu.roll(along[t], 1, 0),
                    )
                    edge[z, :, spans[t]] = along[t]
                    div = (grad_z[t] - flow_z[t]) + (along[t] - above) + (scaled[t] - left)
                    target(z, rows, spans[t], base[t] + 0.05 * div)
            flow_z = grad_z
        return carry

    lax.fori_loop(0, height // TILE, band, 0)


def smooth_kernel(place_ref, earlier_ref, own_ref, low_ref, high_ref, out_ref, field, middle, edge):
    ring, layers, depth, columns = own_ref.shape
    height = ring * depth
    keep_low = place_ref[1].astype(jnp.float32)
    keep_high = place_ref[2].astype(jnp.float32)

    def fill(i, carry):
        top = pl.multiple_of(i * depth, depth)
        for z in range(HALO):
            field[z, pl.ds(top, depth), :] = low_ref[i, z]
            field[HALO + layers + z, pl.ds(top, depth), :] = high_ref[i, z]
        for z in range(layers):
            field[HALO + z, pl.ds(top, depth), :] = own_ref[i, z]
        return carry

    lax.fori_loop(0, ring, fill, 0)
    for z in range(layers + 2 * HALO):
        field[z, height : height + 1, :] = field[z, height - 1 : height, :]

    def keep(z, rows, span, value):
        if z == HALO - 1:
            value = value * keep_low
        if z == HALO + layers:
            value = value * keep_high
        middle[z, rows, span] = value

    def finish(z, rows, span, value):
        out_ref[z - HALO, rows, span] = value

    sweep(field, keep, edge, HALO - 1, HALO + layers)
    for z in range(HALO - 1, HALO + layers + 1):
        middle[z, height : height + 1, :] = middle[z, height - 1 : height, :]
    sweep(middle, finish, edge, HALO, HALO + layers - 1)


def smooth(place, earlier, own, low, high):
    ring, layers, depth, columns = own.shape
    deep, height = layers + 2 * HALO, ring * depth
    return pl.pallas_call(
        smooth_kernel,
        in_specs=[SMEM, ANY, VMEM, VMEM, VMEM],
        out_specs=VMEM,
        out_shape=jax.ShapeDtypeStruct((layers, height, columns), jnp.float32),
        scratch_shapes=[
            pltpu.VMEM((deep, height + TILE, columns), jnp.float32),
            pltpu.VMEM((deep, height + TILE, columns), jnp.float32),
            pltpu.VMEM((deep, TILE, columns), jnp.float32),
        ],
        compiler_params=pltpu.CompilerParams(vmem_limit_bytes=16 * 2**20),
        name="smooth",
    )(place, earlier, own, low, high)


def windows(weights, shifts, bands):
    band_rows = weights.shape[1]
    rows_i = jnp.arange(band_rows, dtype=jnp.int32)[:, None]
    rows_j = jnp.arange(band_rows, dtype=jnp.int32)[None, :]
    placer = ((rows_i == rows_j + shifts[0, 0]) & (rows_j < bands[0, 0])).astype(jnp.float32)
    return jnp.sum(placer[None, :, :, None] * weights[:, None, :, :], axis=2)


def per_device(weights, shifts, bands, volume, measured):
    layers, height, columns = volume.shape
    own_rows = measured.shape[1]
    ring = lax.axis_size("ang") // 2
    depth = height // ring
    slab = lax.axis_index("slab")
    last_slab = lax.axis_size("slab") - 1
    place = jnp.stack(
        [lax.axis_index("ang") // 2, slab > 0, slab < last_slab]
    ).astype(jnp.int32)

    window = windows(weights, shifts, bands)
    low = window[:, :own_rows]
    count = window.shape[0] * own_rows
    flat = lambda block: block.reshape(count, layers)
    line = jnp.pad(window.reshape(1, -1), ((0, TILE - 1), (0, columns - window.size)))
    back = pack(flat(low), line, volume, measured)
    following = to_previous(back)
    window_before = from_behind(window, "slab", 1)
    whole, window_late = late(volume, window, back)
    before = to_next(whole)
    other = from_far_at_row_ends(window_late)
    high_next = jnp.where(slab % ROW == ROW - 1, other, window)[:, own_rows:]

    window_after = following[-TILE, : window.size].reshape(window.shape)
    low_after, high_before = window_after[:, :own_rows], window_before[:, own_rows:]
    total_own = jnp.sum(low, axis=2) + jnp.sum(high_before, axis=2)
    total_next = jnp.sum(low_after, axis=2) + jnp.sum(high_next, axis=2)
    share_own = 1.0 / jnp.maximum(total_own, 1.0)
    share_next = jnp.where(slab < last_slab, 1.0 / jnp.maximum(total_next, 1.0), 0.0)
    coefs_own = flat(low) * share_own.reshape(count, 1)
    coefs_next = flat(high_next) * share_next.reshape(count, 1)
    back_coefs = jnp.concatenate([coefs_own, coefs_next])
    normal_before = jnp.sum(coefs_own[:, :, None] * flat(high_before)[:, None, :], axis=0)
    normal_own = jnp.sum(coefs_next[:, :, None] * flat(high_next)[:, None, :], axis=0)
    column_part = jnp.sum(window, axis=(0, 1))
    sums = jnp.concatenate([normal_before, normal_own, column_part[:, None]], axis=1)
    sums = jnp.pad(sums, ((0, TILE - layers), (0, LANES - 2 * layers - 1)))

    sent = spread(back_coefs, sums, back, following, height, ring)
    near = gather(over_ring(sent), before)
    field = over_ring(update(place, near, from_far(near), before, volume, ring))
    residual, done = residual_of(flat(high_before), before, back, measured.shape)
    halo_low = to_next(field[:, layers - HALO :])
    halo_high = to_previous(field[:, :HALO])
    updated = smooth(place, done, field, halo_low, halo_high)
    return (updated, residual)


def solution(mesh):
    return jax.shard_map(
        per_device,
        mesh=mesh,
        in_specs=(
            P("ang", None, "slab"),
            P("ang", "slab"),
            P("ang", "slab"),
            P("slab", None, None),
            P("ang", "slab", None, None),
        ),
        out_specs=(P("slab", None, None), P("ang", "slab", None, None)),
        check_vma=False,
    )
```

```python
import jax
import jax.numpy as jnp
from jax import lax
from jax.experimental import pallas as pl
from jax.experimental.pallas import tpu as pltpu
from jax.sharding import PartitionSpec as P

TILE = 8
LANES = 128
HALO = 2


def from_behind(block, axis, distance):
    devices = range(lax.axis_size(axis))
    route = [(i - distance, i) for i in devices if i - distance in devices]
    return lax.ppermute(block, axis, route)


def ring_groups():
    count = lax.axis_size("ang")
    return [list(range(0, count, 2)), list(range(1, count, 2))]


def over_ring(pieces):
    return lax.all_to_all(
        pieces, "ang", split_axis=0, concat_axis=0, axis_index_groups=ring_groups()
    )


ROW = 16


def route(pairs):
    count, slabs = lax.axis_size("ang"), lax.axis_size("slab")
    return [
        (a * slabs + s, (a if s // ROW == t // ROW else a ^ 1) * slabs + t)
        for a in range(count)
        for s, t in pairs
        if 0 <= t < slabs
    ]


def along_column(block, distance):
    count, slabs = lax.axis_size("ang"), lax.axis_size("slab")
    pairs = []
    for a in range(count):
        for t in range(slabs):
            there = ((a % 2 * ROW + t % ROW) // 2 + distance) % ROW
            to_ang = a - a % 2 + there * 2 // ROW
            to_slab = t - t % ROW + there * 2 % ROW + t % 2
            pairs.append((a * slabs + t, to_ang * slabs + to_slab))
    return lax.ppermute(block, ("ang", "slab"), pairs)


def from_far(block):
    half = (block.shape[0] // TILE + 1) // 2 * TILE
    most = ROW // 2 - 1
    up, down = along_column(block[:half], 1), along_column(block[half:], -1)
    return jnp.concatenate([along_column(up, most), along_column(down, -most)])


def from_far_at_row_ends(block):
    count, slabs = lax.axis_size("ang"), lax.axis_size("slab")
    ends = range(ROW - 1, slabs, ROW)
    pairs = [(a * slabs + t, (a ^ 1) * slabs + t) for a in range(count) for t in ends]
    return lax.ppermute(block, ("ang", "slab"), pairs)


def to_next(block):
    pairs = [(s, s + 1) for s in range(lax.axis_size("slab"))]
    return lax.ppermute(block, ("ang", "slab"), route(pairs))


def over_ring(pieces):
    return lax.all_to_all(
        pieces, "ang", split_axis=0, concat_axis=0, axis_index_groups=ring_groups()
    )


ROW = 16


def route(pairs):
    count, slabs = lax.axis_size("ang"), lax.axis_size("slab")
    return [
        (a * slabs + s, (a if s // ROW == t // ROW else a ^ 1) * slabs + t)
        for a in range(count)
        for s, t in pairs
        if 0 <= t < slabs
    ]


def from_far(block):
    return lax.ppermute(block, "ang", [(a, a ^ 1) for a in range(lax.axis_size("ang"))])


def within_chip(block):
    return lax.ppermute(block, "slab", [(s, s ^ 1) for s in range(lax.axis_size("slab"))])


def across_chips(block):
    pairs = [(s, s + 1 if s % 2 else s - 1) for s in range(lax.axis_size("slab"))]
    return lax.ppermute(block, ("ang", "slab"), route(pairs))


def from_far_at_row_ends(block):
    count, slabs = lax.axis_size("ang"), lax.axis_size("slab")
    ends = range(ROW - 1, slabs, ROW)
    pairs = [(a * slabs + t, (a ^ 1) * slabs + t) for a in range(count) for t in ends]
    return lax.ppermute(block, ("ang", "slab"), pairs)


def to_next(block):
    pairs = [(s, s + 1) for s in range(lax.axis_size("slab"))]
    return lax.ppermute(block, ("ang", "slab"), route(pairs))


def to_previous(block):
    pairs = [(s, s - 1) for s in range(lax.axis_size("slab"))]
    return lax.ppermute(block, ("ang", "slab"), route(pairs))


VMEM = pl.BlockSpec(memory_space=pltpu.VMEM)
SMEM = pl.BlockSpec(memory_space=pltpu.SMEM)
ANY = pl.BlockSpec(memory_space=pl.ANY)


def splats(ref):
    rows, columns = ref.shape
    return [[jnp.full((TILE, LANES), ref[k, z]) for z in range(columns)] for k in range(rows)]


def combine(planes, coefs):
    total = planes[0] * coefs[0]
    for plane, coef in zip(planes[1:], coefs[1:]):
        total = total + plane * coef
    return total


def pack_kernel(coef_ref, window_ref, volume_ref, measured_ref, out_ref):
    angles, rows, height, columns = measured_ref.shape
    layers = volume_ref.shape[0]
    depth = 2 * TILE
    coefs = splats(coef_ref)
    out_ref[angles * rows * height :, :] = window_ref[...]

    def chunk(i, carry):
        top = pl.multiple_of(i * depth, depth)
        for t in range(columns // LANES):
            lanes = pl.ds(t * LANES, LANES)
            planes = [volume_ref[z, pl.ds(top, depth), lanes] for z in range(layers)]
            for a in range(angles):
                for r in range(rows):
                    k = a * rows + r
                    value = measured_ref[a, r, pl.ds(top, depth), lanes].astype(jnp.float32)
                    for j in range(depth // TILE):
                        tile = slice(j * TILE, (j + 1) * TILE)
                        row = pl.multiple_of(k * height + top + j * TILE, TILE)
                        out_ref[pl.ds(row, TILE), lanes] = value[tile] - combine(
                            [plane[tile] for plane in planes], coefs[k]
                        )
        return carry

    lax.fori_loop(0, height // depth, chunk, 0)


def pack(coefs, window, volume, measured):
    angles, rows, height, columns = measured.shape
    return pl.pallas_call(
        pack_kernel,
        in_specs=[SMEM, VMEM, VMEM, VMEM],
        out_specs=VMEM,
        out_shape=jax.ShapeDtypeStruct((angles * rows * height + TILE, columns), jnp.float32),
        compiler_params=pltpu.CompilerParams(vmem_limit_bytes=8 * 2**20),
        name="pack",
    )(coefs, window, volume, measured)


def spread_kernel(coef_ref, sums_ref, own_ref, next_ref, out_ref):
    count, layers = coef_ref.shape
    ring = out_ref.shape[0]
    columns = own_ref.shape[1]
    height = (own_ref.shape[0] - TILE) // (count // 2)
    depth = height // ring
    ytiles, xtiles = depth // TILE, columns // LANES
    coefs = splats(coef_ref)
    body = layers * ytiles * xtiles * TILE

    def chunk(i, carry):
        top = i * depth
        for t in range(xtiles):
            lanes = pl.ds(t * LANES, LANES)
            for j in range(ytiles):
                planes = [
                    ref[pl.ds(pl.multiple_of(k * height + top + j * TILE, TILE), TILE), lanes]
                    for ref in (own_ref, next_ref)
                    for k in range(count // 2)
                ]
                for z in range(layers):
                    row = ((z * ytiles + j) * xtiles + t) * TILE
                    out_ref[i, row : row + TILE, :] = combine(planes, [c[z] for c in coefs])
        out_ref[i, body : body + TILE, :] = sums_ref[...]
        return carry

    lax.fori_loop(0, ring, chunk, 0)


def spread(coefs, sums, own, following, height, ring):
    layers, columns = coefs.shape[1], own.shape[1]
    length = layers * (height // ring) * columns // LANES + TILE
    return pl.pallas_call(
        spread_kernel,
        in_specs=[SMEM, VMEM, VMEM, VMEM],
        out_specs=VMEM,
        out_shape=jax.ShapeDtypeStruct((ring, length, LANES), jnp.float32),
        compiler_params=pltpu.CompilerParams(vmem_limit_bytes=8 * 2**20),
        name="spread",
    )(coefs, sums, own, following)


def gather_kernel(parts_ref, earlier_ref, mine_ref):
    ring, length, _ = parts_ref.shape
    step = next(n for n in (5 * TILE, 3 * TILE, TILE) if length % n == 0)

    def add(i, carry):
        rows = pl.ds(pl.multiple_of(i * step, TILE), step)
        total = parts_ref[0, rows, :]
        for part in range(1, ring):
            total = total + parts_ref[part, rows, :]
        mine_ref[rows, :] = total
        return carry

    lax.fori_loop(0, length // step, add, 0)


def gather(parts, earlier):
    return pl.pallas_call(
        gather_kernel,
        in_specs=[VMEM, ANY],
        out_specs=VMEM,
        out_shape=jax.ShapeDtypeStruct(parts.shape[1:], jnp.float32),
        compiler_params=pltpu.CompilerParams(vmem_limit_bytes=8 * 2**20),
        name="gather",
    )(parts, earlier)


def late_kernel(volume_ref, window_ref, earlier_ref, whole_ref, window_out_ref):
    window_out_ref[...] = window_ref[...]
    for z in range(volume_ref.shape[0]):
        whole_ref[z] = volume_ref[z]


def late(volume, window, earlier):
    return pl.pallas_call(
        late_kernel,
        in_specs=[VMEM, VMEM, ANY],
        out_specs=[VMEM, VMEM],
        out_shape=[
            jax.ShapeDtypeStruct(volume.shape, jnp.float32),
            jax.ShapeDtypeStruct(window.shape, jnp.float32),
        ],
        compiler_params=pltpu.CompilerParams(vmem_limit_bytes=8 * 2**20),
        cost_estimate=pl.CostEstimate(flops=0, bytes_accessed=32 * 2**20, transcendentals=0),
        name="late",
    )(volume, window, earlier)


def residual_kernel(coef_ref, before_ref, own_ref, out_ref, done_ref):
    done_ref[...] = jnp.zeros_like(done_ref)
    angles, rows, height, columns = out_ref.shape
    layers = before_ref.shape[0]
    depth = 2 * TILE
    coefs = [[coef_ref[k, z] for z in range(layers)] for k in range(angles * rows)]

    def chunk(i, carry):
        top = pl.multiple_of(i * depth, depth)
        for t in range(columns // LANES):
            lanes = pl.ds(t * LANES, LANES)
            planes = [before_ref[z, pl.ds(top, depth), lanes] for z in range(layers)]
            for a in range(angles):
                for r in range(rows):
                    k = a * rows + r
                    total = planes[0] * coefs[k][0]
                    for z in range(1, layers):
                        total = total + planes[z] * coefs[k][z]
                    row = pl.multiple_of(k * height + top, depth)
                    out_ref[a, r, pl.ds(top, depth), lanes] = (
                        own_ref[pl.ds(row, depth), lanes] - total
                    )
        return carry

    lax.fori_loop(0, height // depth, chunk, 0)


def residual_of(coefs, before, own, shape):
    return pl.pallas_call(
        residual_kernel,
        in_specs=[SMEM, VMEM, VMEM],
        out_specs=[VMEM, VMEM],
        out_shape=[
            jax.ShapeDtypeStruct(shape, jnp.float32),
            jax.ShapeDtypeStruct((TILE, LANES), jnp.float32),
        ],
        compiler_params=pltpu.CompilerParams(vmem_limit_bytes=8 * 2**20),
        cost_estimate=pl.CostEstimate(flops=0, bytes_accessed=16 * 2**20, transcendentals=0),
        name="residual",
    )(coefs, before, own)


def update_kernel(place_ref, near_ref, far_ref, before_ref, volume_ref, out_ref):
    copies, layers, depth, columns = out_ref.shape
    ytiles, xtiles = depth // TILE, columns // LANES
    body = layers * ytiles * xtiles * TILE
    top = pl.multiple_of(place_ref[0] * depth, depth)
    sums = near_ref[body:, :] + far_ref[body:, :]
    share = 1.0 / sums[:, 2 * layers : 2 * layers + 1]
    sums = sums * share

    def splat(value):
        return jnp.broadcast_to(value, (TILE, LANES))

    shares = [splat(share[z : z + 1, :]) for z in range(layers)]
    coefs = [
        [splat(sums[z : z + 1, k : k + 1]) for k in range(2 * layers)] for z in range(layers)
    ]
    for t in range(xtiles):
        lanes = pl.ds(t * LANES, LANES)
        for j in range(ytiles):
            rows = pl.ds(pl.multiple_of(top + j * TILE, TILE), TILE)
            planes = [ref[z, rows, lanes] for ref in (before_ref, volume_ref) for z in range(layers)]
            for z in range(layers):
                row = ((z * ytiles + j) * xtiles + t) * TILE
                total = (near_ref[row : row + TILE, :] + far_ref[row : row + TILE, :]) * shares[z]
                value = planes[layers + z] + (total - combine(planes, coefs[z]))
                for copy in range(copies):
                    out_ref[copy, z, pl.ds(j * TILE, TILE), lanes] = value


def update(place, near, far, before, volume, ring):
    layers, height, columns = volume.shape
    return pl.pallas_call(
        update_kernel,
        in_specs=[SMEM] + [VMEM] * 4,
        out_specs=VMEM,
        out_shape=jax.ShapeDtypeStruct((ring, layers, height // ring, columns), jnp.float32),
        compiler_params=pltpu.CompilerParams(vmem_limit_bytes=8 * 2**20),
        name="update",
    )(place, near, far, before, volume)


def sweep(source, target, edge, lowest, highest):
    tall, columns = source.shape[1:]
    height = tall - TILE
    xtiles = columns // LANES
    lane = lax.broadcasted_iota(jnp.int32, (TILE, LANES), 1)
    level = lax.broadcasted_iota(jnp.int32, (TILE, LANES), 0)
    last_lane, first_lane = lane == LANES - 1, lane == 0
    last_row, first_row = level == TILE - 1, level == 0
    spans = [pl.ds(t * LANES, LANES) for t in range(xtiles)]
    for z in range(lowest, highest + 1):
        edge[z, :, :] = jnp.zeros((TILE, columns), jnp.float32)

    def band(i, carry):
        top = pl.multiple_of(i * TILE, TILE)
        rows = pl.ds(top, TILE)
        below = pl.ds(top + TILE, 1)
        upper = [source[lowest - 1, rows, span] for span in spans]
        flow_z = None
        for z in range(lowest - 1, highest + 1):
            base, upper = upper, [source[z + 1, rows, span] for span in spans]
            turned = [pltpu.roll(b, LANES - 1, 1) for b in base]
            grad_z, along, scaled = [], [], []
            for t in range(xtiles):
                rise = upper[t] - base[t]
                nearby = jnp.where(
                    last_row,
                    jnp.broadcast_to(source[z, below, spans[t]], (TILE, LANES)),
                    pltpu.roll(base[t], TILE - 1, 0),
                )
                down = nearby - base[t]
                right = jnp.where(
                    last_lane, turned[t + 1] if t + 1 < xtiles else base[t], turned[t]
                )
                across = right - base[t]
                scale = lax.rsqrt(rise * rise + down * down + across * across + 0.01)
                grad_z.append(rise * scale)
                along.append(down * scale)
                scaled.append(across * scale)
            if z >= lowest:
                moved = [pltpu.roll(p, 1, 1) for p in scaled]
                for t in range(xtiles):
                    left = jnp.where(first_lane, moved[t - 1] if t else 0.0, moved[t])
                    above = jnp.where(
                        first_row,
                        jnp.broadcast_to(edge[z, TILE - 1 : TILE, spans[t]], (TILE, LANES)),
                        pltpu.roll(along[t], 1, 0),
                    )
                    edge[z, :, spans[t]] = along[t]
                    div = (grad_z[t] - flow_z[t]) + (along[t] - above) + (scaled[t] - left)
                    target(z, rows, spans[t], base[t] + 0.05 * div)
            flow_z = grad_z
        return carry

    lax.fori_loop(0, height // TILE, band, 0)


def smooth_kernel(place_ref, earlier_ref, own_ref, low_ref, high_ref, out_ref, field, middle, edge):
    ring, layers, depth, columns = own_ref.shape
    height = ring * depth
    keep_low = place_ref[1].astype(jnp.float32)
    keep_high = place_ref[2].astype(jnp.float32)

    def fill(i, carry):
        top = pl.multiple_of(i * depth, depth)
        for z in range(HALO):
            field[z, pl.ds(top, depth), :] = low_ref[i, z]
            field[HALO + layers + z, pl.ds(top, depth), :] = high_ref[i, z]
        for z in range(layers):
            field[HALO + z, pl.ds(top, depth), :] = own_ref[i, z]
        return carry

    lax.fori_loop(0, ring, fill, 0)
    for z in range(layers + 2 * HALO):
        field[z, height : height + 1, :] = field[z, height - 1 : height, :]

    def keep(z, rows, span, value):
        if z == HALO - 1:
            value = value * keep_low
        if z == HALO + layers:
            value = value * keep_high
        middle[z, rows, span] = value

    def finish(z, rows, span, value):
        out_ref[z - HALO, rows, span] = value

    sweep(field, keep, edge, HALO - 1, HALO + layers)
    for z in range(HALO - 1, HALO + layers + 1):
        middle[z, height : height + 1, :] = middle[z, height - 1 : height, :]
    sweep(middle, finish, edge, HALO, HALO + layers - 1)


def smooth(place, earlier, own, low, high):
    ring, layers, depth, columns = own.shape
    deep, height = layers + 2 * HALO, ring * depth
    return pl.pallas_call(
        smooth_kernel,
        in_specs=[SMEM, ANY, VMEM, VMEM, VMEM],
        out_specs=VMEM,
        out_shape=jax.ShapeDtypeStruct((layers, height, columns), jnp.float32),
        scratch_shapes=[
            pltpu.VMEM((deep, height + TILE, columns), jnp.float32),
            pltpu.VMEM((deep, height + TILE, columns), jnp.float32),
            pltpu.VMEM((deep, TILE, columns), jnp.float32),
        ],
        compiler_params=pltpu.CompilerParams(vmem_limit_bytes=16 * 2**20),
        name="smooth",
    )(place, earlier, own, low, high)


def windows(weights, shifts, bands):
    band_rows = weights.shape[1]
    rows_i = jnp.arange(band_rows, dtype=jnp.int32)[:, None]
    rows_j = jnp.arange(band_rows, dtype=jnp.int32)[None, :]
    placer = ((rows_i == rows_j + shifts[0, 0]) & (rows_j < bands[0, 0])).astype(jnp.float32)
    return jnp.sum(placer[None, :, :, None] * weights[:, None, :, :], axis=2)


def per_device(weights, shifts, bands, volume, measured):
    layers, height, columns = volume.shape
    own_rows = measured.shape[1]
    ring = lax.axis_size("ang") // 2
    depth = height // ring
    slab = lax.axis_index("slab")
    last_slab = lax.axis_size("slab") - 1
    place = jnp.stack(
        [lax.axis_index("ang") // 2, slab > 0, slab < last_slab]
    ).astype(jnp.int32)

    window = windows(weights, shifts, bands)
    low = window[:, :own_rows]
    count = window.shape[0] * own_rows
    flat = lambda block: block.reshape(count, layers)
    line = jnp.pad(window.reshape(1, -1), ((0, TILE - 1), (0, columns - window.size)))
    back = pack(flat(low), line, volume, measured)
    following = to_previous(back)
    window_before = from_behind(window, "slab", 1)
    whole, window_late = late(volume, window, back)
    before = to_next(whole)
    other = from_far_at_row_ends(window_late)
    high_next = jnp.where(slab % ROW == ROW - 1, other, window)[:, own_rows:]

    window_after = following[-TILE, : window.size].reshape(window.shape)
    low_after, high_before = window_after[:, :own_rows], window_before[:, own_rows:]
    total_own = jnp.sum(low, axis=2) + jnp.sum(high_before, axis=2)
    total_next = jnp.sum(low_after, axis=2) + jnp.sum(high_next, axis=2)
    share_own = 1.0 / jnp.maximum(total_own, 1.0)
    share_next = jnp.where(slab < last_slab, 1.0 / jnp.maximum(total_next, 1.0), 0.0)
    coefs_own = flat(low) * share_own.reshape(count, 1)
    coefs_next = flat(high_next) * share_next.reshape(count, 1)
    back_coefs = jnp.concatenate([coefs_own, coefs_next])
    normal_before = jnp.sum(coefs_own[:, :, None] * flat(high_before)[:, None, :], axis=0)
    normal_own = jnp.sum(coefs_next[:, :, None] * flat(high_next)[:, None, :], axis=0)
    column_part = jnp.sum(window, axis=(0, 1))
    sums = jnp.concatenate([normal_before, normal_own, column_part[:, None]], axis=1)
    sums = jnp.pad(sums, ((0, TILE - layers), (0, LANES - 2 * layers - 1)))

    sent = spread(back_coefs, sums, back, following, height, ring)
    near = gather(over_ring(sent), before)
    field = over_ring(update(place, near, from_far(near), before, volume, ring))
    residual, done = residual_of(flat(high_before), before, back, measured.shape)
    halo_low = to_next(field[:, layers - HALO :])
    halo_high = to_previous(field[:, :HALO])
    updated = smooth(place, done, field, halo_low, halo_high)
    return (updated, residual)


def solution(mesh):
    return jax.shard_map(
        per_device,
        mesh=mesh,
        in_specs=(
            P("ang", None, "slab"),
            P("ang", "slab"),
            P("ang", "slab"),
            P("slab", None, None),
            P("ang", "slab", None, None),
        ),
        out_specs=(P("slab", None, None), P("ang", "slab", None, None)),
        check_vma=False,
    )
```
